256 devices in a mesh: dp: 64 (over x, z, y_hi), space: 4 (over y_lo, core).
Axes of the slice: x: 4, y: 4 (y_hi: 2, y_lo: 2; y = y_hi * 2 + y_lo), z: 8, core: 2. Of those that a mesh axis runs over, the one named last changes fastest.
Arguments:
- section_input: bfloat16 [64, 2, 4, 64, 640], P('dp', None, 'space'), may hold values from -6 to 6
- target: bfloat16 [64, 2, 4, 64, 640], P('dp', None, 'space'), may hold values from -6 to 6
- conv_weight: bfloat16 [3, 3, 640, 640], replicated, may hold values from -0.078125 to 0.078125
- conv_bias: float32 [640], replicated, may hold values from -3 to 3
- norm_gain: float32 [640], replicated, may hold values from 0.5 to 1.5
- qkv_weight: bfloat16 [640, 1920], replicated, may hold values from -1 to 1
- out_weight: bfloat16 [640, 640], replicated, may hold values from -0.25 to 0.25
- time_weight: bfloat16 [320, 640], replicated, may hold values from -0.3125 to 0.3125
- timesteps: int32 [64], P('dp'), may hold values from 0 to 999
- labels: int32 [64], P('dp'), may hold values from 0 to 1
- ref_error: float32 [64, 2], P('dp'), may hold values from 4 to 6
Outputs:
- input_grad: bfloat16 [64, 2, 4, 64, 640], P('dp', None, 'space')
- conv_weight_grad: float32 [3, 3, 640, 640], P(None, None, None, 'dp')
- qkv_weight_grad: float32 [640, 1920], P(None, 'dp')
- out_weight_grad: float32 [640, 640], P(None, 'dp')
- time_weight_grad: float32 [320, 640], P(None, 'dp')
- gain_grad: float32 [640], P('dp')
- bias_grad: float32 [640], P('dp')
- pair_loss: float32 [64], P('dp')
The draws below stay inside these ranges and needn't reach their ends.
All inputs are finite; a program needn't handle non-finite values.
Results may differ from the reference program's by a relative error of at most 0.027.
Values may be sent and summed in bfloat16 or wider, within the bound.
No kernel may reach another device: no remote copies, remote signals or barrier semaphores. Data moves between devices by JAX's collectives and lax.ppermute only.
A program may use at most 128 MiB of HBM per device.

```python
import math
import jax
import jax.numpy as jnp
from jax import lax

C = 640
HEADS = 10
GROUPS = 32
TDIM = 320
COLS = 64
ROWS = 4
PAIRS = 64


def draw_section_input(key, part):
    key = jax.random.fold_in(key, 11)
    shape = (PAIRS, 2, ROWS, COLS, C)
    values = jnp.clip(jax.random.normal(key, shape, jnp.float32), -6.0, 6.0)
    return values.astype(jnp.bfloat16)


def draw_qkv_weight(key, part):
    key = jax.random.fold_in(key, 23)
    keys = jax.random.split(key, 1)
    spread = 1.0 / math.sqrt(C)
    weights = jnp.clip(jax.random.normal(keys[0], (C, 3 * C), jnp.float32), -6.0, 6.0) * spread
    return weights.astype(jnp.bfloat16)


def plant(values, own_key, smallest, high):
    place = [jax.random.randint(jax.random.fold_in(own_key, axis), (), 0, length) for axis, length in enumerate(values.shape)]
    widest = values.shape.index(max(values.shape))
    neighbour = place[:widest] + [(place[widest] + 1) % values.shape[widest]] + place[widest + 1:]
    return values.at[tuple(place)].set(smallest).at[tuple(neighbour)].set(high)


def steps_of(key, extent, pieces, low, high):
    gain, own = 1.0, jax.random.fold_in(key, 6)
    for dim, blocks in pieces:
        draws = jnp.exp(jax.random.uniform(jax.random.fold_in(own, dim), (blocks,), jnp.float32, low / len(pieces), high / len(pieces)))
        gain = gain * jnp.repeat(draws, extent[dim] // blocks).reshape([-1 if axis == dim else 1 for axis in range(len(extent))])
    return gain


def scatter_about(rng, shape, scale, most, pieces=(), kind=jnp.bfloat16):
    array = jax.random.normal(rng, shape, jnp.float32) * scale
    if len(pieces) > 0:
        array = steps_of(rng, shape, pieces, -0.22, 0.18) * array
    return jnp.clip(array, min=-most, max=most).astype(kind)


def setup_inputs(seed: int = 0) -> dict:
    key_list = jax.random.split(jax.random.key(seed), 12)
    return {
        "section_input": draw_section_input(jax.random.fold_in(key_list[11], 71), 0),
        "target": scatter_about(key_list[1], (PAIRS, 2, ROWS, COLS, C), 1.0, 6.0, ((0, 64), (2, 4))),
        "conv_weight": scatter_about(key_list[2], (3, 3, C, C), (9 * C) ** -0.5, 0.078125),
        "conv_bias": scatter_about(key_list[3], (C,), 0.5, 3.0, (), jnp.float32),
        "norm_gain": jnp.clip(1.0 + 0.1 * jax.random.normal(key_list[4], (C,), jnp.float32), 0.5, 1.5),
        "qkv_weight": draw_qkv_weight(jax.random.fold_in(key_list[11], 71), 0),
        "out_weight": scatter_about(key_list[6], (C, C), C ** -0.5, 0.25),
        "time_weight": scatter_about(key_list[7], (TDIM, C), TDIM ** -0.5, 0.3125),
        "timesteps": plant(jax.random.randint(key_list[8], (PAIRS,), 0, 1000), jax.random.fold_in(key_list[8], 1), 0, 999).astype(jnp.int32),
        "labels": plant(jax.random.randint(key_list[9], (PAIRS,), 0, 2), jax.random.fold_in(key_list[9], 1), 0, 1).astype(jnp.int32),
        "ref_error": jnp.clip(4.0 + 2.0 * jax.random.uniform(key_list[10], (PAIRS, 2), jnp.float32) ** steps_of(key_list[10], (PAIRS, 2), ((0, 64),), -0.2, 0.2), 4.0, 6.0),
    }


norm_eps = 1e-05
dpo_beta = 2.0

def sinusoid(step_vals):
    half_dim = TDIM // 2
    freqs = jnp.exp(-math.log(10000.0) * jnp.arange(half_dim, dtype=jnp.float32) / half_dim)
    angles = step_vals.astype(jnp.float32)[:, None] * freqs[None, :]
    return jnp.concatenate([jnp.cos(angles), jnp.sin(angles)], axis=1).astype(jnp.bfloat16)

def conv_apply(padded, weight):
    total = jnp.zeros(padded.shape[:1] + (ROWS, COLS, C), jnp.float32)
    for row_off in range(3):
        for col_off in range(3):
            window = padded[:, row_off:row_off + ROWS, col_off:col_off + COLS, :].astype(jnp.float32)
            total = total + jnp.einsum('bhwc,cd->bhwd', window, weight[row_off, col_off].astype(jnp.float32))
    return total

def reference(section_input, target, conv_weight, conv_bias, norm_gain, qkv_weight, out_weight, time_weight, timesteps, labels, ref_error):
    head_dim = C // HEADS
    group_width = C // GROUPS
    group_count = ROWS * COLS * group_width
    tokens = ROWS * COLS
    scale_factor = 1.0 / math.sqrt(head_dim)
    time_feats = sinusoid(timesteps)
    time_shift = jnp.dot(time_feats, time_weight, preferred_element_type=jnp.float32)
    qkv_f = qkv_weight.astype(jnp.float32)
    out_f = out_weight.astype(jnp.float32)
    conv_f = conv_weight.astype(jnp.float32)

    def one_pair(totals, inputs):
        images, target_img, shift, label_val, ref_pair, feats = inputs
        values = images.astype(jnp.float32)
        grouped = values.reshape(2, ROWS, COLS, GROUPS, group_width)
        mean_val = lax.optimization_barrier(jnp.sum(grouped, (1, 2, 4))) / group_count
        square_mean = lax.optimization_barrier(jnp.sum(grouped * grouped, (1, 2, 4))) / group_count
        inv_std = lax.rsqrt(square_mean - mean_val * mean_val + norm_eps)
        normed_g = (grouped - mean_val[:, None, None, :, None]) * inv_std[:, None, None, :, None]
        normed = normed_g.reshape(2, ROWS, COLS, C)
        act_in = normed * norm_gain
        activated = jax.nn.silu(act_in).astype(jnp.bfloat16)
        padded = jnp.pad(activated, ((0, 0), (1, 1), (1, 1), (0, 0)))
        conv_out = conv_apply(padded, conv_weight)
        resid = (values + conv_out + conv_bias + shift[None, None, None, :]).astype(jnp.bfloat16)
        resid_flat = resid.reshape(2, tokens, C)
        proj_qkv = jnp.einsum('bnc,cd->bnd', resid_flat.astype(jnp.float32), qkv_f).astype(jnp.bfloat16)
        queries = proj_qkv[..., :C].reshape(2, tokens, HEADS, head_dim).astype(jnp.float32)
        key_rows = proj_qkv[..., C:2 * C].reshape(2, tokens, HEADS, head_dim).astype(jnp.float32)
        value_rows = proj_qkv[..., 2 * C:].reshape(2, tokens, HEADS, head_dim).astype(jnp.float32)
        scores = jnp.einsum('bqhd,bkhd->bhqk', queries, key_rows) * scale_factor
        top_score = lax.optimization_barrier(jnp.max(scores, axis=-1, keepdims=True))
        exp_scores = jnp.exp(scores - top_score)
        attn_probs = exp_scores / lax.optimization_barrier(jnp.sum(exp_scores, axis=-1, keepdims=True))
        probs_low = attn_probs.astype(jnp.bfloat16).astype(jnp.float32)
        attended = jnp.einsum('bhqk,bkhd->bqhd', probs_low, value_rows).reshape(2, tokens, C).astype(jnp.bfloat16)
        output = resid_flat.astype(jnp.float32) + jnp.einsum('bnc,cd->bnd', attended.astype(jnp.float32), out_f)
        deviation = output - target_img.reshape(2, tokens, C).astype(jnp.float32)
        image_error = lax.optimization_barrier(jnp.sum(deviation * deviation, axis=(1, 2))) / (tokens * C)
        sign_vals = jnp.where(jnp.arange(2) == label_val, 1.0, -1.0).astype(jnp.float32)
        margin = jnp.sum(sign_vals * (image_error - ref_pair))
        pair_loss = jax.nn.softplus(dpo_beta * margin)
        image_weight = sign_vals * (dpo_beta * jax.nn.sigmoid(dpo_beta * margin))
        out_grad = (image_weight[:, None, None] * deviation).astype(jnp.bfloat16).astype(jnp.float32)
        grad_out = jnp.einsum('bnc,bnd->cd', attended.astype(jnp.float32), out_grad)
        attended_grad = jnp.einsum('bnd,cd->bnc', out_grad, out_f).astype(jnp.bfloat16).astype(jnp.float32)
        attended_grad = attended_grad.reshape(2, tokens, HEADS, head_dim)
        prob_grad = jnp.einsum('bqhd,bkhd->bhqk', attended_grad, value_rows)
        row_dot = lax.optimization_barrier(jnp.sum(attn_probs * prob_grad, axis=-1, keepdims=True))
        score_grad = (attn_probs * (prob_grad - row_dot) * scale_factor).astype(jnp.bfloat16).astype(jnp.float32)
        query_grad = jnp.einsum('bhqk,bkhd->bqhd', score_grad, key_rows).astype(jnp.bfloat16)
        key_grad = jnp.einsum('bhqk,bqhd->bkhd', score_grad, queries).astype(jnp.bfloat16)
        value_grad = jnp.einsum('bhqk,bqhd->bkhd', probs_low, attended_grad).astype(jnp.bfloat16)
        qkv_grad = jnp.concatenate([query_grad.reshape(2, tokens, C), key_grad.reshape(2, tokens, C), value_grad.reshape(2, tokens, C)], axis=2).astype(jnp.float32)
        grad_qkv = jnp.einsum('bnc,bnd->cd', resid_flat.astype(jnp.float32), qkv_grad)
        resid_grad = out_grad + jnp.einsum('bnd,cd->bnc', qkv_grad, qkv_f)
        resid_grad = resid_grad.reshape(2, ROWS, COLS, C)
        conv_grad = resid_grad.astype(jnp.bfloat16)
        per_image = lax.optimization_barrier(jnp.sum(conv_grad.astype(jnp.float32), axis=(1, 2)))
        grad_bias = lax.optimization_barrier(jnp.sum(per_image, axis=0))
        grad_time = jnp.outer(feats.astype(jnp.float32), grad_bias)
        conv_grad_f = conv_grad.astype(jnp.float32)
        kernel_rows = []
        for row_off in range(3):
            kernel_cols = []
            for col_off in range(3):
                window = padded[:, row_off:row_off + ROWS, col_off:col_off + COLS, :].astype(jnp.float32)
                kernel_cols.append(jnp.einsum('bhwc,bhwd->cd', window, conv_grad_f))
            kernel_rows.append(jnp.stack(kernel_cols))
        grad_conv = jnp.stack(kernel_rows)
        grad_pad = jnp.pad(conv_grad_f, ((0, 0), (1, 1), (1, 1), (0, 0)))
        act_grad = jnp.zeros((2, ROWS, COLS, C), jnp.float32)
        for row_off in range(3):
            for col_off in range(3):
                window = grad_pad[:, 2 - row_off:2 - row_off + ROWS, 2 - col_off:2 - col_off + COLS, :]
                act_grad = act_grad + jnp.einsum('bhwd,cd->bhwc', window, conv_f[row_off, col_off])
        sigma = jax.nn.sigmoid(act_in)
        pre_grad = act_grad * (sigma * (1.0 + act_in * (1.0 - sigma)))
        grad_gain = lax.optimization_barrier(jnp.sum(pre_grad * normed, axis=(0, 1, 2)))
        scaled = (pre_grad * norm_gain).reshape(2, ROWS, COLS, GROUPS, group_width)
        mean_one = lax.optimization_barrier(jnp.sum(scaled, (1, 2, 4))) / group_count
        mean_two = lax.optimization_barrier(jnp.sum(scaled * normed_g, (1, 2, 4))) / group_count
        inner_grad = inv_std[:, None, None, :, None] * (scaled - mean_one[:, None, None, :, None] - normed_g * mean_two[:, None, None, :, None])
        input_grad = (resid_grad + inner_grad.reshape(2, ROWS, COLS, C)).astype(jnp.bfloat16)
        new_totals = (totals[0] + grad_conv, totals[1] + grad_qkv, totals[2] + grad_out, totals[3] + grad_time, totals[4] + grad_gain, totals[5] + grad_bias)
        return (new_totals, (input_grad, pair_loss))
    start = (jnp.zeros((3, 3, C, C), jnp.float32), jnp.zeros((C, 3 * C), jnp.float32), jnp.zeros((C, C), jnp.float32), jnp.zeros((TDIM, C), jnp.float32), jnp.zeros((C,), jnp.float32), jnp.zeros((C,), jnp.float32))
    totals, stacked = lax.scan(one_pair, start, (section_input, target, time_shift, labels, ref_error, time_feats))
    return (stacked[0], totals[0], totals[1], totals[2], totals[3], totals[4], totals[5], stacked[1])
```

```python
import math

import jax
import jax.numpy as jnp
from jax import lax
from jax.sharding import Mesh
from jax.sharding import PartitionSpec as P

HEADS = 10
GROUPS = 32
TDIM = 320


norm_eps = 1e-05
dpo_beta = 2.0


def sinusoid(step_vals):
    half_dim = TDIM // 2
    freqs = jnp.exp(-math.log(10000.0) * jnp.arange(half_dim, dtype=jnp.float32) / half_dim)
    angles = step_vals.astype(jnp.float32)[:, None] * freqs[None, :]
    return jnp.concatenate([jnp.cos(angles), jnp.sin(angles)], axis=1).astype(jnp.bfloat16)


PAIR_AXES = ("x", "z", "y_hi")
SPACE_AXES = ("y_lo", "core")
CHUNK_ROWS = 176


def halo_rows(values):
    return jnp.pad(values, ((0, 0), (1, 1), (1, 1), (0, 0)))


def image_sums(values):
    return values


def sum_over_pairs(chunks):
    rows = chunks.shape[1]
    split = chunks.reshape(4, 8, 2, rows, 128).transpose(0, 2, 1, 3, 4)
    split = split.reshape(8, 8 * rows, 128)
    moved = lax.all_to_all(split, ("x", "y_hi"), 0, 0)
    half = jnp.sum(moved.astype(jnp.float32), axis=0).astype(jnp.bfloat16)
    moved = lax.all_to_all(half.reshape(8, rows, 128), "z", 0, 0)
    return jnp.sum(moved.astype(jnp.float32), axis=0)


def on_device(
    section_input,
    target,
    conv_weight,
    conv_bias,
    norm_gain,
    qkv_weight,
    out_weight,
    time_weight,
    timesteps,
    labels,
    ref_error,
):
    in_shape = section_input.shape
    section_input = lax.all_gather(section_input, SPACE_AXES, axis=2, tiled=True)
    target = lax.all_gather(target, SPACE_AXES, axis=2, tiled=True)
    part = lax.axis_index(SPACE_AXES)
    pair_count, _, row_count, col_count, channels = section_input.shape
    batch_size = pair_count * 2
    local_tok = row_count * col_count
    total_rows = row_count
    head_dim = channels // HEADS
    group_width = channels // GROUPS
    group_count = total_rows * col_count * group_width
    scale_factor = 1.0 / math.sqrt(head_dim)
    images = section_input.reshape(batch_size, row_count, col_count, channels)
    values = images.astype(jnp.float32)
    grouped = values.reshape(batch_size, row_count, col_count, GROUPS, group_width)
    moments = image_sums(
        jnp.stack([jnp.sum(grouped, (1, 2, 4)), jnp.sum(grouped * grouped, (1, 2, 4))])
    )
    mean_val = moments[0] / group_count
    square_mean = moments[1] / group_count
    inv_std = lax.rsqrt(square_mean - mean_val * mean_val + norm_eps)
    normed_g = (grouped - mean_val[:, None, None, :, None]) * inv_std[:, None, None, :, None]
    normed = normed_g.reshape(batch_size, row_count, col_count, channels)
    act_in = normed * norm_gain
    activated = jax.nn.silu(act_in).astype(jnp.bfloat16)
    padded = halo_rows(activated)
    time_feats = sinusoid(timesteps)
    time_shift = jnp.dot(time_feats, time_weight, preferred_element_type=jnp.float32)
    shift_img = jnp.repeat(time_shift, 2, axis=0)
    conv_out = jnp.zeros((batch_size * local_tok, channels), jnp.float32)
    for row_off in range(3):
        for col_off in range(3):
            window = padded[
                :, row_off : row_off + row_count, col_off : col_off + col_count, :
            ].reshape(-1, channels)
            conv_out = conv_out + jnp.dot(
                window, conv_weight[row_off, col_off], preferred_element_type=jnp.float32
            )
    conv_out = conv_out.reshape(batch_size, row_count, col_count, channels)
    resid = (values + conv_out + conv_bias + shift_img[:, None, None, :]).astype(jnp.bfloat16)
    resid_flat = resid.reshape(batch_size * local_tok, channels)
    proj_qkv = jnp.dot(resid_flat, qkv_weight, preferred_element_type=jnp.float32).astype(
        jnp.bfloat16
    )
    proj_qkv = proj_qkv.reshape(batch_size, local_tok, 3 * channels)
    queries = proj_qkv[..., :channels].reshape(batch_size, local_tok, HEADS, head_dim)
    gathered = proj_qkv[..., channels:]
    key_rows = gathered[..., :channels].reshape(batch_size, -1, HEADS, head_dim)
    value_rows = gathered[..., channels:].reshape(batch_size, -1, HEADS, head_dim)
    scores = (
        jnp.einsum("bqhd,bkhd->bhqk", queries, key_rows, preferred_element_type=jnp.float32)
        * scale_factor
    )
    top_score = jnp.max(scores, axis=-1, keepdims=True)
    exp_scores = jnp.exp(scores - top_score)
    denom = jnp.sum(exp_scores, axis=-1, keepdims=True)
    attn_probs = exp_scores / denom
    probs_low = attn_probs.astype(jnp.bfloat16)
    attended = jnp.einsum(
        "bhqk,bkhd->bqhd", probs_low, value_rows, preferred_element_type=jnp.float32
    )
    attended = attended.astype(jnp.bfloat16).reshape(batch_size * local_tok, channels)
    output = resid_flat.astype(jnp.float32) + jnp.dot(
        attended, out_weight, preferred_element_type=jnp.float32
    )
    deviation = output - target.reshape(batch_size * local_tok, channels).astype(jnp.float32)
    square_dev = jnp.sum((deviation * deviation).reshape(batch_size, local_tok * channels), axis=1)
    image_error = image_sums(square_dev) / (total_rows * col_count * channels)
    error_pairs = image_error.reshape(pair_count, 2)
    sign_vals = jnp.where(jnp.arange(2)[None, :] == labels[:, None], 1.0, -1.0).astype(jnp.float32)
    margin = jnp.sum(sign_vals * (error_pairs - ref_error), axis=1)
    pair_loss = jax.nn.softplus(dpo_beta * margin)
    image_weight = (sign_vals * (dpo_beta * jax.nn.sigmoid(dpo_beta * margin))[:, None]).reshape(
        batch_size
    )
    out_grad = (jnp.repeat(image_weight, local_tok)[:, None] * deviation).astype(jnp.bfloat16)
    quarter = channels // 4
    attended_part = lax.dynamic_slice_in_dim(attended, part * quarter, quarter, axis=1)
    grad_out = jnp.einsum("nc,nd->dc", attended_part, out_grad, preferred_element_type=jnp.float32)
    attended_grad = jnp.einsum(
        "nd,cd->nc", out_grad, out_weight, preferred_element_type=jnp.float32
    ).astype(jnp.bfloat16)
    attended_grad = attended_grad.reshape(batch_size, local_tok, HEADS, head_dim)
    prob_grad = jnp.einsum(
        "bqhd,bkhd->bhqk", attended_grad, value_rows, preferred_element_type=jnp.float32
    )
    row_dot = jnp.sum(attn_probs * prob_grad, axis=-1, keepdims=True)
    score_grad = (attn_probs * (prob_grad - row_dot) * scale_factor).astype(jnp.bfloat16)
    query_grad = jnp.einsum(
        "bhqk,bkhd->bqhd", score_grad, key_rows, preferred_element_type=jnp.float32
    ).astype(jnp.bfloat16)
    key_part = jnp.einsum(
        "bhqk,bqhd->bkhd", score_grad, queries, preferred_element_type=jnp.float32
    )
    value_part = jnp.einsum(
        "bhqk,bqhd->bkhd", probs_low, attended_grad, preferred_element_type=jnp.float32
    )
    kv_part = jnp.concatenate(
        [key_part.reshape(batch_size, -1, channels), value_part.reshape(batch_size, -1, channels)],
        axis=2,
    )
    kv_grad = kv_part.astype(jnp.bfloat16)
    qkv_grad = jnp.concatenate(
        [query_grad.reshape(batch_size, local_tok, channels), kv_grad], axis=2
    )
    qkv_grad = qkv_grad.reshape(batch_size * local_tok, 3 * channels)
    resid_part = lax.dynamic_slice_in_dim(resid_flat, part * quarter, quarter, axis=1)
    grad_qkv = jnp.einsum("nc,nd->dc", resid_part, qkv_grad, preferred_element_type=jnp.float32)
    resid_grad = out_grad.astype(jnp.float32) + jnp.einsum(
        "nd,cd->nc", qkv_grad, qkv_weight, preferred_element_type=jnp.float32
    )
    resid_grad = resid_grad.reshape(batch_size, row_count, col_count, channels)
    conv_grad = resid_grad.astype(jnp.bfloat16)
    per_image = jnp.sum(conv_grad, axis=(1, 2), dtype=jnp.float32)
    grad_bias = jnp.sum(per_image, axis=0)
    pair_sums = jnp.sum(per_image.reshape(pair_count, 2, channels), axis=1)
    feats_part = lax.dynamic_slice_in_dim(
        time_feats.astype(jnp.float32), part * (TDIM // 4), TDIM // 4, axis=1
    )
    grad_time = jnp.dot(pair_sums.T, feats_part, precision=lax.Precision.HIGHEST)
    conv_flat = conv_grad.reshape(-1, channels)
    padded_part = lax.dynamic_slice_in_dim(padded, part * quarter, quarter, axis=3)
    windows = []
    for row_off in range(3):
        for col_off in range(3):
            windows.append(
                padded_part[
                    :, row_off : row_off + row_count, col_off : col_off + col_count, :
                ].reshape(-1, quarter)
            )
    grad_conv = jnp.einsum(
        "nc,nd->dc",
        jnp.concatenate(windows, axis=1),
        conv_flat,
        preferred_element_type=jnp.float32,
    )
    grad_pad = halo_rows(conv_grad)
    act_grad = jnp.zeros((batch_size * local_tok, channels), jnp.float32)
    for row_off in range(3):
        for col_off in range(3):
            window = grad_pad[
                :, 2 - row_off : 2 - row_off + row_count, 2 - col_off : 2 - col_off + col_count, :
            ].reshape(-1, channels)
            act_grad = act_grad + jnp.einsum(
                "nd,cd->nc",
                window,
                conv_weight[row_off, col_off],
                preferred_element_type=jnp.float32,
            )
    act_grad = act_grad.reshape(batch_size, row_count, col_count, channels)
    sigma = jax.nn.sigmoid(act_in)
    pre_grad = act_grad * (sigma * (1.0 + act_in * (1.0 - sigma)))
    grad_gain = jnp.sum(pre_grad * normed, axis=(0, 1, 2))
    scaled = (pre_grad * norm_gain).reshape(batch_size, row_count, col_count, GROUPS, group_width)
    back_moments = image_sums(
        jnp.stack([jnp.sum(scaled, (1, 2, 4)), jnp.sum(scaled * normed_g, (1, 2, 4))])
    )
    mean_one = back_moments[0] / group_count
    mean_two = back_moments[1] / group_count
    inner_grad = inv_std[:, None, None, :, None] * (
        scaled - mean_one[:, None, None, :, None] - normed_g * mean_two[:, None, None, :, None]
    )
    input_grad = (
        resid_grad + inner_grad.reshape(batch_size, row_count, col_count, channels)
    ).astype(jnp.bfloat16)
    input_grad = lax.dynamic_slice_in_dim(
        input_grad.reshape(section_input.shape), part, 1, axis=2
    ).reshape(in_shape)
    owners = 64
    own = channels // owners
    rows = jnp.concatenate(
        [grad_conv, grad_out, grad_time, grad_gain[:, None], grad_bias[:, None]], axis=1
    ).astype(jnp.bfloat16)
    width = rows.shape[1]
    flat = jnp.concatenate(
        [
            rows.reshape(owners, own * width),
            grad_qkv.astype(jnp.bfloat16).reshape(owners, 3 * own * quarter),
        ],
        axis=1,
    )
    size = flat.shape[1]
    flat = jnp.pad(flat, ((0, 0), (0, CHUNK_ROWS * 128 - size)))
    total = sum_over_pairs(flat.reshape(owners, CHUNK_ROWS, 128))
    whole = lax.all_gather(total, SPACE_AXES, axis=0, tiled=False).reshape(4, -1)
    rows = whole[:, : own * width].reshape(4, own, width)
    qkv_rows = whole[:, own * width : size].reshape(4, 3 * own, quarter)
    conv_rows = rows[:, :, : 9 * quarter].reshape(4, own, 3, 3, quarter)
    conv_rows = conv_rows.transpose(2, 3, 0, 4, 1).reshape(3, 3, channels, own)
    out_rows = rows[:, :, 9 * quarter : 10 * quarter].transpose(0, 2, 1).reshape(channels, own)
    time_rows = rows[:, :, 10 * quarter : 10 * quarter + TDIM // 4]
    time_rows = time_rows.transpose(0, 2, 1).reshape(TDIM, own)
    qkv_out = qkv_rows.transpose(0, 2, 1).reshape(channels, 3 * own)
    return (
        input_grad,
        conv_rows,
        qkv_out,
        out_rows,
        time_rows,
        rows[0, :, width - 2],
        rows[0, :, width - 1],
        pair_loss,
    )


def solution(mesh):
    fine = Mesh(mesh.devices.reshape(4, 8, 2, 2, 2), ("x", "z", "y_hi", "y_lo", "core"))
    placed = (
        P(PAIR_AXES, None, SPACE_AXES, None, None),
        P(PAIR_AXES, None, SPACE_AXES, None, None),
        P(),
        P(),
        P(),
        P(),
        P(),
        P(),
        P(PAIR_AXES),
        P(PAIR_AXES),
        P(PAIR_AXES, None),
    )
    return jax.shard_map(
        on_device,
        mesh=fine,
        in_specs=placed,
        out_specs=(
            P(PAIR_AXES, None, SPACE_AXES, None, None),
            P(None, None, None, PAIR_AXES),
            P(None, PAIR_AXES),
            P(None, PAIR_AXES),
            P(None, PAIR_AXES),
            P(PAIR_AXES),
            P(PAIR_AXES),
            P(PAIR_AXES),
        ),
        check_vma=False,
    )
```

```python
import math

import jax
import jax.numpy as jnp
import numpy as np
from jax import lax
from jax.experimental import pallas as pl
from jax.experimental.pallas import tpu as pltpu
from jax.sharding import Mesh
from jax.sharding import PartitionSpec as P

HEADS = 10
GROUPS = 32
TDIM = 320
C = 640
COLS = 64
ROWS = 4
TOK = 2 * ROWS * COLS
IMG = ROWS * COLS
BAND = 2 * COLS
HEAD_PAIRS = HEADS // 2
GROUP_COUNT = ROWS * COLS * (C // GROUPS)
SCALE = 1.0 / math.sqrt(C // HEADS)
EPS = 1e-05
BETA = 2.0

PAIR_AXES = ("x", "z", "y_hi")
SPACE_AXES = ("y_lo", "core")
MESH_AXES = ("x", "z", "y_hi", "y_lo", "core")
MESH_SHAPE = (4, 8, 2, 2, 2)
OWN = C // 64
TAP_BLOCKS = 12
BLOCKS = 5 + TAP_BLOCKS
WIDTH = BLOCKS * 128
CHUNK = 176
MIB = 1024 * 1024

f32 = jnp.float32
bf16 = jnp.bfloat16

NN = (((1,), (0,)), ((), ()))
NT = (((1,), (1,)), ((), ()))
TN = (((0,), (0,)), ((), ()))


def dot(a, b, dims=NN):
    return lax.dot_general(a, b, dims, preferred_element_type=f32)


def owner_columns():
    n = np.arange(C)
    x, y, z, j = n // 160, (n % 160) // 80, (n % 80) // OWN, n % OWN
    owner = 16 * x + 2 * z + y
    table = np.zeros((8, C), np.int32)
    table[0] = 3 * OWN * owner + j
    table[1] = OWN * owner + j
    return table


def frequencies():
    half = TDIM // 2
    return np.exp(-math.log(10000.0) * (np.arange(TDIM) % half) / half).astype(np.float32)[None]


def row(i):
    return pl.ds(i, 1)


def group_sums(rows):
    a = lax.broadcasted_iota(jnp.int32, (C, C), 0)
    b = lax.broadcasted_iota(jnp.int32, (C, C), 1)
    same = ((a * 3277) >> 16) == ((b * 3277) >> 16)
    ones = jnp.where(same, 1.0, 0.0).astype(bf16)
    high = rows.astype(bf16).astype(f32)
    rest = rows - high
    middle = rest.astype(bf16).astype(f32)
    low = rest - middle
    stack = jnp.concatenate([high, middle, low, jnp.zeros_like(rows)], axis=0).astype(bf16)
    sums = dot(stack, ones)
    return sums[0:4] + sums[4:8] + sums[8:12]


def sigmoid(v):
    return 1.0 / (1.0 + jnp.exp(-v))


def blocks():
    return [(r, m, (2 * r + m) * COLS) for r in range(ROWS) for m in range(2)]


def shifted(v, step):
    at = lax.broadcasted_iota(jnp.int32, (COLS, C), 0)
    if step == 1:
        return jnp.where(at == 0, 0.0, pltpu.roll(v, 1, 0))
    return jnp.where(at == COLS - 1, 0.0, pltpu.roll(v, COLS - 1, 0))


def head_halves(v):
    lane = lax.broadcasted_iota(jnp.int32, (1, 128), 1)
    first = jnp.where(lane < 64, 1.0, 0.0).astype(bf16)
    second = jnp.where(lane < 64, 0.0, 1.0).astype(bf16)
    return jnp.concatenate([v * first, v * second], axis=0)


def head_join(v):
    lane = lax.broadcasted_iota(jnp.int32, (IMG, 128), 1)
    return jnp.where(lane < 64, v[:IMG], v[IMG:])


def pair_kernel(
    part_ref,
    step_ref,
    label_ref,
    error_ref,
    x_ref,
    t_ref,
    conv_ref,
    bias_ref,
    gain_ref,
    qkvw_ref,
    outw_ref,
    timew_ref,
    freq_ref,
    table_ref,
    wire_ref,
    cg_ref,
    own_ref,
    stat_ref,
    margin_ref,
    acat,
    acc,
    resid,
    qkv,
    probs,
    attended,
    dev,
    gall,
    dattn,
    asel,
    feats_s,
):
    part = part_ref[0]
    sums, squares = [], []
    for m in range(2):
        total = jnp.zeros((1, C), f32)
        square = jnp.zeros((1, C), f32)
        for r in range(ROWS):
            v = x_ref[pl.ds((2 * r + m) * COLS, COLS), :].astype(f32)
            total = total + jnp.sum(v, axis=0, keepdims=True)
            square = square + jnp.sum(v * v, axis=0, keepdims=True)
        sums.append(total)
        squares.append(square)
    moments = group_sums(jnp.concatenate(sums + squares, axis=0)) / GROUP_COUNT
    mean = moments[0:2]
    inv = lax.rsqrt(moments[2:4] - mean * mean + EPS)
    stat_ref[...] = jnp.concatenate([mean, inv, jnp.zeros((4, C), f32)], axis=0)
    gain = gain_ref[...]
    acat[0:BAND, :] = jnp.zeros((BAND, 3 * C), bf16)
    acat[pl.ds(BAND + TOK, BAND), :] = jnp.zeros((BAND, 3 * C), bf16)
    for r, m, at in blocks():
        v = x_ref[pl.ds(at, COLS), :].astype(f32)
        a = (v - mean[m : m + 1]) * inv[m : m + 1] * gain
        act = a * sigmoid(a)
        here = pl.ds(BAND + at, COLS)
        acat[here, 0:C] = shifted(act, 1).astype(bf16)
        acat[here, C : 2 * C] = act.astype(bf16)
        acat[here, 2 * C : 3 * C] = shifted(act, -1).astype(bf16)
    angle = step_ref[0].astype(f32) * freq_ref[...]
    lane = lax.broadcasted_iota(jnp.int32, (1, TDIM), 1)
    feats = jnp.where(lane < TDIM // 2, jnp.cos(angle), jnp.sin(angle))
    feats_s[...] = jnp.zeros((8, 384), f32)
    feats_s[0:1, 0:TDIM] = feats
    feats_s[0:1, TDIM : TDIM + 1] = jnp.ones((1, 1), f32)
    shift = dot(jnp.broadcast_to(feats, (16, TDIM)).astype(bf16), timew_ref[...])[0:1]
    offset = shift + bias_ref[...]
    acc[...] = dot(acat[0:TOK, :], conv_ref[0])
    acc[...] += dot(acat[pl.ds(BAND, TOK), :], conv_ref[1])
    acc[...] += dot(acat[pl.ds(2 * BAND, TOK), :], conv_ref[2])
    resid[...] = (x_ref[...].astype(f32) + acc[...] + offset).astype(bf16)
    for third in range(3):
        cols = pl.ds(third * C, C)
        proj = dot(resid[...], qkvw_ref[:, cols]).astype(bf16)
        for r, m, at in blocks():
            qkv[m, pl.ds(r * COLS, COLS), cols] = proj[at : at + COLS]
    for m in range(2):
        for h in range(HEAD_PAIRS):
            q2 = head_halves(qkv[m, :, pl.ds(h * 128, 128)])
            k = qkv[m, :, pl.ds(C + h * 128, 128)]
            v = qkv[m, :, pl.ds(2 * C + h * 128, 128)]
            scores = dot(k, q2, NT) * SCALE
            exps = jnp.exp(scores - jnp.max(scores, axis=0, keepdims=True))
            p = exps * (1.0 / jnp.sum(exps, axis=0, keepdims=True))
            probs[m * HEAD_PAIRS + h] = p
            joined = head_join(dot(p.astype(bf16), v, TN)).astype(bf16)
            for r in range(ROWS):
                attended[pl.ds((2 * r + m) * COLS, COLS), pl.ds(h * 128, 128)] = joined[
                    r * COLS : (r + 1) * COLS
                ]
    dev[...] = (
        resid[...].astype(f32) + dot(attended[...], outw_ref[...]) - t_ref[...].astype(f32)
    )
    margin = jnp.zeros((1, 1), f32)
    signs = []
    for m in range(2):
        total = jnp.zeros((1, C), f32)
        for r in range(ROWS):
            d = dev[pl.ds((2 * r + m) * COLS, COLS), :]
            total = total + jnp.sum(d * d, axis=0, keepdims=True)
        error = jnp.sum(total, axis=1, keepdims=True) / (IMG * C)
        sign = jnp.where(label_ref[0] == m, 1.0, -1.0)
        signs.append(sign)
        margin = margin + sign * (error - error_ref[0, m])
    margin_ref[...] = jnp.broadcast_to(margin, (8, 128))
    slope = BETA * sigmoid(BETA * margin)
    for r, m, at in blocks():
        here = pl.ds(at, COLS)
        gall[here, 3 * C : 4 * C] = (signs[m] * slope * dev[here, :]).astype(bf16)
    out_grad = gall[:, 3 * C : 4 * C]
    da = dot(out_grad, outw_ref[...], NT).astype(bf16)
    for r, m, at in blocks():
        dattn[m, pl.ds(r * COLS, COLS), :] = da[at : at + COLS]
    for m in range(2):
        for h in range(HEAD_PAIRS):
            q2 = head_halves(qkv[m, :, pl.ds(h * 128, 128)])
            k = qkv[m, :, pl.ds(C + h * 128, 128)]
            v = qkv[m, :, pl.ds(2 * C + h * 128, 128)]
            da2 = head_halves(dattn[m, :, pl.ds(h * 128, 128)])
            p = probs[m * HEAD_PAIRS + h]
            dp = dot(v, da2, NT)
            dots = jnp.sum(p * dp, axis=0, keepdims=True)
            ds = (p * (dp - dots) * SCALE).astype(bf16)
            dq = head_join(dot(ds, k, TN)).astype(bf16)
            dk = dot(ds, q2).astype(bf16)
            dv = dot(p.astype(bf16), da2).astype(bf16)
            for r in range(ROWS):
                here = pl.ds((2 * r + m) * COLS, COLS)
                rows = slice(r * COLS, (r + 1) * COLS)
                gall[here, pl.ds(h * 128, 128)] = dq[rows]
                gall[here, pl.ds(C + h * 128, 128)] = dk[rows]
                gall[here, pl.ds(2 * C + h * 128, 128)] = dv[rows]
    acc[...] = out_grad.astype(f32) + dot(gall[:, 0 : 3 * C], qkvw_ref[...], NT)
    cg_ref[...] = acc[...].astype(bf16)
    own_ref[...] = acc[pl.ds(pl.multiple_of(part * BAND, BAND), BAND), :]
    at_row = lax.broadcasted_iota(jnp.int32, (C, C), 0)
    pick = jnp.where(at_row == table_ref[1:2, :], 1.0, 0.0).astype(bf16)
    conv_grad = dot(cg_ref[...], pick).astype(bf16)
    for k in range(TAP_BLOCKS):
        place = part * TAP_BLOCKS + k
        cols = slice(k * 128, (k + 1) * 128)

        def tap(place=place, cols=cols):
            up = place // 15
            lane = pl.multiple_of((place - 15 * up) * 128, 128)
            asel[:, cols] = acat[pl.ds(pl.multiple_of(up * BAND, BAND), TOK), pl.ds(lane, 128)]

        if k < 9:
            tap()
        else:
            pl.when(part < 3)(tap)

            @pl.when(part == 3)
            def _(k=k, cols=cols):
                f = feats_s[0:1, (k - 9) * 128 : (k - 8) * 128]
                asel[:, cols] = jnp.broadcast_to(f, (TOK, 128)).astype(bf16)

    wire_ref[:, C:] = dot(conv_grad, asel[...], TN).astype(bf16)

    @pl.when(part < 3)
    def _():
        rows = lax.broadcasted_iota(jnp.int32, (3 * C, C), 0)
        third = jnp.where(rows == table_ref[0:1, :] + OWN * part, 1.0, 0.0).astype(bf16)
        g = dot(gall[:, 0 : 3 * C], third).astype(bf16)
        wire_ref[:, 0:C] = dot(g, resid[...], TN).astype(bf16)

    @pl.when(part == 3)
    def _():
        g = dot(gall[:, 3 * C : 4 * C], pick).astype(bf16)
        wire_ref[:, 0:C] = dot(g, attended[...], TN).astype(bf16)


def pair_call(part, steps, labels, errors, x, t, conv, bias, gain, qkvw, outw, timew):
    smem = pl.BlockSpec(memory_space=pltpu.SMEM)
    vmem = pl.BlockSpec(memory_space=pltpu.VMEM)
    return pl.pallas_call(
        pair_kernel,
        out_shape=(
            jax.ShapeDtypeStruct((C, WIDTH), bf16),
            jax.ShapeDtypeStruct((TOK, C), bf16),
            jax.ShapeDtypeStruct((BAND, C), f32),
            jax.ShapeDtypeStruct((8, C), f32),
            jax.ShapeDtypeStruct((8, 128), f32),
        ),
        in_specs=[smem] * 4 + [vmem] * 10,
        out_specs=[vmem] * 5,
        scratch_shapes=[
            pltpu.VMEM((TOK + 2 * BAND, 3 * C), bf16),
            pltpu.VMEM((TOK, C), f32),
            pltpu.VMEM((TOK, C), bf16),
            pltpu.VMEM((2, IMG, 3 * C), bf16),
            pltpu.VMEM((2 * HEAD_PAIRS, IMG, 2 * IMG), f32),
            pltpu.VMEM((TOK, C), bf16),
            pltpu.VMEM((TOK, C), f32),
            pltpu.VMEM((TOK, 4 * C), bf16),
            pltpu.VMEM((2, IMG, C), bf16),
            pltpu.VMEM((TOK, TAP_BLOCKS * 128), bf16),
            pltpu.VMEM((8, 384), f32),
        ],
        compiler_params=pltpu.CompilerParams(vmem_limit_bytes=56 * MIB),
        name="pair",
    )(
        part,
        steps,
        labels,
        errors,
        x,
        t,
        conv,
        bias,
        gain,
        qkvw,
        outw,
        timew,
        frequencies(),
        owner_columns(),
    )


def input_kernel(
    part_ref, x_ref, cg_ref, own_ref, stat_ref, gain_ref, conv_ref, in_ref, gg_ref, gcat, acc
):
    part = part_ref[0]
    gcat[0:BAND, :] = jnp.zeros((BAND, 3 * C), bf16)
    gcat[pl.ds(BAND + TOK, BAND), :] = jnp.zeros((BAND, 3 * C), bf16)
    for r, m, at in blocks():
        g = cg_ref[pl.ds(at, COLS), :]
        here = pl.ds(BAND + at, COLS)
        gcat[here, 0:C] = shifted(g.astype(f32), -1).astype(bf16)
        gcat[here, C : 2 * C] = g
        gcat[here, 2 * C : 3 * C] = shifted(g.astype(f32), 1).astype(bf16)
    for i in range(3):
        for j in range(3):
            term = dot(
                gcat[pl.ds((2 - i) * BAND, TOK), j * C : (j + 1) * C],
                conv_ref[i, j * C : (j + 1) * C, :],
                NT,
            )
            if i == 0 and j == 0:
                acc[...] = term
            else:
                acc[...] += term
    gain = gain_ref[...]
    gain_sum = jnp.zeros((1, C), f32)
    ones = [jnp.zeros((1, C), f32) for _ in range(2)]
    twos = [jnp.zeros((1, C), f32) for _ in range(2)]
    for r, m, at in blocks():
        here = pl.ds(at, COLS)
        normed = (x_ref[here, :].astype(f32) - stat_ref[row(m), :]) * stat_ref[row(2 + m), :]
        a = normed * gain
        s = sigmoid(a)
        pre = acc[here, :] * (s * (1.0 + a * (1.0 - s)))
        gain_sum = gain_sum + jnp.sum(pre * normed, axis=0, keepdims=True)
        scaled = pre * gain
        acc[here, :] = scaled
        ones[m] = ones[m] + jnp.sum(scaled, axis=0, keepdims=True)
        twos[m] = twos[m] + jnp.sum(scaled * normed, axis=0, keepdims=True)
    gg_ref[...] = jnp.broadcast_to(gain_sum, (8, C))
    means = group_sums(jnp.concatenate(ones + twos, axis=0)) / GROUP_COUNT
    for m in range(2):
        here = pl.ds(pl.multiple_of(part * BAND + m * COLS, COLS), COLS)
        inv = stat_ref[row(2 + m), :]
        normed = (x_ref[here, :].astype(f32) - stat_ref[row(m), :]) * inv
        inner = inv * (acc[here, :] - means[m : m + 1] - normed * means[2 + m : 3 + m])
        mine = slice(m * COLS, (m + 1) * COLS)
        in_ref[mine, :] = (own_ref[mine, :] + inner).astype(bf16)


def input_call(part, x, cg, own, stat, gain, conv):
    smem = pl.BlockSpec(memory_space=pltpu.SMEM)
    vmem = pl.BlockSpec(memory_space=pltpu.VMEM)
    return pl.pallas_call(
        input_kernel,
        out_shape=(
            jax.ShapeDtypeStruct((BAND, C), bf16),
            jax.ShapeDtypeStruct((8, C), f32),
        ),
        in_specs=[smem] + [vmem] * 6,
        out_specs=[vmem] * 2,
        scratch_shapes=[
            pltpu.VMEM((TOK + 2 * BAND, 3 * C), bf16),
            pltpu.VMEM((TOK, C), f32),
        ],
        compiler_params=pltpu.CompilerParams(vmem_limit_bytes=40 * MIB),
        cost_estimate=pl.CostEstimate(
            flops=2 * TOK * 9 * C * C, bytes_accessed=9 * C * C * 2, transcendentals=TOK * C
        ),
        name="input",
    )(part, x, cg, own, stat, gain, conv)


def half_kernel(a_ref, gain_ref, out_ref, acc, mid):
    total = a_ref[0].astype(f32)
    for i in range(1, 8):
        total = total + a_ref[i].astype(f32)
    acc[...] = total
    mid[:, OWN * BLOCKS :, :] = jnp.zeros((8, CHUNK - OWN * BLOCKS, 128), f32)
    for i in range(8):
        for k in range(BLOCKS):
            mid[i, OWN * k : OWN * (k + 1), :] = acc[
                OWN * i : OWN * (i + 1), 128 * k : 128 * (k + 1)
            ]
        mid[i, OWN * BLOCKS : OWN * BLOCKS + 1, :] = gain_ref[i : i + 1, :]
    out_ref[...] = mid[...].astype(bf16)


def half_call(a, gains):
    vmem = pl.BlockSpec(memory_space=pltpu.VMEM)
    return pl.pallas_call(
        half_kernel,
        out_shape=jax.ShapeDtypeStruct((8, CHUNK, 128), bf16),
        in_specs=[vmem] * 2,
        out_specs=vmem,
        scratch_shapes=[
            pltpu.VMEM((80, WIDTH), f32),
            pltpu.VMEM((8, CHUNK, 128), f32),
        ],
        compiler_params=pltpu.CompilerParams(vmem_limit_bytes=32 * MIB),
        name="half",
    )(a, gains)


def total_kernel(a_ref, out_ref):
    total = a_ref[0].astype(f32)
    for i in range(1, 8):
        total = total + a_ref[i].astype(f32)
    out_ref[...] = total


def total_call(a):
    vmem = pl.BlockSpec(memory_space=pltpu.VMEM)
    return pl.pallas_call(
        total_kernel,
        out_shape=jax.ShapeDtypeStruct((CHUNK, 128), f32),
        in_specs=[vmem],
        out_specs=vmem,
        compiler_params=pltpu.CompilerParams(vmem_limit_bytes=16 * MIB),
        name="total",
    )(a)


def unpack(whole):
    rest = whole[:, : 5 * OWN].reshape(4, 5, OWN, 128)
    qkv = rest[:3].transpose(1, 3, 0, 2).reshape(C, 3 * OWN)
    out = rest[3].transpose(0, 2, 1).reshape(C, OWN)
    taps = whole[:, 5 * OWN : OWN * BLOCKS].reshape(4 * TAP_BLOCKS, OWN, 128)
    conv = taps[:45].reshape(3, 3, 5, OWN, 128).transpose(0, 1, 2, 4, 3).reshape(3, 3, C, OWN)
    tail = taps[45:].transpose(0, 2, 1).reshape(3 * 128, OWN)
    return conv, qkv, out, tail[:TDIM], whole[0, OWN * BLOCKS, :OWN], tail[TDIM]


def on_device(
    section_input,
    target,
    conv_weight,
    conv_bias,
    norm_gain,
    qkv_weight,
    out_weight,
    time_weight,
    timesteps,
    labels,
    ref_error,
):
    part = lax.axis_index(SPACE_AXES).astype(jnp.int32).reshape(1)
    x = lax.all_gather(section_input.reshape(BAND, C), SPACE_AXES, axis=0, tiled=True)
    t = lax.all_gather(target.reshape(BAND, C), SPACE_AXES, axis=0, tiled=True)
    conv = conv_weight.reshape(3, 3 * C, C)
    gain = norm_gain.reshape(1, C)
    wire, cg, own, stat, margin = pair_call(
        part,
        timesteps,
        labels,
        ref_error,
        x,
        t,
        conv,
        conv_bias.reshape(1, C),
        gain,
        qkv_weight,
        out_weight,
        time_weight,
    )
    moved = lax.all_to_all(wire.reshape(8, 80, WIDTH), ("x", "y_hi"), 0, 0)
    input_grad, gains = input_call(part, x, cg, own, stat, gain, conv)
    gains = lax.psum(gains[0], ("x", "y_hi")).reshape(4, 8, 2, OWN)
    gains = lax.dynamic_slice_in_dim(gains, lax.axis_index("x"), 1, 0)
    gains = lax.dynamic_slice_in_dim(gains, lax.axis_index("y_hi"), 1, 2).reshape(8, OWN)
    gains = jnp.pad(gains, ((0, 0), (0, 128 - OWN)))
    moved = lax.all_to_all(half_call(moved, gains), "z", 0, 0)
    whole = lax.all_gather(total_call(moved), SPACE_AXES, axis=0, tiled=False)
    conv_out, qkv_out, out_out, time_out, gain_out, bias_out = unpack(whole)
    pair_loss = jax.nn.softplus(BETA * margin[0, 0:1])
    return (
        input_grad.reshape(section_input.shape),
        conv_out,
        qkv_out,
        out_out,
        time_out,
        gain_out,
        bias_out,
        pair_loss,
    )


def solution(mesh):
    fine = Mesh(mesh.devices.reshape(MESH_SHAPE), MESH_AXES)
    pairs = P(PAIR_AXES)
    rows = P(PAIR_AXES, None, SPACE_AXES, None, None)
    return jax.shard_map(
        on_device,
        mesh=fine,
        in_specs=(rows, rows, P(), P(), P(), P(), P(), P(), pairs, pairs, pairs),
        out_specs=(
            rows,
            P(None, None, None, PAIR_AXES),
            P(None, PAIR_AXES),
            P(None, PAIR_AXES),
            P(None, PAIR_AXES),
            pairs,
            pairs,
            pairs,
        ),
        check_vma=False,
    )
```

```python
import math

import jax
import jax.numpy as jnp
import numpy as np
from jax import lax
from jax.experimental import pallas as pl
from jax.experimental.pallas import tpu as pltpu
from jax.sharding import Mesh
from jax.sharding import PartitionSpec as P

HEADS = 10
GROUPS = 32
TDIM = 320
C = 640
COLS = 64
ROWS = 4
TOK = 2 * ROWS * COLS
IMG = ROWS * COLS
BAND = 2 * COLS
HEAD_PAIRS = HEADS // 2
GROUP_COUNT = ROWS * COLS * (C // GROUPS)
SCALE = 1.0 / math.sqrt(C // HEADS)
EPS = 1e-05
BETA = 2.0

PAIR_AXES = ("x", "z", "y_hi")
SPACE_AXES = ("y_lo", "core")
MESH_AXES = ("x", "z", "y_hi", "y_lo", "core")
MESH_SHAPE = (4, 8, 2, 2, 2)
OWN = C // 64
TAP_BLOCKS = 12
BLOCKS = 5 + TAP_BLOCKS
WIDTH = BLOCKS * 128
CHUNK = 176
MIB = 1024 * 1024
LIMIT = 40

f32 = jnp.float32
bf16 = jnp.bfloat16

NN = (((1,), (0,)), ((), ()))
NT = (((1,), (1,)), ((), ()))
TN = (((0,), (0,)), ((), ()))


def dot(a, b, dims=NN):
    return lax.dot_general(a, b, dims, preferred_element_type=f32)


def frequencies():
    half = TDIM // 2
    return np.exp(-math.log(10000.0) * (np.arange(TDIM) % half) / half).astype(np.float32)[None]


def wire_columns(step, width):
    n = lax.broadcasted_iota(jnp.int32, (160, width), 0)
    y = jnp.where(n >= 80, 1, 0)
    rest = n - 80 * y
    z = (rest * 6554) >> 16
    return 2 * step * z + step * y + rest - OWN * z


def row(i):
    return pl.ds(i, 1)


def group_sums(rows):
    a = lax.broadcasted_iota(jnp.int32, (C, C), 0)
    b = lax.broadcasted_iota(jnp.int32, (C, C), 1)
    same = ((a * 3277) >> 16) == ((b * 3277) >> 16)
    ones = jnp.where(same, 1.0, 0.0).astype(bf16)
    high = rows.astype(bf16).astype(f32)
    rest = rows - high
    middle = rest.astype(bf16).astype(f32)
    low = rest - middle
    stack = jnp.concatenate([high, middle, low, jnp.zeros_like(rows)], axis=0).astype(bf16)
    sums = dot(stack, ones)
    return sums[0:4] + sums[4:8] + sums[8:12]


def sigmoid(v):
    return 1.0 / (1.0 + jnp.exp(-v))


def blocks():
    return [(r, m, (2 * r + m) * COLS) for r in range(ROWS) for m in range(2)]


def shifted(v, step):
    at = lax.broadcasted_iota(jnp.int32, (COLS, C), 0)
    if step == 1:
        return jnp.where(at == 0, 0.0, pltpu.roll(v, 1, 0))
    return jnp.where(at == COLS - 1, 0.0, pltpu.roll(v, COLS - 1, 0))


def head_halves(v):
    lane = lax.broadcasted_iota(jnp.int32, (1, 128), 1)
    first = jnp.where(lane < 64, 1.0, 0.0).astype(bf16)
    second = jnp.where(lane < 64, 0.0, 1.0).astype(bf16)
    return jnp.concatenate([v * first, v * second], axis=0)


def head_join(v):
    lane = lax.broadcasted_iota(jnp.int32, (IMG, 128), 1)
    return jnp.where(lane < 64, v[:IMG], v[IMG:])


def pair_kernel(
    part_ref,
    step_ref,
    label_ref,
    error_ref,
    x_ref,
    t_ref,
    conv_ref,
    bias_ref,
    gain_ref,
    qkvw_ref,
    outw_ref,
    timew_ref,
    freq_ref,
    wire_ref,
    cg_ref,
    own_ref,
    stat_ref,
    margin_ref,
    acat,
    acc,
    resid,
    qkv,
    probs,
    attended,
    dev,
    gall,
    dattn,
    asel,
    feats_s,
    turned,
):
    part = part_ref[0]
    sums, squares = [], []
    for m in range(2):
        total = jnp.zeros((1, C), f32)
        square = jnp.zeros((1, C), f32)
        for r in range(ROWS):
            v = x_ref[pl.ds((2 * r + m) * COLS, COLS), :].astype(f32)
            total = total + jnp.sum(v, axis=0, keepdims=True)
            square = square + jnp.sum(v * v, axis=0, keepdims=True)
        sums.append(total)
        squares.append(square)
    moments = group_sums(jnp.concatenate(sums + squares, axis=0)) / GROUP_COUNT
    mean = moments[0:2]
    inv = lax.rsqrt(moments[2:4] - mean * mean + EPS)
    stat_ref[...] = jnp.concatenate([mean, inv, jnp.zeros((4, C), f32)], axis=0)
    gain = gain_ref[...].reshape(1, C)
    acat[0:BAND, :] = jnp.zeros((BAND, 3 * C), bf16)
    acat[pl.ds(BAND + TOK, BAND), :] = jnp.zeros((BAND, 3 * C), bf16)
    for r, m, at in blocks():
        v = x_ref[pl.ds(at, COLS), :].astype(f32)
        a = (v - mean[m : m + 1]) * inv[m : m + 1] * gain
        act = a * sigmoid(a)
        here = pl.ds(BAND + at, COLS)
        acat[here, 0:C] = shifted(act, 1).astype(bf16)
        acat[here, C : 2 * C] = act.astype(bf16)
        acat[here, 2 * C : 3 * C] = shifted(act, -1).astype(bf16)
    angle = step_ref[0].astype(f32) * freq_ref[...]
    lane = lax.broadcasted_iota(jnp.int32, (1, TDIM), 1)
    feats = jnp.where(lane < TDIM // 2, jnp.cos(angle), jnp.sin(angle))
    feats_s[...] = jnp.zeros((8, 384), f32)
    feats_s[0:1, 0:TDIM] = feats
    shift = dot(jnp.broadcast_to(feats, (16, TDIM)).astype(bf16), timew_ref[...])[0:1]
    offset = shift + bias_ref[...].reshape(1, C)
    acc[...] = dot(acat[0:TOK, :], conv_ref[0])
    acc[...] += dot(acat[pl.ds(BAND, TOK), :], conv_ref[1])
    acc[...] += dot(acat[pl.ds(2 * BAND, TOK), :], conv_ref[2])
    resid[...] = (x_ref[...].astype(f32) + acc[...] + offset).astype(bf16)
    for third in range(3):
        cols = pl.ds(third * C, C)
        proj = dot(resid[...], qkvw_ref[:, cols]).astype(bf16)
        for r, m, at in blocks():
            qkv[m, pl.ds(r * COLS, COLS), cols] = proj[at : at + COLS]
    for m in range(2):
        for h in range(HEAD_PAIRS):
            q2 = head_halves(qkv[m, :, pl.ds(h * 128, 128)])
            k = qkv[m, :, pl.ds(C + h * 128, 128)]
            v = qkv[m, :, pl.ds(2 * C + h * 128, 128)]
            scores = dot(k, q2, NT) * SCALE
            exps = jnp.exp(scores - jnp.max(scores, axis=0, keepdims=True))
            p = exps * (1.0 / jnp.sum(exps, axis=0, keepdims=True))
            probs[m * HEAD_PAIRS + h] = p
            joined = head_join(dot(p.astype(bf16), v, TN)).astype(bf16)
            for r in range(ROWS):
                attended[pl.ds((2 * r + m) * COLS, COLS), pl.ds(h * 128, 128)] = joined[
                    r * COLS : (r + 1) * COLS
                ]
    dev[...] = (
        resid[...].astype(f32) + dot(attended[...], outw_ref[...]) - t_ref[...].astype(f32)
    )
    margin = jnp.zeros((1, 1), f32)
    signs = []
    for m in range(2):
        total = jnp.zeros((1, C), f32)
        for r in range(ROWS):
            d = dev[pl.ds((2 * r + m) * COLS, COLS), :]
            total = total + jnp.sum(d * d, axis=0, keepdims=True)
        error = jnp.sum(total, axis=1, keepdims=True) / (IMG * C)
        sign = jnp.where(label_ref[0] == m, 1.0, -1.0)
        signs.append(sign)
        margin = margin + sign * (error - error_ref[0, m])
    margin_ref[...] = jnp.broadcast_to(margin, (8, 128))
    slope = BETA * sigmoid(BETA * margin)
    for r, m, at in blocks():
        here = pl.ds(at, COLS)
        gall[here, 3 * C : 4 * C] = (signs[m] * slope * dev[here, :]).astype(bf16)
    out_grad = gall[:, 3 * C : 4 * C]
    da = dot(out_grad, outw_ref[...], NT).astype(bf16)
    for r, m, at in blocks():
        dattn[m, pl.ds(r * COLS, COLS), :] = da[at : at + COLS]
    for m in range(2):
        for h in range(HEAD_PAIRS):
            q2 = head_halves(qkv[m, :, pl.ds(h * 128, 128)])
            k = qkv[m, :, pl.ds(C + h * 128, 128)]
            v = qkv[m, :, pl.ds(2 * C + h * 128, 128)]
            da2 = head_halves(dattn[m, :, pl.ds(h * 128, 128)])
            p = probs[m * HEAD_PAIRS + h]
            dp = dot(v, da2, NT)
            dots = jnp.sum(p * dp, axis=0, keepdims=True)
            ds = (p * (dp - dots) * SCALE).astype(bf16)
            dq = head_join(dot(ds, k, TN)).astype(bf16)
            dk = dot(ds, q2).astype(bf16)
            dv = dot(p.astype(bf16), da2).astype(bf16)
            for r in range(ROWS):
                here = pl.ds((2 * r + m) * COLS, COLS)
                rows = slice(r * COLS, (r + 1) * COLS)
                gall[here, pl.ds(h * 128, 128)] = dq[rows]
                gall[here, pl.ds(C + h * 128, 128)] = dk[rows]
                gall[here, pl.ds(2 * C + h * 128, 128)] = dv[rows]
    acc[...] = out_grad.astype(f32) + dot(gall[:, 0 : 3 * C], qkvw_ref[...], NT)
    cg_ref[...] = acc[...].astype(bf16)
    own_ref[...] = acc[pl.ds(pl.multiple_of(part * BAND, BAND), BAND), :]
    lane = lax.broadcasted_iota(jnp.int32, (160, 2 * IMG), 1)
    own_cols = wire_columns(OWN, 2 * IMG)[:, 0:IMG]
    for x in range(4):
        low = 128 * x
        pick = jnp.where(lane[:, 0:IMG] == own_cols + 32 * x, 1.0, 0.0).astype(bf16)
        turned[160 * x : 160 * (x + 1), :] = dot(pick, cg_ref[:, low : low + IMG], NT).astype(bf16)
    for k in range(TAP_BLOCKS):
        place = part * TAP_BLOCKS + k
        cols = slice(k * 128, (k + 1) * 128)

        def tap(place=place, cols=cols):
            up = place // 15
            lane = pl.multiple_of((place - 15 * up) * 128, 128)
            asel[:, cols] = acat[pl.ds(pl.multiple_of(up * BAND, BAND), TOK), pl.ds(lane, 128)]

        if k < 9:
            tap()
        else:
            pl.when(part < 3)(tap)

            @pl.when(part == 3)
            def _(k=k, cols=cols):
                f = feats_s[0:1, (k - 9) * 128 : (k - 8) * 128]
                asel[:, cols] = jnp.broadcast_to(f, (TOK, 128)).astype(bf16)

    wire_ref[:, C:] = dot(turned[...], asel[...]).astype(bf16)

    @pl.when(part < 3)
    def _():
        at = lax.broadcasted_iota(jnp.int32, (160, C), 1)
        cols = wire_columns(3 * OWN, C) + OWN * part
        for x, low in enumerate((0, 384, 896, 1280)):
            pick = jnp.where(at == cols + (480 * x - low), 1.0, 0.0).astype(bf16)
            turned[160 * x : 160 * (x + 1), :] = dot(pick, gall[:, low : low + C], NT).astype(bf16)
        wire_ref[:, 0:C] = dot(turned[...], resid[...]).astype(bf16)

    @pl.when(part == 3)
    def _():
        for x in range(4):
            low = 3 * C + 128 * x
            pick = jnp.where(lane[:, 0:IMG] == own_cols + 32 * x, 1.0, 0.0).astype(bf16)
            turned[160 * x : 160 * (x + 1), :] = dot(pick, gall[:, low : low + IMG], NT).astype(
                bf16
            )
        wire_ref[:, 0:C] = dot(turned[...], attended[...]).astype(bf16)


def pair_call(part, steps, labels, errors, x, t, conv, bias, gain, qkvw, outw, timew):
    smem = pl.BlockSpec(memory_space=pltpu.SMEM)
    vmem = pl.BlockSpec(memory_space=pltpu.VMEM)
    return pl.pallas_call(
        pair_kernel,
        out_shape=(
            jax.ShapeDtypeStruct((C, WIDTH), bf16),
            jax.ShapeDtypeStruct((TOK, C), bf16),
            jax.ShapeDtypeStruct((BAND, C), f32),
            jax.ShapeDtypeStruct((8, C), f32),
            jax.ShapeDtypeStruct((8, 128), f32),
        ),
        in_specs=[smem] * 4 + [vmem] * 9,
        out_specs=[vmem] * 5,
        scratch_shapes=[
            pltpu.VMEM((TOK + 2 * BAND, 3 * C), bf16),
            pltpu.VMEM((TOK, C), f32),
            pltpu.VMEM((TOK, C), bf16),
            pltpu.VMEM((2, IMG, 3 * C), bf16),
            pltpu.VMEM((2 * HEAD_PAIRS, IMG, 2 * IMG), f32),
            pltpu.VMEM((TOK, C), bf16),
            pltpu.VMEM((TOK, C), f32),
            pltpu.VMEM((TOK, 4 * C), bf16),
            pltpu.VMEM((2, IMG, C), bf16),
            pltpu.VMEM((TOK, TAP_BLOCKS * 128), bf16),
            pltpu.VMEM((8, 384), f32),
            pltpu.VMEM((C, TOK), bf16),
        ],
        compiler_params=pltpu.CompilerParams(vmem_limit_bytes=LIMIT * MIB),
        name="pair",
    )(
        part,
        steps,
        labels,
        errors,
        x,
        t,
        conv,
        bias,
        gain,
        qkvw,
        outw,
        timew,
        frequencies(),
    )


def input_kernel(
    part_ref, x_ref, cg_ref, own_ref, stat_ref, gain_ref, conv_ref, in_ref, gg_ref, gcat, acc
):
    part = part_ref[0]
    gcat[0:BAND, :] = jnp.zeros((BAND, 3 * C), bf16)
    gcat[pl.ds(BAND + TOK, BAND), :] = jnp.zeros((BAND, 3 * C), bf16)
    for r, m, at in blocks():
        g = cg_ref[pl.ds(at, COLS), :]
        here = pl.ds(BAND + at, COLS)
        gcat[here, 0:C] = shifted(g.astype(f32), -1).astype(bf16)
        gcat[here, C : 2 * C] = g
        gcat[here, 2 * C : 3 * C] = shifted(g.astype(f32), 1).astype(bf16)
    for i in range(3):
        for j in range(3):
            term = dot(
                gcat[pl.ds((2 - i) * BAND, TOK), j * C : (j + 1) * C],
                conv_ref[i, j * C : (j + 1) * C, :],
                NT,
            )
            if i == 0 and j == 0:
                acc[...] = term
            else:
                acc[...] += term
    gain = gain_ref[...].reshape(1, C)
    gain_sum = jnp.zeros((1, C), f32)
    ones = [jnp.zeros((1, C), f32) for _ in range(2)]
    twos = [jnp.zeros((1, C), f32) for _ in range(2)]
    for r, m, at in blocks():
        here = pl.ds(at, COLS)
        normed = (x_ref[here, :].astype(f32) - stat_ref[row(m), :]) * stat_ref[row(2 + m), :]
        a = normed * gain
        s = sigmoid(a)
        pre = acc[here, :] * (s * (1.0 + a * (1.0 - s)))
        gain_sum = gain_sum + jnp.sum(pre * normed, axis=0, keepdims=True)
        scaled = pre * gain
        acc[here, :] = scaled
        ones[m] = ones[m] + jnp.sum(scaled, axis=0, keepdims=True)
        twos[m] = twos[m] + jnp.sum(scaled * normed, axis=0, keepdims=True)
    bias_sum = jnp.sum(cg_ref[...].astype(f32), axis=0, keepdims=True)
    gg_ref[...] = jnp.concatenate([gain_sum, bias_sum], axis=0)
    means = group_sums(jnp.concatenate(ones + twos, axis=0)) / GROUP_COUNT
    for m in range(2):
        here = pl.ds(pl.multiple_of(part * BAND + m * COLS, COLS), COLS)
        inv = stat_ref[row(2 + m), :]
        normed = (x_ref[here, :].astype(f32) - stat_ref[row(m), :]) * inv
        inner = inv * (acc[here, :] - means[m : m + 1] - normed * means[2 + m : 3 + m])
        mine = slice(m * COLS, (m + 1) * COLS)
        in_ref[mine, :] = (own_ref[mine, :] + inner).astype(bf16)


def input_call(part, x, cg, own, stat, gain, conv):
    smem = pl.BlockSpec(memory_space=pltpu.SMEM)
    vmem = pl.BlockSpec(memory_space=pltpu.VMEM)
    return pl.pallas_call(
        input_kernel,
        out_shape=(
            jax.ShapeDtypeStruct((BAND, C), bf16),
            jax.ShapeDtypeStruct((2, C), f32),
        ),
        in_specs=[smem] + [vmem] * 6,
        out_specs=[vmem] * 2,
        scratch_shapes=[
            pltpu.VMEM((TOK + 2 * BAND, 3 * C), bf16),
            pltpu.VMEM((TOK, C), f32),
        ],
        compiler_params=pltpu.CompilerParams(vmem_limit_bytes=40 * MIB),
        cost_estimate=pl.CostEstimate(
            flops=2 * TOK * 9 * C * C, bytes_accessed=9 * C * C * 2, transcendentals=TOK * C
        ),
        name="input",
    )(part, x, cg, own, stat, gain, conv)


def half_kernel(a_ref, out_ref, acc, mid):
    total = a_ref[0].astype(f32)
    for i in range(1, 8):
        total = total + a_ref[i].astype(f32)
    acc[...] = total
    mid[:, OWN * BLOCKS :, :] = jnp.zeros((8, CHUNK - OWN * BLOCKS, 128), f32)
    for i in range(8):
        for k in range(BLOCKS):
            mid[i, OWN * k : OWN * (k + 1), :] = acc[
                OWN * i : OWN * (i + 1), 128 * k : 128 * (k + 1)
            ]
    out_ref[...] = mid[...].astype(bf16)


def half_call(a):
    vmem = pl.BlockSpec(memory_space=pltpu.VMEM)
    return pl.pallas_call(
        half_kernel,
        out_shape=jax.ShapeDtypeStruct((8, CHUNK, 128), bf16),
        in_specs=[vmem],
        out_specs=vmem,
        scratch_shapes=[
            pltpu.VMEM((80, WIDTH), f32),
            pltpu.VMEM((8, CHUNK, 128), f32),
        ],
        compiler_params=pltpu.CompilerParams(vmem_limit_bytes=32 * MIB),
        name="half",
    )(a)


def total_kernel(a_ref, out_ref):
    total = a_ref[0].astype(f32)
    for i in range(1, 8):
        total = total + a_ref[i].astype(f32)
    out_ref[...] = total


def total_call(a):
    vmem = pl.BlockSpec(memory_space=pltpu.VMEM)
    return pl.pallas_call(
        total_kernel,
        out_shape=jax.ShapeDtypeStruct((CHUNK, 128), f32),
        in_specs=[vmem],
        out_specs=vmem,
        compiler_params=pltpu.CompilerParams(vmem_limit_bytes=16 * MIB),
        name="total",
    )(a)


def unpack_kernel(all_ref, conv_ref, qkv_ref, out_ref, time_ref):
    for part in range(4):
        for k in range(5):
            rows = all_ref[part, OWN * k : OWN * (k + 1), :]
            cols = slice(128 * k, 128 * (k + 1))
            if part < 3:
                qkv_ref[OWN * part : OWN * (part + 1), cols] = rows
            else:
                out_ref[:, cols] = rows
        for k in range(TAP_BLOCKS):
            rows = all_ref[part, OWN * (5 + k) : OWN * (6 + k), :]
            place = part * TAP_BLOCKS + k
            tap, block = place // 5, place % 5
            if place < 45:
                conv_ref[tap // 3, :, tap % 3, 128 * block : 128 * (block + 1)] = rows
            else:
                wide = min(128, TDIM - 128 * (place - 45))
                low = 128 * (place - 45)
                time_ref[:, low : low + wide] = rows[:, 0:wide]


def unpack_call(whole):
    vmem = pl.BlockSpec(memory_space=pltpu.VMEM)
    return pl.pallas_call(
        unpack_kernel,
        out_shape=(
            jax.ShapeDtypeStruct((3, OWN, 3, C), f32),
            jax.ShapeDtypeStruct((3 * OWN, C), f32),
            jax.ShapeDtypeStruct((OWN, C), f32),
            jax.ShapeDtypeStruct((OWN, TDIM), f32),
        ),
        in_specs=[vmem],
        out_specs=[vmem] * 4,
        compiler_params=pltpu.CompilerParams(vmem_limit_bytes=16 * MIB),
        name="unpack",
    )(whole)


def on_device(
    section_input,
    target,
    conv_weight,
    conv_bias,
    norm_gain,
    qkv_weight,
    out_weight,
    time_weight,
    timesteps,
    labels,
    ref_error,
):
    part = lax.axis_index(SPACE_AXES).astype(jnp.int32).reshape(1)
    x = lax.all_gather(section_input.reshape(BAND, C), SPACE_AXES, axis=0, tiled=True)
    t = lax.all_gather(target.reshape(BAND, C), SPACE_AXES, axis=0, tiled=True)
    conv = conv_weight.reshape(3, 3 * C, C)
    wire, cg, own, stat, margin = pair_call(
        part,
        timesteps,
        labels,
        ref_error,
        x,
        t,
        conv,
        conv_bias,
        norm_gain,
        qkv_weight,
        out_weight,
        time_weight,
    )
    moved = lax.all_to_all(wire.reshape(8, 80, WIDTH), ("x", "y_hi"), 0, 0)
    input_grad, gains = input_call(part, x, cg, own, stat, norm_gain, conv)
    gains = lax.psum(gains, "z")
    moved = lax.all_to_all(half_call(moved), "z", 0, 0)
    gains = lax.psum(gains, ("x", "y_hi"))
    gains = lax.dynamic_slice_in_dim(gains, lax.axis_index(PAIR_AXES) * OWN, OWN, 1)
    whole = lax.all_gather(total_call(moved), SPACE_AXES, axis=0, tiled=False)
    conv_out, qkv_out, out_out, time_out = unpack_call(whole)
    pair_loss = jax.nn.softplus(BETA * margin[0, 0:1])
    return (
        input_grad.reshape(section_input.shape),
        conv_out.transpose(0, 2, 3, 1),
        qkv_out.T,
        out_out.T,
        time_out.T,
        gains[0],
        gains[1],
        pair_loss,
    )


def solution(mesh):
    fine = Mesh(mesh.devices.reshape(MESH_SHAPE), MESH_AXES)
    pairs = P(PAIR_AXES)
    rows = P(PAIR_AXES, None, SPACE_AXES, None, None)
    return jax.shard_map(
        on_device,
        mesh=fine,
        in_specs=(rows, rows, P(), P(), P(), P(), P(), P(), pairs, pairs, pairs),
        out_specs=(
            rows,
            P(None, None, None, PAIR_AXES),
            P(None, PAIR_AXES),
            P(None, PAIR_AXES),
            P(None, PAIR_AXES),
            pairs,
            pairs,
            pairs,
        ),
        check_vma=False,
    )
```

```python
import math

import jax
import jax.numpy as jnp
import numpy as np
from jax import lax
from jax.experimental import pallas as pl
from jax.experimental.pallas import tpu as pltpu
from jax.sharding import Mesh
from jax.sharding import PartitionSpec as P

HEADS = 10
GROUPS = 32
TDIM = 320
C = 640
COLS = 64
ROWS = 4
TOK = 2 * ROWS * COLS
IMG = ROWS * COLS
BAND = 2 * COLS
HEAD_PAIRS = HEADS // 2
GROUP_COUNT = ROWS * COLS * (C // GROUPS)
SCALE = 1.0 / math.sqrt(C // HEADS)
EPS = 1e-05
BETA = 2.0

PAIR_AXES = ("x", "z", "y_hi")
SPACE_AXES = ("y_lo", "core")
MESH_AXES = ("x", "z", "y_hi", "y_lo", "core")
MESH_SHAPE = (4, 8, 2, 2, 2)
OWN = C // 64
TAP_BLOCKS = 12
BLOCKS = 5 + TAP_BLOCKS
WIDTH = BLOCKS * 128
CHUNK = 176
MIB = 1024 * 1024
LIMIT = 56

f32 = jnp.float32
bf16 = jnp.bfloat16

NN = (((1,), (0,)), ((), ()))
NT = (((1,), (1,)), ((), ()))
TN = (((0,), (0,)), ((), ()))


def dot(a, b, dims=NN):
    return lax.dot_general(a, b, dims, preferred_element_type=f32)


def frequencies():
    half = TDIM // 2
    return np.exp(-math.log(10000.0) * (np.arange(TDIM) % half) / half).astype(np.float32)[None]


def wire_columns(step, width):
    n = lax.broadcasted_iota(jnp.int32, (160, width), 0)
    y = jnp.where(n >= 80, 1, 0)
    rest = n - 80 * y
    z = (rest * 6554) >> 16
    return 2 * step * z + step * y + rest - OWN * z


def row(i):
    return pl.ds(i, 1)


def group_sums(rows):
    a = lax.broadcasted_iota(jnp.int32, (C, C), 0)
    b = lax.broadcasted_iota(jnp.int32, (C, C), 1)
    same = ((a * 3277) >> 16) == ((b * 3277) >> 16)
    ones = jnp.where(same, 1.0, 0.0).astype(bf16)
    high = rows.astype(bf16).astype(f32)
    rest = rows - high
    middle = rest.astype(bf16).astype(f32)
    low = rest - middle
    stack = jnp.concatenate([high, middle, low, jnp.zeros_like(rows)], axis=0).astype(bf16)
    sums = dot(stack, ones)
    return sums[0:4] + sums[4:8] + sums[8:12]


def sigmoid(v):
    return 1.0 / (1.0 + jnp.exp(-v))


def blocks():
    return [(r, m, (2 * r + m) * COLS) for r in range(ROWS) for m in range(2)]


def shifted(v, step):
    at = lax.broadcasted_iota(jnp.int32, (COLS, C), 0)
    if step == 1:
        return jnp.where(at == 0, 0.0, pltpu.roll(v, 1, 0))
    return jnp.where(at == COLS - 1, 0.0, pltpu.roll(v, COLS - 1, 0))


def head_halves(v):
    lane = lax.broadcasted_iota(jnp.int32, (1, 128), 1)
    first = jnp.where(lane < 64, 1.0, 0.0).astype(bf16)
    second = jnp.where(lane < 64, 0.0, 1.0).astype(bf16)
    return jnp.concatenate([v * first, v * second], axis=0)


def head_join(v):
    lane = lax.broadcasted_iota(jnp.int32, (IMG, 128), 1)
    return jnp.where(lane < 64, v[:IMG], v[IMG:])


def pair_kernel(
    part_ref,
    step_ref,
    label_ref,
    error_ref,
    x_ref,
    t_ref,
    conv_ref,
    bias_ref,
    gain_ref,
    qkvw_ref,
    outw_ref,
    timew_ref,
    freq_ref,
    wire_ref,
    cg_ref,
    own_ref,
    stat_ref,
    margin_ref,
    acat,
    acc,
    resid,
    qkv,
    probs,
    attended,
    dev,
    gall,
    dattn,
    asel,
    feats_s,
    turned,
    wire_s,
    cg_s,
    own_s,
    t_s,
    conv_s,
    qkvw_s,
    outw_s,
    timew_s,
    sems,
):
    part = part_ref[0]
    taps = [pltpu.make_async_copy(conv_ref.at[i], conv_s.at[i], sems.at[i]) for i in range(3)]
    load_time = pltpu.make_async_copy(timew_ref, timew_s, sems.at[3])
    load_qkv = pltpu.make_async_copy(qkvw_ref, qkvw_s, sems.at[4])
    load_out = pltpu.make_async_copy(outw_ref, outw_s, sems.at[5])
    load_t = pltpu.make_async_copy(t_ref, t_s, sems.at[6])
    taps[0].start()
    load_time.start()
    taps[1].start()
    sums, squares = [], []
    for m in range(2):
        total = jnp.zeros((1, C), f32)
        square = jnp.zeros((1, C), f32)
        for r in range(ROWS):
            v = x_ref[pl.ds((2 * r + m) * COLS, COLS), :].astype(f32)
            total = total + jnp.sum(v, axis=0, keepdims=True)
            square = square + jnp.sum(v * v, axis=0, keepdims=True)
        sums.append(total)
        squares.append(square)
    moments = group_sums(jnp.concatenate(sums + squares, axis=0)) / GROUP_COUNT
    mean = moments[0:2]
    inv = lax.rsqrt(moments[2:4] - mean * mean + EPS)
    stat_ref[...] = jnp.concatenate([mean, inv, jnp.zeros((4, C), f32)], axis=0)
    gain = gain_ref[...].reshape(1, C)
    acat[0:BAND, :] = jnp.zeros((BAND, 3 * C), bf16)
    acat[pl.ds(BAND + TOK, BAND), :] = jnp.zeros((BAND, 3 * C), bf16)
    for r, m, at in blocks():
        v = x_ref[pl.ds(at, COLS), :].astype(f32)
        a = (v - mean[m : m + 1]) * inv[m : m + 1] * gain
        act = a * sigmoid(a)
        here = pl.ds(BAND + at, COLS)
        acat[here, 0:C] = shifted(act, 1).astype(bf16)
        acat[here, C : 2 * C] = act.astype(bf16)
        acat[here, 2 * C : 3 * C] = shifted(act, -1).astype(bf16)
    angle = step_ref[0].astype(f32) * freq_ref[...]
    lane = lax.broadcasted_iota(jnp.int32, (1, TDIM), 1)
    feats = jnp.where(lane < TDIM // 2, jnp.cos(angle), jnp.sin(angle))
    feats_s[...] = jnp.zeros((8, 384), f32)
    feats_s[0:1, 0:TDIM] = feats
    load_time.wait()
    shift = dot(jnp.broadcast_to(feats, (16, TDIM)).astype(bf16), timew_s[...])[0:1]
    offset = shift + bias_ref[...].reshape(1, C)
    taps[0].wait()
    taps[2].start()
    load_qkv.start()
    acc[...] = dot(acat[0:TOK, :], conv_s[0])
    taps[1].wait()
    acc[...] += dot(acat[pl.ds(BAND, TOK), :], conv_s[1])
    taps[2].wait()
    acc[...] += dot(acat[pl.ds(2 * BAND, TOK), :], conv_s[2])
    resid[...] = (x_ref[...].astype(f32) + acc[...] + offset).astype(bf16)
    load_qkv.wait()
    load_out.start()
    load_t.start()
    for third in range(3):
        cols = pl.ds(third * C, C)
        proj = dot(resid[...], qkvw_s[:, cols]).astype(bf16)
        for r, m, at in blocks():
            qkv[m, pl.ds(r * COLS, COLS), cols] = proj[at : at + COLS]
    for m in range(2):
        for h in range(HEAD_PAIRS):
            q2 = head_halves(qkv[m, :, pl.ds(h * 128, 128)])
            k = qkv[m, :, pl.ds(C + h * 128, 128)]
            v = qkv[m, :, pl.ds(2 * C + h * 128, 128)]
            scores = dot(k, q2, NT) * SCALE
            exps = jnp.exp(scores - jnp.max(scores, axis=0, keepdims=True))
            p = exps * (1.0 / jnp.sum(exps, axis=0, keepdims=True))
            probs[m * HEAD_PAIRS + h] = p
            joined = head_join(dot(p.astype(bf16), v, TN)).astype(bf16)
            for r in range(ROWS):
                attended[pl.ds((2 * r + m) * COLS, COLS), pl.ds(h * 128, 128)] = joined[
                    r * COLS : (r + 1) * COLS
                ]
    load_out.wait()
    load_t.wait()
    dev[...] = (
        resid[...].astype(f32) + dot(attended[...], outw_s[...]) - t_s[...].astype(f32)
    )
    margin = jnp.zeros((1, 1), f32)
    signs = []
    for m in range(2):
        total = jnp.zeros((1, C), f32)
        for r in range(ROWS):
            d = dev[pl.ds((2 * r + m) * COLS, COLS), :]
            total = total + jnp.sum(d * d, axis=0, keepdims=True)
        error = jnp.sum(total, axis=1, keepdims=True) / (IMG * C)
        sign = jnp.where(label_ref[0] == m, 1.0, -1.0)
        signs.append(sign)
        margin = margin + sign * (error - error_ref[0, m])
    margin_ref[...] = jnp.broadcast_to(margin, (8, 128))
    slope = BETA * sigmoid(BETA * margin)
    for r, m, at in blocks():
        here = pl.ds(at, COLS)
        gall[here, 3 * C : 4 * C] = (signs[m] * slope * dev[here, :]).astype(bf16)
    out_grad = gall[:, 3 * C : 4 * C]
    da = dot(out_grad, outw_s[...], NT).astype(bf16)
    for r, m, at in blocks():
        dattn[m, pl.ds(r * COLS, COLS), :] = da[at : at + COLS]
    for m in range(2):
        for h in range(HEAD_PAIRS):
            q2 = head_halves(qkv[m, :, pl.ds(h * 128, 128)])
            k = qkv[m, :, pl.ds(C + h * 128, 128)]
            v = qkv[m, :, pl.ds(2 * C + h * 128, 128)]
            da2 = head_halves(dattn[m, :, pl.ds(h * 128, 128)])
            p = probs[m * HEAD_PAIRS + h]
            dp = dot(v, da2, NT)
            dots = jnp.sum(p * dp, axis=0, keepdims=True)
            ds = (p * (dp - dots) * SCALE).astype(bf16)
            dq = head_join(dot(ds, k, TN)).astype(bf16)
            dk = dot(ds, q2).astype(bf16)
            dv = dot(p.astype(bf16), da2).astype(bf16)
            for r in range(ROWS):
                here = pl.ds((2 * r + m) * COLS, COLS)
                rows = slice(r * COLS, (r + 1) * COLS)
                gall[here, pl.ds(h * 128, 128)] = dq[rows]
                gall[here, pl.ds(C + h * 128, 128)] = dk[rows]
                gall[here, pl.ds(2 * C + h * 128, 128)] = dv[rows]
    acc[...] = out_grad.astype(f32) + dot(gall[:, 0 : 3 * C], qkvw_s[...], NT)
    cg_s[...] = acc[...].astype(bf16)
    own_s[...] = acc[pl.ds(pl.multiple_of(part * BAND, BAND), BAND), :]
    stores = [
        pltpu.make_async_copy(cg_s, cg_ref, sems.at[7]),
        pltpu.make_async_copy(own_s, own_ref, sems.at[8]),
    ]
    for store in stores:
        store.start()
    lane = lax.broadcasted_iota(jnp.int32, (160, 2 * IMG), 1)
    own_cols = wire_columns(OWN, 2 * IMG)[:, 0:IMG]
    for x in range(4):
        low = 128 * x
        pick = jnp.where(lane[:, 0:IMG] == own_cols + 32 * x, 1.0, 0.0).astype(bf16)
        turned[160 * x : 160 * (x + 1), :] = dot(pick, cg_s[:, low : low + IMG], NT).astype(bf16)
    for k in range(TAP_BLOCKS):
        place = part * TAP_BLOCKS + k
        cols = slice(k * 128, (k + 1) * 128)

        def tap(place=place, cols=cols):
            up = place // 15
            lane = pl.multiple_of((place - 15 * up) * 128, 128)
            asel[:, cols] = acat[pl.ds(pl.multiple_of(up * BAND, BAND), TOK), pl.ds(lane, 128)]

        if k < 9:
            tap()
        else:
            pl.when(part < 3)(tap)

            @pl.when(part == 3)
            def _(k=k, cols=cols):
                f = feats_s[0:1, (k - 9) * 128 : (k - 8) * 128]
                asel[:, cols] = jnp.broadcast_to(f, (TOK, 128)).astype(bf16)

    for i, low in enumerate((C, C + 768)):
        cols = slice(low, low + 768)
        wire_s[:, cols] = dot(turned[...], asel[:, low - C : low - C + 768]).astype(bf16)
        store = pltpu.make_async_copy(wire_s.at[:, cols], wire_ref.at[:, cols], sems.at[9 + i])
        store.start()
        stores.append(store)

    @pl.when(part < 3)
    def _():
        at = lax.broadcasted_iota(jnp.int32, (160, C), 1)
        cols = wire_columns(3 * OWN, C) + OWN * part
        for x, low in enumerate((0, 384, 896, 1280)):
            pick = jnp.where(at == cols + (480 * x - low), 1.0, 0.0).astype(bf16)
            turned[160 * x : 160 * (x + 1), :] = dot(pick, gall[:, low : low + C], NT).astype(bf16)
        wire_s[:, 0:C] = dot(turned[...], resid[...]).astype(bf16)

    @pl.when(part == 3)
    def _():
        for x in range(4):
            low = 3 * C + 128 * x
            pick = jnp.where(lane[:, 0:IMG] == own_cols + 32 * x, 1.0, 0.0).astype(bf16)
            turned[160 * x : 160 * (x + 1), :] = dot(pick, gall[:, low : low + IMG], NT).astype(
                bf16
            )
        wire_s[:, 0:C] = dot(turned[...], attended[...]).astype(bf16)

    store = pltpu.make_async_copy(wire_s.at[:, 0:C], wire_ref.at[:, 0:C], sems.at[11])
    store.start()
    for each in stores + [store]:
        each.wait()


def pair_call(part, steps, labels, errors, x, t, conv, bias, gain, qkvw, outw, timew):
    smem = pl.BlockSpec(memory_space=pltpu.SMEM)
    vmem = pl.BlockSpec(memory_space=pltpu.VMEM)
    hbm = pl.BlockSpec(memory_space=pl.ANY)
    return pl.pallas_call(
        pair_kernel,
        out_shape=(
            jax.ShapeDtypeStruct((C, WIDTH), bf16),
            jax.ShapeDtypeStruct((TOK, C), bf16),
            jax.ShapeDtypeStruct((BAND, C), f32),
            jax.ShapeDtypeStruct((8, C), f32),
            jax.ShapeDtypeStruct((8, 128), f32),
        ),
        in_specs=[smem] * 4 + [vmem, hbm, hbm, vmem, vmem, hbm, hbm, hbm, vmem],
        out_specs=[hbm] * 3 + [vmem] * 2,
        scratch_shapes=[
            pltpu.VMEM((TOK + 2 * BAND, 3 * C), bf16),
            pltpu.VMEM((TOK, C), f32),
            pltpu.VMEM((TOK, C), bf16),
            pltpu.VMEM((2, IMG, 3 * C), bf16),
            pltpu.VMEM((2 * HEAD_PAIRS, IMG, 2 * IMG), f32),
            pltpu.VMEM((TOK, C), bf16),
            pltpu.VMEM((TOK, C), f32),
            pltpu.VMEM((TOK, 4 * C), bf16),
            pltpu.VMEM((2, IMG, C), bf16),
            pltpu.VMEM((TOK, TAP_BLOCKS * 128), bf16),
            pltpu.VMEM((8, 384), f32),
            pltpu.VMEM((C, TOK), bf16),
            pltpu.VMEM((C, WIDTH), bf16),
            pltpu.VMEM((TOK, C), bf16),
            pltpu.VMEM((BAND, C), f32),
            pltpu.VMEM((TOK, C), bf16),
            pltpu.VMEM((3, 3 * C, C), bf16),
            pltpu.VMEM((C, 3 * C), bf16),
            pltpu.VMEM((C, C), bf16),
            pltpu.VMEM((TDIM, C), bf16),
            pltpu.SemaphoreType.DMA((12,)),
        ],
        compiler_params=pltpu.CompilerParams(vmem_limit_bytes=LIMIT * MIB),
        name="pair",
    )(
        part,
        steps,
        labels,
        errors,
        x,
        t,
        conv,
        bias,
        gain,
        qkvw,
        outw,
        timew,
        frequencies(),
    )


def input_kernel(
    part_ref, x_ref, cg_ref, own_ref, stat_ref, gain_ref, conv_ref, in_ref, gg_ref, gcat, acc
):
    part = part_ref[0]
    gcat[0:BAND, :] = jnp.zeros((BAND, 3 * C), bf16)
    gcat[pl.ds(BAND + TOK, BAND), :] = jnp.zeros((BAND, 3 * C), bf16)
    for r, m, at in blocks():
        g = cg_ref[pl.ds(at, COLS), :]
        here = pl.ds(BAND + at, COLS)
        gcat[here, 0:C] = shifted(g.astype(f32), -1).astype(bf16)
        gcat[here, C : 2 * C] = g
        gcat[here, 2 * C : 3 * C] = shifted(g.astype(f32), 1).astype(bf16)
    for i in range(3):
        for j in range(3):
            term = dot(
                gcat[pl.ds((2 - i) * BAND, TOK), j * C : (j + 1) * C],
                conv_ref[i, j * C : (j + 1) * C, :],
                NT,
            )
            if i == 0 and j == 0:
                acc[...] = term
            else:
                acc[...] += term
    gain = gain_ref[...].reshape(1, C)
    gain_sum = jnp.zeros((1, C), f32)
    ones = [jnp.zeros((1, C), f32) for _ in range(2)]
    twos = [jnp.zeros((1, C), f32) for _ in range(2)]
    for r, m, at in blocks():
        here = pl.ds(at, COLS)
        normed = (x_ref[here, :].astype(f32) - stat_ref[row(m), :]) * stat_ref[row(2 + m), :]
        a = normed * gain
        s = sigmoid(a)
        pre = acc[here, :] * (s * (1.0 + a * (1.0 - s)))
        gain_sum = gain_sum + jnp.sum(pre * normed, axis=0, keepdims=True)
        scaled = pre * gain
        acc[here, :] = scaled
        ones[m] = ones[m] + jnp.sum(scaled, axis=0, keepdims=True)
        twos[m] = twos[m] + jnp.sum(scaled * normed, axis=0, keepdims=True)
    bias_sum = jnp.sum(cg_ref[...].astype(f32), axis=0, keepdims=True)
    gg_ref[...] = jnp.concatenate([gain_sum, bias_sum], axis=0)
    means = group_sums(jnp.concatenate(ones + twos, axis=0)) / GROUP_COUNT
    for m in range(2):
        here = pl.ds(pl.multiple_of(part * BAND + m * COLS, COLS), COLS)
        inv = stat_ref[row(2 + m), :]
        normed = (x_ref[here, :].astype(f32) - stat_ref[row(m), :]) * inv
        inner = inv * (acc[here, :] - means[m : m + 1] - normed * means[2 + m : 3 + m])
        mine = slice(m * COLS, (m + 1) * COLS)
        in_ref[mine, :] = (own_ref[mine, :] + inner).astype(bf16)


def input_call(part, x, cg, own, stat, gain, conv):
    smem = pl.BlockSpec(memory_space=pltpu.SMEM)
    vmem = pl.BlockSpec(memory_space=pltpu.VMEM)
    return pl.pallas_call(
        input_kernel,
        out_shape=(
            jax.ShapeDtypeStruct((BAND, C), bf16),
            jax.ShapeDtypeStruct((2, C), f32),
        ),
        in_specs=[smem] + [vmem] * 6,
        out_specs=[vmem] * 2,
        scratch_shapes=[
            pltpu.VMEM((TOK + 2 * BAND, 3 * C), bf16),
            pltpu.VMEM((TOK, C), f32),
        ],
        compiler_params=pltpu.CompilerParams(vmem_limit_bytes=40 * MIB),
        cost_estimate=pl.CostEstimate(
            flops=2 * TOK * 9 * C * C, bytes_accessed=9 * C * C * 2, transcendentals=TOK * C
        ),
        name="input",
    )(part, x, cg, own, stat, gain, conv)


def half_kernel(a_ref, out_ref, acc, mid):
    total = a_ref[0].astype(f32)
    for i in range(1, 8):
        total = total + a_ref[i].astype(f32)
    acc[...] = total
    mid[:, OWN * BLOCKS :, :] = jnp.zeros((8, CHUNK - OWN * BLOCKS, 128), f32)
    for i in range(8):
        for k in range(BLOCKS):
            mid[i, OWN * k : OWN * (k + 1), :] = acc[
                OWN * i : OWN * (i + 1), 128 * k : 128 * (k + 1)
            ]
    out_ref[...] = mid[...].astype(bf16)


def half_call(a):
    vmem = pl.BlockSpec(memory_space=pltpu.VMEM)
    return pl.pallas_call(
        half_kernel,
        out_shape=jax.ShapeDtypeStruct((8, CHUNK, 128), bf16),
        in_specs=[vmem],
        out_specs=vmem,
        scratch_shapes=[
            pltpu.VMEM((80, WIDTH), f32),
            pltpu.VMEM((8, CHUNK, 128), f32),
        ],
        compiler_params=pltpu.CompilerParams(vmem_limit_bytes=32 * MIB),
        name="half",
    )(a)


def total_kernel(a_ref, out_ref):
    total = a_ref[0].astype(f32)
    for i in range(1, 8):
        total = total + a_ref[i].astype(f32)
    out_ref[...] = total


def total_call(a):
    vmem = pl.BlockSpec(memory_space=pltpu.VMEM)
    return pl.pallas_call(
        total_kernel,
        out_shape=jax.ShapeDtypeStruct((CHUNK, 128), f32),
        in_specs=[vmem],
        out_specs=vmem,
        compiler_params=pltpu.CompilerParams(vmem_limit_bytes=16 * MIB),
        name="total",
    )(a)


def unpack_kernel(all_ref, conv_ref, qkv_ref, out_ref, time_ref):
    for part in range(4):
        for k in range(5):
            rows = all_ref[part, OWN * k : OWN * (k + 1), :]
            cols = slice(128 * k, 128 * (k + 1))
            if part < 3:
                qkv_ref[OWN * part : OWN * (part + 1), cols] = rows
            else:
                out_ref[:, cols] = rows
        for k in range(TAP_BLOCKS):
            rows = all_ref[part, OWN * (5 + k) : OWN * (6 + k), :]
            place = part * TAP_BLOCKS + k
            tap, block = place // 5, place % 5
            if place < 45:
                conv_ref[tap // 3, :, tap % 3, 128 * block : 128 * (block + 1)] = rows
            else:
                wide = min(128, TDIM - 128 * (place - 45))
                low = 128 * (place - 45)
                time_ref[:, low : low + wide] = rows[:, 0:wide]


def unpack_call(whole):
    vmem = pl.BlockSpec(memory_space=pltpu.VMEM)
    return pl.pallas_call(
        unpack_kernel,
        out_shape=(
            jax.ShapeDtypeStruct((3, OWN, 3, C), f32),
            jax.ShapeDtypeStruct((3 * OWN, C), f32),
            jax.ShapeDtypeStruct((OWN, C), f32),
            jax.ShapeDtypeStruct((OWN, TDIM), f32),
        ),
        in_specs=[vmem],
        out_specs=[vmem] * 4,
        compiler_params=pltpu.CompilerParams(vmem_limit_bytes=16 * MIB),
        name="unpack",
    )(whole)


def on_device(
    section_input,
    target,
    conv_weight,
    conv_bias,
    norm_gain,
    qkv_weight,
    out_weight,
    time_weight,
    timesteps,
    labels,
    ref_error,
):
    part = lax.axis_index(SPACE_AXES).astype(jnp.int32).reshape(1)
    x = lax.all_gather(section_input.reshape(BAND, C), SPACE_AXES, axis=0, tiled=True)
    t = lax.all_gather(target.reshape(BAND, C), SPACE_AXES, axis=0, tiled=True)
    conv = conv_weight.reshape(3, 3 * C, C)
    wire, cg, own, stat, margin = pair_call(
        part,
        timesteps,
        labels,
        ref_error,
        x,
        t,
        conv,
        conv_bias,
        norm_gain,
        qkv_weight,
        out_weight,
        time_weight,
    )
    moved = lax.all_to_all(wire.reshape(8, 80, WIDTH), ("x", "y_hi"), 0, 0)
    input_grad, gains = input_call(part, x, cg, own, stat, norm_gain, conv)
    gains = lax.psum(gains, "z")
    moved, gains = lax.optimization_barrier((moved, gains))
    moved = lax.all_to_all(half_call(moved), "z", 0, 0)
    gains = lax.psum(gains, ("x", "y_hi"))
    gains = lax.dynamic_slice_in_dim(gains, lax.axis_index(PAIR_AXES) * OWN, OWN, 1)
    whole = lax.all_gather(total_call(moved), SPACE_AXES, axis=0, tiled=False)
    conv_out, qkv_out, out_out, time_out = unpack_call(whole)
    pair_loss = jax.nn.softplus(BETA * margin[0, 0:1])
    return (
        input_grad.reshape(section_input.shape),
        conv_out.transpose(0, 2, 3, 1),
        qkv_out.T,
        out_out.T,
        time_out.T,
        gains[0],
        gains[1],
        pair_loss,
    )


def solution(mesh):
    fine = Mesh(mesh.devices.reshape(MESH_SHAPE), MESH_AXES)
    pairs = P(PAIR_AXES)
    rows = P(PAIR_AXES, None, SPACE_AXES, None, None)
    return jax.shard_map(
        on_device,
        mesh=fine,
        in_specs=(rows, rows, P(), P(), P(), P(), P(), P(), pairs, pairs, pairs),
        out_specs=(
            rows,
            P(None, None, None, PAIR_AXES),
            P(None, PAIR_AXES),
            P(None, PAIR_AXES),
            P(None, PAIR_AXES),
            pairs,
            pairs,
            pairs,
        ),
        check_vma=False,
    )
```

```python
import math

import jax
import jax.numpy as jnp
import numpy as np
from jax import lax
from jax.experimental import pallas as pl
from jax.experimental.pallas import tpu as pltpu
from jax.sharding import Mesh
from jax.sharding import PartitionSpec as P

HEADS = 10
GROUPS = 32
TDIM = 320
C = 640
COLS = 64
ROWS = 4
TOK = 2 * ROWS * COLS
IMG = ROWS * COLS
BAND = 2 * COLS
HEAD_PAIRS = HEADS // 2
GROUP_COUNT = ROWS * COLS * (C // GROUPS)
SCALE = 1.0 / math.sqrt(C // HEADS)
EPS = 1e-05
BETA = 2.0

PAIR_AXES = ("x", "z", "y_hi")
SPACE_AXES = ("y_lo", "core")
MESH_AXES = ("x", "z", "y_hi", "y_lo", "core")
MESH_SHAPE = (4, 8, 2, 2, 2)
OWN = C // 64
TAP_BLOCKS = 12
BLOCKS = 5 + TAP_BLOCKS
WIDTH = BLOCKS * 128
CHUNK = 176
MIB = 1024 * 1024
LIMIT = 56

f32 = jnp.float32
bf16 = jnp.bfloat16

NN = (((1,), (0,)), ((), ()))
NT = (((1,), (1,)), ((), ()))
TN = (((0,), (0,)), ((), ()))


def dot(a, b, dims=NN):
    return lax.dot_general(a, b, dims, preferred_element_type=f32)


def frequencies():
    half = TDIM // 2
    return np.exp(-math.log(10000.0) * (np.arange(TDIM) % half) / half).astype(np.float32)[None]


def wire_columns(step, width):
    n = lax.broadcasted_iota(jnp.int32, (160, width), 0)
    y = jnp.where(n >= 80, 1, 0)
    rest = n - 80 * y
    z = (rest * 6554) >> 16
    return 2 * step * z + step * y + rest - OWN * z


def row(i):
    return pl.ds(i, 1)


def group_sums(rows):
    a = lax.broadcasted_iota(jnp.int32, (C, C), 0)
    b = lax.broadcasted_iota(jnp.int32, (C, C), 1)
    same = ((a * 3277) >> 16) == ((b * 3277) >> 16)
    ones = jnp.where(same, 1.0, 0.0).astype(bf16)
    high = rows.astype(bf16).astype(f32)
    rest = rows - high
    middle = rest.astype(bf16).astype(f32)
    low = rest - middle
    stack = jnp.concatenate([high, middle, low, jnp.zeros_like(rows)], axis=0).astype(bf16)
    sums = dot(stack, ones)
    return sums[0:4] + sums[4:8] + sums[8:12]


def sigmoid(v):
    return 1.0 / (1.0 + jnp.exp(-v))


def blocks():
    return [(r, m, (2 * r + m) * COLS) for r in range(ROWS) for m in range(2)]


def shifted(v, step):
    at = lax.broadcasted_iota(jnp.int32, (COLS, C), 0)
    if step == 1:
        return jnp.where(at == 0, 0.0, pltpu.roll(v, 1, 0))
    return jnp.where(at == COLS - 1, 0.0, pltpu.roll(v, COLS - 1, 0))


def head_halves(v):
    lane = lax.broadcasted_iota(jnp.int32, (1, 128), 1)
    first = jnp.where(lane < 64, 1.0, 0.0).astype(bf16)
    second = jnp.where(lane < 64, 0.0, 1.0).astype(bf16)
    return jnp.concatenate([v * first, v * second], axis=0)


def head_join(v):
    lane = lax.broadcasted_iota(jnp.int32, (IMG, 128), 1)
    return jnp.where(lane < 64, v[:IMG], v[IMG:])


def pair_kernel(
    part_ref,
    step_ref,
    label_ref,
    error_ref,
    own_xt_ref,
    y_xt_ref,
    core_xt_ref,
    far_xt_ref,
    conv_ref,
    bias_ref,
    gain_ref,
    qkvw_ref,
    outw_ref,
    timew_ref,
    freq_ref,
    wire_ref,
    x_ref,
    cg_ref,
    own_ref,
    stat_ref,
    margin_ref,
    acat,
    acc,
    resid,
    qkv,
    probs,
    attended,
    dev,
    gall,
    dattn,
    asel,
    feats_s,
    turned,
    wire_s,
    cg_s,
    own_s,
    x_s,
    t_s,
    conv_s,
    qkvw_s,
    outw_s,
    timew_s,
    sems,
):
    part = part_ref[0]
    taps = [pltpu.make_async_copy(conv_ref.at[i], conv_s.at[i], sems.at[i]) for i in range(3)]
    load_time = pltpu.make_async_copy(timew_ref, timew_s, sems.at[3])
    load_qkv = pltpu.make_async_copy(qkvw_ref, qkvw_s, sems.at[4])
    load_out = pltpu.make_async_copy(outw_ref, outw_s, sems.at[5])
    load_x, load_t = [], []
    for i, (ref, way) in enumerate(
        ((own_xt_ref, 0), (core_xt_ref, 1), (y_xt_ref, 2), (far_xt_ref, 3))
    ):
        rows = pl.ds(pl.multiple_of((part ^ way) * BAND, BAND), BAND)
        load_x.append(
            pltpu.make_async_copy(ref.at[pl.ds(0, BAND)], x_s.at[rows], sems.at[12 + i])
        )
        load_t.append(
            pltpu.make_async_copy(ref.at[pl.ds(BAND, BAND)], t_s.at[rows], sems.at[16 + i])
        )
    for load in load_x:
        load.start()
    taps[0].start()
    load_time.start()
    taps[1].start()
    for load in load_x:
        load.wait()
    stores = [pltpu.make_async_copy(x_s, x_ref, sems.at[6])]
    sums, squares = [], []
    for m in range(2):
        total = jnp.zeros((1, C), f32)
        square = jnp.zeros((1, C), f32)
        for r in range(ROWS):
            v = x_s[pl.ds((2 * r + m) * COLS, COLS), :].astype(f32)
            total = total + jnp.sum(v, axis=0, keepdims=True)
            square = square + jnp.sum(v * v, axis=0, keepdims=True)
        sums.append(total)
        squares.append(square)
    moments = group_sums(jnp.concatenate(sums + squares, axis=0)) / GROUP_COUNT
    mean = moments[0:2]
    inv = lax.rsqrt(moments[2:4] - mean * mean + EPS)
    stat_ref[...] = jnp.concatenate([mean, inv, jnp.zeros((4, C), f32)], axis=0)
    gain = gain_ref[...].reshape(1, C)
    acat[0:BAND, :] = jnp.zeros((BAND, 3 * C), bf16)
    acat[pl.ds(BAND + TOK, BAND), :] = jnp.zeros((BAND, 3 * C), bf16)
    for r, m, at in blocks():
        v = x_s[pl.ds(at, COLS), :].astype(f32)
        a = (v - mean[m : m + 1]) * inv[m : m + 1] * gain
        act = a * sigmoid(a)
        here = pl.ds(BAND + at, COLS)
        acat[here, 0:C] = shifted(act, 1).astype(bf16)
        acat[here, C : 2 * C] = act.astype(bf16)
        acat[here, 2 * C : 3 * C] = shifted(act, -1).astype(bf16)
    angle = step_ref[0].astype(f32) * freq_ref[...]
    lane = lax.broadcasted_iota(jnp.int32, (1, TDIM), 1)
    feats = jnp.where(lane < TDIM // 2, jnp.cos(angle), jnp.sin(angle))
    feats_s[...] = jnp.zeros((8, 384), f32)
    feats_s[0:1, 0:TDIM] = feats
    load_time.wait()
    shift = dot(jnp.broadcast_to(feats, (16, TDIM)).astype(bf16), timew_s[...])[0:1]
    offset = shift + bias_ref[...].reshape(1, C)
    taps[0].wait()
    taps[2].start()
    load_qkv.start()
    stores[0].start()
    acc[...] = dot(acat[0:TOK, :], conv_s[0])
    taps[1].wait()
    acc[...] += dot(acat[pl.ds(BAND, TOK), :], conv_s[1])
    taps[2].wait()
    acc[...] += dot(acat[pl.ds(2 * BAND, TOK), :], conv_s[2])
    resid[...] = (x_s[...].astype(f32) + acc[...] + offset).astype(bf16)
    load_qkv.wait()
    load_out.start()
    for load in load_t:
        load.start()
    for third in range(3):
        cols = pl.ds(third * C, C)
        proj = dot(resid[...], qkvw_s[:, cols]).astype(bf16)
        for r, m, at in blocks():
            qkv[m, pl.ds(r * COLS, COLS), cols] = proj[at : at + COLS]
    for m in range(2):
        for h in range(HEAD_PAIRS):
            q2 = head_halves(qkv[m, :, pl.ds(h * 128, 128)])
            k = qkv[m, :, pl.ds(C + h * 128, 128)]
            v = qkv[m, :, pl.ds(2 * C + h * 128, 128)]
            scores = dot(k, q2, NT) * SCALE
            exps = jnp.exp(scores - jnp.max(scores, axis=0, keepdims=True))
            p = exps * (1.0 / jnp.sum(exps, axis=0, keepdims=True))
            probs[m * HEAD_PAIRS + h] = p
            joined = head_join(dot(p.astype(bf16), v, TN)).astype(bf16)
            for r in range(ROWS):
                attended[pl.ds((2 * r + m) * COLS, COLS), pl.ds(h * 128, 128)] = joined[
                    r * COLS : (r + 1) * COLS
                ]
    load_out.wait()
    for load in load_t:
        load.wait()
    dev[...] = (
        resid[...].astype(f32) + dot(attended[...], outw_s[...]) - t_s[...].astype(f32)
    )
    margin = jnp.zeros((1, 1), f32)
    signs = []
    for m in range(2):
        total = jnp.zeros((1, C), f32)
        for r in range(ROWS):
            d = dev[pl.ds((2 * r + m) * COLS, COLS), :]
            total = total + jnp.sum(d * d, axis=0, keepdims=True)
        error = jnp.sum(total, axis=1, keepdims=True) / (IMG * C)
        sign = jnp.where(label_ref[0] == m, 1.0, -1.0)
        signs.append(sign)
        margin = margin + sign * (error - error_ref[0, m])
    margin_ref[...] = jnp.broadcast_to(margin, (8, 128))
    slope = BETA * sigmoid(BETA * margin)
    for r, m, at in blocks():
        here = pl.ds(at, COLS)
        gall[here, 3 * C : 4 * C] = (signs[m] * slope * dev[here, :]).astype(bf16)
    out_grad = gall[:, 3 * C : 4 * C]
    da = dot(out_grad, outw_s[...], NT).astype(bf16)
    for r, m, at in blocks():
        dattn[m, pl.ds(r * COLS, COLS), :] = da[at : at + COLS]
    for m in range(2):
        for h in range(HEAD_PAIRS):
            q2 = head_halves(qkv[m, :, pl.ds(h * 128, 128)])
            k = qkv[m, :, pl.ds(C + h * 128, 128)]
            v = qkv[m, :, pl.ds(2 * C + h * 128, 128)]
            da2 = head_halves(dattn[m, :, pl.ds(h * 128, 128)])
            p = probs[m * HEAD_PAIRS + h]
            dp = dot(v, da2, NT)
            dots = jnp.sum(p * dp, axis=0, keepdims=True)
            ds = (p * (dp - dots) * SCALE).astype(bf16)
            dq = head_join(dot(ds, k, TN)).astype(bf16)
            dk = dot(ds, q2).astype(bf16)
            dv = dot(p.astype(bf16), da2).astype(bf16)
            for r in range(ROWS):
                here = pl.ds((2 * r + m) * COLS, COLS)
                rows = slice(r * COLS, (r + 1) * COLS)
                gall[here, pl.ds(h * 128, 128)] = dq[rows]
                gall[here, pl.ds(C + h * 128, 128)] = dk[rows]
                gall[here, pl.ds(2 * C + h * 128, 128)] = dv[rows]
    acc[...] = out_grad.astype(f32) + dot(gall[:, 0 : 3 * C], qkvw_s[...], NT)
    cg_s[...] = acc[...].astype(bf16)
    own_s[...] = acc[pl.ds(pl.multiple_of(part * BAND, BAND), BAND), :]
    stores.append(pltpu.make_async_copy(cg_s, cg_ref, sems.at[7]))
    stores.append(pltpu.make_async_copy(own_s, own_ref, sems.at[8]))
    for store in stores[1:]:
        store.start()
    lane = lax.broadcasted_iota(jnp.int32, (160, 2 * IMG), 1)
    own_cols = wire_columns(OWN, 2 * IMG)[:, 0:IMG]
    for x in range(4):
        low = 128 * x
        pick = jnp.where(lane[:, 0:IMG] == own_cols + 32 * x, 1.0, 0.0).astype(bf16)
        turned[160 * x : 160 * (x + 1), :] = dot(pick, cg_s[:, low : low + IMG], NT).astype(bf16)
    for k in range(TAP_BLOCKS):
        place = part * TAP_BLOCKS + k
        cols = slice(k * 128, (k + 1) * 128)

        def tap(place=place, cols=cols):
            up = place // 15
            lane = pl.multiple_of((place - 15 * up) * 128, 128)
            asel[:, cols] = acat[pl.ds(pl.multiple_of(up * BAND, BAND), TOK), pl.ds(lane, 128)]

        if k < 9:
            tap()
        else:
            pl.when(part < 3)(tap)

            @pl.when(part == 3)
            def _(k=k, cols=cols):
                f = feats_s[0:1, (k - 9) * 128 : (k - 8) * 128]
                asel[:, cols] = jnp.broadcast_to(f, (TOK, 128)).astype(bf16)

    for i, low in enumerate((C, C + 768)):
        cols = slice(low, low + 768)
        wire_s[:, cols] = dot(turned[...], asel[:, low - C : low - C + 768]).astype(bf16)
        store = pltpu.make_async_copy(wire_s.at[:, cols], wire_ref.at[:, cols], sems.at[9 + i])
        store.start()
        stores.append(store)

    @pl.when(part < 3)
    def _():
        at = lax.broadcasted_iota(jnp.int32, (160, C), 1)
        cols = wire_columns(3 * OWN, C) + OWN * part
        for x, low in enumerate((0, 384, 896, 1280)):
            pick = jnp.where(at == cols + (480 * x - low), 1.0, 0.0).astype(bf16)
            turned[160 * x : 160 * (x + 1), :] = dot(pick, gall[:, low : low + C], NT).astype(bf16)
        wire_s[:, 0:C] = dot(turned[...], resid[...]).astype(bf16)

    @pl.when(part == 3)
    def _():
        for x in range(4):
            low = 3 * C + 128 * x
            pick = jnp.where(lane[:, 0:IMG] == own_cols + 32 * x, 1.0, 0.0).astype(bf16)
            turned[160 * x : 160 * (x + 1), :] = dot(pick, gall[:, low : low + IMG], NT).astype(
                bf16
            )
        wire_s[:, 0:C] = dot(turned[...], attended[...]).astype(bf16)

    store = pltpu.make_async_copy(wire_s.at[:, 0:C], wire_ref.at[:, 0:C], sems.at[11])
    store.start()
    for each in stores + [store]:
        each.wait()


def pair_call(part, steps, labels, errors, own, near, core, far, conv, bias, gain, qkvw, outw, timew):
    smem = pl.BlockSpec(memory_space=pltpu.SMEM)
    vmem = pl.BlockSpec(memory_space=pltpu.VMEM)
    hbm = pl.BlockSpec(memory_space=pl.ANY)
    return pl.pallas_call(
        pair_kernel,
        out_shape=(
            jax.ShapeDtypeStruct((C, WIDTH), bf16),
            jax.ShapeDtypeStruct((TOK, C), bf16),
            jax.ShapeDtypeStruct((TOK, C), bf16),
            jax.ShapeDtypeStruct((BAND, C), f32),
            jax.ShapeDtypeStruct((8, C), f32),
            jax.ShapeDtypeStruct((8, 128), f32),
        ),
        in_specs=[smem] * 4 + [vmem] * 4 + [hbm] + [vmem] * 2 + [hbm] * 3 + [vmem],
        out_specs=[hbm] * 4 + [vmem] * 2,
        scratch_shapes=[
            pltpu.VMEM((TOK + 2 * BAND, 3 * C), bf16),
            pltpu.VMEM((TOK, C), f32),
            pltpu.VMEM((TOK, C), bf16),
            pltpu.VMEM((2, IMG, 3 * C), bf16),
            pltpu.VMEM((2 * HEAD_PAIRS, IMG, 2 * IMG), f32),
            pltpu.VMEM((TOK, C), bf16),
            pltpu.VMEM((TOK, C), f32),
            pltpu.VMEM((TOK, 4 * C), bf16),
            pltpu.VMEM((2, IMG, C), bf16),
            pltpu.VMEM((TOK, TAP_BLOCKS * 128), bf16),
            pltpu.VMEM((8, 384), f32),
            pltpu.VMEM((C, TOK), bf16),
            pltpu.VMEM((C, WIDTH), bf16),
            pltpu.VMEM((TOK, C), bf16),
            pltpu.VMEM((BAND, C), f32),
            pltpu.VMEM((TOK, C), bf16),
            pltpu.VMEM((TOK, C), bf16),
            pltpu.VMEM((3, 3 * C, C), bf16),
            pltpu.VMEM((C, 3 * C), bf16),
            pltpu.VMEM((C, C), bf16),
            pltpu.VMEM((TDIM, C), bf16),
            pltpu.SemaphoreType.DMA((20,)),
        ],
        compiler_params=pltpu.CompilerParams(vmem_limit_bytes=LIMIT * MIB),
        name="pair",
    )(
        part,
        steps,
        labels,
        errors,
        own,
        near,
        core,
        far,
        conv,
        bias,
        gain,
        qkvw,
        outw,
        timew,
        frequencies(),
    )


def input_kernel(
    part_ref, x_ref, cg_ref, own_ref, stat_ref, gain_ref, conv_ref, in_ref, gg_ref, gcat, acc
):
    part = part_ref[0]
    gcat[0:BAND, :] = jnp.zeros((BAND, 3 * C), bf16)
    gcat[pl.ds(BAND + TOK, BAND), :] = jnp.zeros((BAND, 3 * C), bf16)
    for r, m, at in blocks():
        g = cg_ref[pl.ds(at, COLS), :]
        here = pl.ds(BAND + at, COLS)
        gcat[here, 0:C] = shifted(g.astype(f32), -1).astype(bf16)
        gcat[here, C : 2 * C] = g
        gcat[here, 2 * C : 3 * C] = shifted(g.astype(f32), 1).astype(bf16)
    for i in range(3):
        for j in range(3):
            term = dot(
                gcat[pl.ds((2 - i) * BAND, TOK), j * C : (j + 1) * C],
                conv_ref[i, j * C : (j + 1) * C, :],
                NT,
            )
            if i == 0 and j == 0:
                acc[...] = term
            else:
                acc[...] += term
    gain = gain_ref[...].reshape(1, C)
    gain_sum = jnp.zeros((1, C), f32)
    ones = [jnp.zeros((1, C), f32) for _ in range(2)]
    twos = [jnp.zeros((1, C), f32) for _ in range(2)]
    for r, m, at in blocks():
        here = pl.ds(at, COLS)
        normed = (x_ref[here, :].astype(f32) - stat_ref[row(m), :]) * stat_ref[row(2 + m), :]
        a = normed * gain
        s = sigmoid(a)
        pre = acc[here, :] * (s * (1.0 + a * (1.0 - s)))
        gain_sum = gain_sum + jnp.sum(pre * normed, axis=0, keepdims=True)
        scaled = pre * gain
        acc[here, :] = scaled
        ones[m] = ones[m] + jnp.sum(scaled, axis=0, keepdims=True)
        twos[m] = twos[m] + jnp.sum(scaled * normed, axis=0, keepdims=True)
    bias_sum = jnp.sum(cg_ref[...].astype(f32), axis=0, keepdims=True)
    gg_ref[...] = jnp.concatenate([gain_sum, bias_sum], axis=0)
    means = group_sums(jnp.concatenate(ones + twos, axis=0)) / GROUP_COUNT
    for m in range(2):
        here = pl.ds(pl.multiple_of(part * BAND + m * COLS, COLS), COLS)
        inv = stat_ref[row(2 + m), :]
        normed = (x_ref[here, :].astype(f32) - stat_ref[row(m), :]) * inv
        inner = inv * (acc[here, :] - means[m : m + 1] - normed * means[2 + m : 3 + m])
        mine = slice(m * COLS, (m + 1) * COLS)
        in_ref[mine, :] = (own_ref[mine, :] + inner).astype(bf16)


def input_call(part, x, cg, own, stat, gain, conv):
    smem = pl.BlockSpec(memory_space=pltpu.SMEM)
    vmem = pl.BlockSpec(memory_space=pltpu.VMEM)
    return pl.pallas_call(
        input_kernel,
        out_shape=(
            jax.ShapeDtypeStruct((BAND, C), bf16),
            jax.ShapeDtypeStruct((2, C), f32),
        ),
        in_specs=[smem] + [vmem] * 6,
        out_specs=[vmem] * 2,
        scratch_shapes=[
            pltpu.VMEM((TOK + 2 * BAND, 3 * C), bf16),
            pltpu.VMEM((TOK, C), f32),
        ],
        compiler_params=pltpu.CompilerParams(vmem_limit_bytes=40 * MIB),
        cost_estimate=pl.CostEstimate(
            flops=2 * TOK * 9 * C * C, bytes_accessed=9 * C * C * 2, transcendentals=TOK * C
        ),
        name="input",
    )(part, x, cg, own, stat, gain, conv)


def half_kernel(a_ref, out_ref, acc, mid):
    total = a_ref[0].astype(f32)
    for i in range(1, 8):
        total = total + a_ref[i].astype(f32)
    acc[...] = total
    mid[:, OWN * BLOCKS :, :] = jnp.zeros((8, CHUNK - OWN * BLOCKS, 128), f32)
    for i in range(8):
        for k in range(BLOCKS):
            mid[i, OWN * k : OWN * (k + 1), :] = acc[
                OWN * i : OWN * (i + 1), 128 * k : 128 * (k + 1)
            ]
    out_ref[...] = mid[...].astype(bf16)


def half_call(a):
    vmem = pl.BlockSpec(memory_space=pltpu.VMEM)
    return pl.pallas_call(
        half_kernel,
        out_shape=jax.ShapeDtypeStruct((8, CHUNK, 128), bf16),
        in_specs=[vmem],
        out_specs=vmem,
        scratch_shapes=[
            pltpu.VMEM((80, WIDTH), f32),
            pltpu.VMEM((8, CHUNK, 128), f32),
        ],
        compiler_params=pltpu.CompilerParams(vmem_limit_bytes=32 * MIB),
        name="half",
    )(a)


def total_kernel(a_ref, out_ref):
    total = a_ref[0].astype(f32)
    for i in range(1, 8):
        total = total + a_ref[i].astype(f32)
    out_ref[...] = total


def total_call(a):
    vmem = pl.BlockSpec(memory_space=pltpu.VMEM)
    return pl.pallas_call(
        total_kernel,
        out_shape=jax.ShapeDtypeStruct((CHUNK, 128), f32),
        in_specs=[vmem],
        out_specs=vmem,
        compiler_params=pltpu.CompilerParams(vmem_limit_bytes=16 * MIB),
        name="total",
    )(a)


def unpack_kernel(all_ref, conv_ref, qkv_ref, out_ref, time_ref):
    for part in range(4):
        for k in range(5):
            rows = all_ref[part, OWN * k : OWN * (k + 1), :]
            cols = slice(128 * k, 128 * (k + 1))
            if part < 3:
                qkv_ref[OWN * part : OWN * (part + 1), cols] = rows
            else:
                out_ref[:, cols] = rows
        for k in range(TAP_BLOCKS):
            rows = all_ref[part, OWN * (5 + k) : OWN * (6 + k), :]
            place = part * TAP_BLOCKS + k
            tap, block = place // 5, place % 5
            if place < 45:
                conv_ref[tap // 3, :, tap % 3, 128 * block : 128 * (block + 1)] = rows
            else:
                wide = min(128, TDIM - 128 * (place - 45))
                low = 128 * (place - 45)
                time_ref[:, low : low + wide] = rows[:, 0:wide]


def unpack_call(whole):
    vmem = pl.BlockSpec(memory_space=pltpu.VMEM)
    return pl.pallas_call(
        unpack_kernel,
        out_shape=(
            jax.ShapeDtypeStruct((3, OWN, 3, C), f32),
            jax.ShapeDtypeStruct((3 * OWN, C), f32),
            jax.ShapeDtypeStruct((OWN, C), f32),
            jax.ShapeDtypeStruct((OWN, TDIM), f32),
        ),
        in_specs=[vmem],
        out_specs=[vmem] * 4,
        compiler_params=pltpu.CompilerParams(vmem_limit_bytes=16 * MIB),
        name="unpack",
    )(whole)


def on_device(
    section_input,
    target,
    conv_weight,
    conv_bias,
    norm_gain,
    qkv_weight,
    out_weight,
    time_weight,
    timesteps,
    labels,
    ref_error,
):
    part = lax.axis_index(SPACE_AXES).astype(jnp.int32).reshape(1)
    swap = [(0, 1), (1, 0)]
    own_xt = jnp.concatenate([section_input.reshape(BAND, C), target.reshape(BAND, C)], axis=0)
    near = lax.ppermute(own_xt, "y_lo", swap)
    core = lax.ppermute(own_xt, "core", swap)
    far = lax.ppermute(near, "core", swap)
    conv = conv_weight.reshape(3, 3 * C, C)
    wire, x, cg, own, stat, margin = pair_call(
        part,
        timesteps,
        labels,
        ref_error,
        own_xt,
        near,
        core,
        far,
        conv,
        conv_bias,
        norm_gain,
        qkv_weight,
        out_weight,
        time_weight,
    )
    moved = lax.all_to_all(wire.reshape(8, 80, WIDTH), ("x", "y_hi"), 0, 0)
    input_grad, gains = input_call(part, x, cg, own, stat, norm_gain, conv)
    gains = lax.psum(gains, "z")
    moved, gains = lax.optimization_barrier((moved, gains))
    half, gains = lax.optimization_barrier((half_call(moved), gains))
    moved = lax.all_to_all(half, "z", 0, 0)
    gains = gains + lax.ppermute(gains, "y_hi", swap)
    gains = gains + lax.ppermute(gains, "x", [(0, 1), (1, 0), (2, 3), (3, 2)])
    gains = gains + lax.ppermute(gains, "x", [(0, 3), (3, 0), (1, 2), (2, 1)])
    gains = lax.dynamic_slice_in_dim(gains, lax.axis_index(PAIR_AXES) * OWN, OWN, 1)
    whole = lax.all_gather(total_call(moved), SPACE_AXES, axis=0, tiled=False)
    conv_out, qkv_out, out_out, time_out = unpack_call(whole)
    pair_loss = jax.nn.softplus(BETA * margin[0, 0:1])
    return (
        input_grad.reshape(section_input.shape),
        conv_out.transpose(0, 2, 3, 1),
        qkv_out.T,
        out_out.T,
        time_out.T,
        gains[0],
        gains[1],
        pair_loss,
    )


def solution(mesh):
    fine = Mesh(mesh.devices.reshape(MESH_SHAPE), MESH_AXES)
    pairs = P(PAIR_AXES)
    rows = P(PAIR_AXES, None, SPACE_AXES, None, None)
    return jax.shard_map(
        on_device,
        mesh=fine,
        in_specs=(rows, rows, P(), P(), P(), P(), P(), P(), pairs, pairs, pairs),
        out_specs=(
            rows,
            P(None, None, None, PAIR_AXES),
            P(None, PAIR_AXES),
            P(None, PAIR_AXES),
            P(None, PAIR_AXES),
            pairs,
            pairs,
            pairs,
        ),
        check_vma=False,
    )
```

```python
import math

import jax
import jax.numpy as jnp
import numpy as np
from jax import lax
from jax.experimental import pallas as pl
from jax.experimental.pallas import tpu as pltpu
from jax.sharding import Mesh
from jax.sharding import PartitionSpec as P

HEADS = 10
GROUPS = 32
TDIM = 320
C = 640
COLS = 64
ROWS = 4
TOK = 2 * ROWS * COLS
IMG = ROWS * COLS
BAND = 2 * COLS
HEAD_PAIRS = HEADS // 2
GROUP_COUNT = ROWS * COLS * (C // GROUPS)
SCALE = 1.0 / math.sqrt(C // HEADS)
EPS = 1e-05
BETA = 2.0

PAIR_AXES = ("x", "z", "y_hi")
SPACE_AXES = ("y_lo", "core")
MESH_AXES = ("x", "z", "y_hi", "y_lo", "core")
MESH_SHAPE = (4, 8, 2, 2, 2)
OWN = C // 64
TAP_BLOCKS = 12
WIDTH = TAP_BLOCKS * 128
TAP_ROWS = OWN * TAP_BLOCKS
CHUNK = 176
SIDE = C + 128
MIB = 1024 * 1024
LIMIT = 56

f32 = jnp.float32
bf16 = jnp.bfloat16

NN = (((1,), (0,)), ((), ()))
NT = (((1,), (1,)), ((), ()))
TN = (((0,), (0,)), ((), ()))


def dot(a, b, dims=NN):
    return lax.dot_general(a, b, dims, preferred_element_type=f32)


def frequencies():
    half = TDIM // 2
    return np.exp(-math.log(10000.0) * (np.arange(TDIM) % half) / half).astype(np.float32)[None]


def wire_columns(step, width):
    n = lax.broadcasted_iota(jnp.int32, (160, width), 0)
    y = jnp.where(n >= 80, 1, 0)
    rest = n - 80 * y
    z = (rest * 6554) >> 16
    return 2 * step * z + step * y + rest - OWN * z


def row(i):
    return pl.ds(i, 1)


def group_sums(rows):
    a = lax.broadcasted_iota(jnp.int32, (C, C), 0)
    b = lax.broadcasted_iota(jnp.int32, (C, C), 1)
    same = ((a * 3277) >> 16) == ((b * 3277) >> 16)
    ones = jnp.where(same, 1.0, 0.0).astype(bf16)
    high = rows.astype(bf16).astype(f32)
    rest = rows - high
    middle = rest.astype(bf16).astype(f32)
    low = rest - middle
    stack = jnp.concatenate([high, middle, low, jnp.zeros_like(rows)], axis=0).astype(bf16)
    sums = dot(stack, ones)
    return sums[0:4] + sums[4:8] + sums[8:12]


def sigmoid(v):
    return 1.0 / (1.0 + jnp.exp(-v))


def blocks():
    return [(r, m, (2 * r + m) * COLS) for r in range(ROWS) for m in range(2)]


def shifted(v, step):
    at = lax.broadcasted_iota(jnp.int32, (COLS, C), 0)
    if step == 1:
        return jnp.where(at == 0, 0.0, pltpu.roll(v, 1, 0))
    return jnp.where(at == COLS - 1, 0.0, pltpu.roll(v, COLS - 1, 0))


def head_halves(v):
    lane = lax.broadcasted_iota(jnp.int32, (1, 128), 1)
    first = jnp.where(lane < 64, 1.0, 0.0).astype(bf16)
    second = jnp.where(lane < 64, 0.0, 1.0).astype(bf16)
    return jnp.concatenate([v * first, v * second], axis=0)


def head_join(v):
    lane = lax.broadcasted_iota(jnp.int32, (IMG, 128), 1)
    return jnp.where(lane < 64, v[:IMG], v[IMG:])


def pair_kernel(
    part_ref,
    step_ref,
    label_ref,
    error_ref,
    own_xt_ref,
    y_xt_ref,
    core_xt_ref,
    far_xt_ref,
    conv_ref,
    bias_ref,
    gain_ref,
    qkvw_ref,
    outw_ref,
    timew_ref,
    freq_ref,
    wire_ref,
    x_ref,
    gall_ref,
    side_ref,
    cg_ref,
    own_ref,
    stat_ref,
    margin_ref,
    acat,
    acc,
    resid,
    qkv,
    probs,
    attended,
    dev,
    gall,
    dattn,
    asel,
    feats_s,
    turned,
    wire_s,
    cg_s,
    own_s,
    x_s,
    t_s,
    side_s,
    conv_s,
    qkvw_s,
    outw_s,
    timew_s,
    sems,
):
    part = part_ref[0]
    taps = [pltpu.make_async_copy(conv_ref.at[i], conv_s.at[i], sems.at[i]) for i in range(3)]
    load_time = pltpu.make_async_copy(timew_ref, timew_s, sems.at[3])
    load_qkv = pltpu.make_async_copy(qkvw_ref, qkvw_s, sems.at[4])
    load_out = pltpu.make_async_copy(outw_ref, outw_s, sems.at[5])
    taps[0].start()
    load_time.start()
    taps[1].start()
    for ref, way in ((own_xt_ref, 0), (core_xt_ref, 1), (y_xt_ref, 2), (far_xt_ref, 3)):
        rows = pl.ds(pl.multiple_of((part ^ way) * BAND, BAND), BAND)
        x_s[rows, :] = ref[0:BAND, :]
        t_s[rows, :] = ref[BAND : 2 * BAND, :]
    stores = [pltpu.make_async_copy(x_s, x_ref, sems.at[6])]
    sums, squares = [], []
    for m in range(2):
        total = jnp.zeros((1, C), f32)
        square = jnp.zeros((1, C), f32)
        for r in range(ROWS):
            v = x_s[pl.ds((2 * r + m) * COLS, COLS), :].astype(f32)
            total = total + jnp.sum(v, axis=0, keepdims=True)
            square = square + jnp.sum(v * v, axis=0, keepdims=True)
        sums.append(total)
        squares.append(square)
    moments = group_sums(jnp.concatenate(sums + squares, axis=0)) / GROUP_COUNT
    mean = moments[0:2]
    inv = lax.rsqrt(moments[2:4] - mean * mean + EPS)
    stat_ref[...] = jnp.concatenate([mean, inv, jnp.zeros((4, C), f32)], axis=0)
    gain = gain_ref[...].reshape(1, C)
    acat[0:BAND, :] = jnp.zeros((BAND, 3 * C), bf16)
    acat[pl.ds(BAND + TOK, BAND), :] = jnp.zeros((BAND, 3 * C), bf16)
    for r, m, at in blocks():
        v = x_s[pl.ds(at, COLS), :].astype(f32)
        a = (v - mean[m : m + 1]) * inv[m : m + 1] * gain
        act = a * sigmoid(a)
        here = pl.ds(BAND + at, COLS)
        acat[here, 0:C] = shifted(act, 1).astype(bf16)
        acat[here, C : 2 * C] = act.astype(bf16)
        acat[here, 2 * C : 3 * C] = shifted(act, -1).astype(bf16)
    angle = step_ref[0].astype(f32) * freq_ref[...]
    lane = lax.broadcasted_iota(jnp.int32, (1, TDIM), 1)
    feats = jnp.where(lane < TDIM // 2, jnp.cos(angle), jnp.sin(angle))
    feats_s[...] = jnp.zeros((8, 384), f32)
    feats_s[0:1, 0:TDIM] = feats
    load_time.wait()
    shift = dot(jnp.broadcast_to(feats, (16, TDIM)).astype(bf16), timew_s[...])[0:1]
    offset = shift + bias_ref[...].reshape(1, C)
    taps[0].wait()
    taps[2].start()
    load_qkv.start()
    stores[0].start()
    acc[...] = dot(acat[0:TOK, :], conv_s[0])
    taps[1].wait()
    acc[...] += dot(acat[pl.ds(BAND, TOK), :], conv_s[1])
    taps[2].wait()
    acc[...] += dot(acat[pl.ds(2 * BAND, TOK), :], conv_s[2])
    resid[...] = (x_s[...].astype(f32) + acc[...] + offset).astype(bf16)
    load_qkv.wait()
    load_out.start()
    for third in range(3):
        cols = pl.ds(third * C, C)
        proj = dot(resid[...], qkvw_s[:, cols]).astype(bf16)
        for r, m, at in blocks():
            qkv[m, pl.ds(r * COLS, COLS), cols] = proj[at : at + COLS]
    for m in range(2):
        for h in range(HEAD_PAIRS):
            q2 = head_halves(qkv[m, :, pl.ds(h * 128, 128)])
            k = qkv[m, :, pl.ds(C + h * 128, 128)]
            v = qkv[m, :, pl.ds(2 * C + h * 128, 128)]
            scores = dot(k, q2, NT) * SCALE
            exps = jnp.exp(scores - jnp.max(scores, axis=0, keepdims=True))
            p = exps * (1.0 / jnp.sum(exps, axis=0, keepdims=True))
            probs[m * HEAD_PAIRS + h] = p
            joined = head_join(dot(p.astype(bf16), v, TN)).astype(bf16)
            for r in range(ROWS):
                attended[pl.ds((2 * r + m) * COLS, COLS), pl.ds(h * 128, 128)] = joined[
                    r * COLS : (r + 1) * COLS
                ]
    load_out.wait()
    dev[...] = (
        resid[...].astype(f32) + dot(attended[...], outw_s[...]) - t_s[...].astype(f32)
    )
    side_s[...] = jnp.where(part == 3, attended[...], resid[...])
    stores.append(pltpu.make_async_copy(side_s, side_ref, sems.at[12]))
    stores[1].start()
    margin = jnp.zeros((1, 1), f32)
    signs = []
    for m in range(2):
        total = jnp.zeros((1, C), f32)
        for r in range(ROWS):
            d = dev[pl.ds((2 * r + m) * COLS, COLS), :]
            total = total + jnp.sum(d * d, axis=0, keepdims=True)
        error = jnp.sum(total, axis=1, keepdims=True) / (IMG * C)
        sign = jnp.where(label_ref[0] == m, 1.0, -1.0)
        signs.append(sign)
        margin = margin + sign * (error - error_ref[0, m])
    margin_ref[...] = jnp.broadcast_to(margin, (8, 128))
    slope = BETA * sigmoid(BETA * margin)
    for r, m, at in blocks():
        here = pl.ds(at, COLS)
        gall[here, 3 * C : 4 * C] = (signs[m] * slope * dev[here, :]).astype(bf16)
    out_grad = gall[:, 3 * C : 4 * C]
    da = dot(out_grad, outw_s[...], NT).astype(bf16)
    for r, m, at in blocks():
        dattn[m, pl.ds(r * COLS, COLS), :] = da[at : at + COLS]
    for m in range(2):
        for h in range(HEAD_PAIRS):
            q2 = head_halves(qkv[m, :, pl.ds(h * 128, 128)])
            k = qkv[m, :, pl.ds(C + h * 128, 128)]
            v = qkv[m, :, pl.ds(2 * C + h * 128, 128)]
            da2 = head_halves(dattn[m, :, pl.ds(h * 128, 128)])
            p = probs[m * HEAD_PAIRS + h]
            dp = dot(v, da2, NT)
            dots = jnp.sum(p * dp, axis=0, keepdims=True)
            ds = (p * (dp - dots) * SCALE).astype(bf16)
            dq = head_join(dot(ds, k, TN)).astype(bf16)
            dk = dot(ds, q2).astype(bf16)
            dv = dot(p.astype(bf16), da2).astype(bf16)
            for r in range(ROWS):
                here = pl.ds((2 * r + m) * COLS, COLS)
                rows = slice(r * COLS, (r + 1) * COLS)
                gall[here, pl.ds(h * 128, 128)] = dq[rows]
                gall[here, pl.ds(C + h * 128, 128)] = dk[rows]
                gall[here, pl.ds(2 * C + h * 128, 128)] = dv[rows]
    stores.append(pltpu.make_async_copy(gall, gall_ref, sems.at[13]))
    stores[2].start()
    acc[...] = out_grad.astype(f32) + dot(gall[:, 0 : 3 * C], qkvw_s[...], NT)
    cg_s[...] = acc[...].astype(bf16)
    own_s[...] = acc[pl.ds(pl.multiple_of(part * BAND, BAND), BAND), :]
    stores.append(pltpu.make_async_copy(cg_s, cg_ref, sems.at[7]))
    stores.append(pltpu.make_async_copy(own_s, own_ref, sems.at[8]))
    for store in stores[3:]:
        store.start()
    lane = lax.broadcasted_iota(jnp.int32, (160, 2 * IMG), 1)
    own_cols = wire_columns(OWN, 2 * IMG)[:, 0:IMG]
    for x in range(4):
        low = 128 * x
        pick = jnp.where(lane[:, 0:IMG] == own_cols + 32 * x, 1.0, 0.0).astype(bf16)
        turned[160 * x : 160 * (x + 1), :] = dot(pick, cg_s[:, low : low + IMG], NT).astype(bf16)
    for k in range(TAP_BLOCKS):
        place = part * TAP_BLOCKS + k
        cols = slice(k * 128, (k + 1) * 128)

        def tap(place=place, cols=cols):
            up = place // 15
            lane = pl.multiple_of((place - 15 * up) * 128, 128)
            asel[:, cols] = acat[pl.ds(pl.multiple_of(up * BAND, BAND), TOK), pl.ds(lane, 128)]

        if k < 9:
            tap()
        else:
            pl.when(part < 3)(tap)

            @pl.when(part == 3)
            def _(k=k, cols=cols):
                f = feats_s[0:1, (k - 9) * 128 : (k - 8) * 128]
                asel[:, cols] = jnp.broadcast_to(f, (TOK, 128)).astype(bf16)

    for i, low in enumerate((0, 768)):
        cols = slice(low, low + 768)
        wire_s[:, cols] = dot(turned[...], asel[:, cols]).astype(bf16)
        store = pltpu.make_async_copy(wire_s.at[:, cols], wire_ref.at[:, cols], sems.at[9 + i])
        store.start()
        stores.append(store)
    for store in stores:
        store.wait()


def pair_call(part, steps, labels, errors, own, near, core, far, conv, bias, gain, qkvw, outw, timew):
    smem = pl.BlockSpec(memory_space=pltpu.SMEM)
    vmem = pl.BlockSpec(memory_space=pltpu.VMEM)
    hbm = pl.BlockSpec(memory_space=pl.ANY)
    return pl.pallas_call(
        pair_kernel,
        out_shape=(
            jax.ShapeDtypeStruct((C, WIDTH), bf16),
            jax.ShapeDtypeStruct((TOK, C), bf16),
            jax.ShapeDtypeStruct((TOK, 4 * C), bf16),
            jax.ShapeDtypeStruct((TOK, C), bf16),
            jax.ShapeDtypeStruct((TOK, C), bf16),
            jax.ShapeDtypeStruct((BAND, C), f32),
            jax.ShapeDtypeStruct((8, C), f32),
            jax.ShapeDtypeStruct((8, 128), f32),
        ),
        in_specs=[smem] * 4 + [vmem] * 4 + [hbm] + [vmem] * 2 + [hbm] * 3 + [vmem],
        out_specs=[hbm] * 6 + [vmem] * 2,
        scratch_shapes=[
            pltpu.VMEM((TOK + 2 * BAND, 3 * C), bf16),
            pltpu.VMEM((TOK, C), f32),
            pltpu.VMEM((TOK, C), bf16),
            pltpu.VMEM((2, IMG, 3 * C), bf16),
            pltpu.VMEM((2 * HEAD_PAIRS, IMG, 2 * IMG), f32),
            pltpu.VMEM((TOK, C), bf16),
            pltpu.VMEM((TOK, C), f32),
            pltpu.VMEM((TOK, 4 * C), bf16),
            pltpu.VMEM((2, IMG, C), bf16),
            pltpu.VMEM((TOK, TAP_BLOCKS * 128), bf16),
            pltpu.VMEM((8, 384), f32),
            pltpu.VMEM((C, TOK), bf16),
            pltpu.VMEM((C, WIDTH), bf16),
            pltpu.VMEM((TOK, C), bf16),
            pltpu.VMEM((BAND, C), f32),
            pltpu.VMEM((TOK, C), bf16),
            pltpu.VMEM((TOK, C), bf16),
            pltpu.VMEM((TOK, C), bf16),
            pltpu.VMEM((3, 3 * C, C), bf16),
            pltpu.VMEM((C, 3 * C), bf16),
            pltpu.VMEM((C, C), bf16),
            pltpu.VMEM((TDIM, C), bf16),
            pltpu.SemaphoreType.DMA((14,)),
        ],
        compiler_params=pltpu.CompilerParams(vmem_limit_bytes=LIMIT * MIB),
        name="pair",
    )(
        part,
        steps,
        labels,
        errors,
        own,
        near,
        core,
        far,
        conv,
        bias,
        gain,
        qkvw,
        outw,
        timew,
        frequencies(),
    )


def input_kernel(
    part_ref, x_ref, cg_ref, own_ref, stat_ref, gain_ref, conv_ref, in_ref, gg_ref, gcat, acc
):
    part = part_ref[0]
    gcat[0:BAND, :] = jnp.zeros((BAND, 3 * C), bf16)
    gcat[pl.ds(BAND + TOK, BAND), :] = jnp.zeros((BAND, 3 * C), bf16)
    for r, m, at in blocks():
        g = cg_ref[pl.ds(at, COLS), :]
        here = pl.ds(BAND + at, COLS)
        gcat[here, 0:C] = shifted(g.astype(f32), -1).astype(bf16)
        gcat[here, C : 2 * C] = g
        gcat[here, 2 * C : 3 * C] = shifted(g.astype(f32), 1).astype(bf16)
    for i in range(3):
        for j in range(3):
            term = dot(
                gcat[pl.ds((2 - i) * BAND, TOK), j * C : (j + 1) * C],
                conv_ref[i, j * C : (j + 1) * C, :],
                NT,
            )
            if i == 0 and j == 0:
                acc[...] = term
            else:
                acc[...] += term
    gain = gain_ref[...].reshape(1, C)
    gain_sum = jnp.zeros((1, C), f32)
    ones = [jnp.zeros((1, C), f32) for _ in range(2)]
    twos = [jnp.zeros((1, C), f32) for _ in range(2)]
    for r, m, at in blocks():
        here = pl.ds(at, COLS)
        normed = (x_ref[here, :].astype(f32) - stat_ref[row(m), :]) * stat_ref[row(2 + m), :]
        a = normed * gain
        s = sigmoid(a)
        pre = acc[here, :] * (s * (1.0 + a * (1.0 - s)))
        gain_sum = gain_sum + jnp.sum(pre * normed, axis=0, keepdims=True)
        scaled = pre * gain
        acc[here, :] = scaled
        ones[m] = ones[m] + jnp.sum(scaled, axis=0, keepdims=True)
        twos[m] = twos[m] + jnp.sum(scaled * normed, axis=0, keepdims=True)
    bias_sum = jnp.sum(cg_ref[...].astype(f32), axis=0, keepdims=True)
    gg_ref[...] = jnp.concatenate([gain_sum, bias_sum], axis=0)
    means = group_sums(jnp.concatenate(ones + twos, axis=0)) / GROUP_COUNT
    for m in range(2):
        here = pl.ds(pl.multiple_of(part * BAND + m * COLS, COLS), COLS)
        inv = stat_ref[row(2 + m), :]
        normed = (x_ref[here, :].astype(f32) - stat_ref[row(m), :]) * inv
        inner = inv * (acc[here, :] - means[m : m + 1] - normed * means[2 + m : 3 + m])
        mine = slice(m * COLS, (m + 1) * COLS)
        in_ref[mine, :] = (own_ref[mine, :] + inner).astype(bf16)


def input_call(part, x, cg, own, stat, gain, conv):
    smem = pl.BlockSpec(memory_space=pltpu.SMEM)
    vmem = pl.BlockSpec(memory_space=pltpu.VMEM)
    return pl.pallas_call(
        input_kernel,
        out_shape=(
            jax.ShapeDtypeStruct((BAND, C), bf16),
            jax.ShapeDtypeStruct((2, C), f32),
        ),
        in_specs=[smem] + [vmem] * 6,
        out_specs=[vmem] * 2,
        scratch_shapes=[
            pltpu.VMEM((TOK + 2 * BAND, 3 * C), bf16),
            pltpu.VMEM((TOK, C), f32),
        ],
        compiler_params=pltpu.CompilerParams(vmem_limit_bytes=40 * MIB),
        cost_estimate=pl.CostEstimate(
            flops=2 * TOK * 9 * C * C, bytes_accessed=9 * C * C * 2, transcendentals=TOK * C
        ),
        name="input",
    )(part, x, cg, own, stat, gain, conv)


def share_kernel(part_ref, z_ref, gall_ref, side_ref, *refs):
    outs, turned, share = refs[:8], refs[8], refs[9]
    part = part_ref[0]

    def place(x, v):
        for y in range(2):
            for z in range(8):
                to, of = 80 * z + 20 * x + OWN * y, 80 * y + OWN * z
                turned[to : to + OWN, :] = v[of : of + OWN]

    @pl.when(part < 3)
    def _():
        at = lax.broadcasted_iota(jnp.int32, (160, C), 1)
        cols = wire_columns(3 * OWN, C) + OWN * part
        for x, low in enumerate((0, 384, 896, 1280)):
            pick = jnp.where(at == cols + (480 * x - low), 1.0, 0.0).astype(bf16)
            place(x, dot(pick, gall_ref[:, low : low + C], NT))

    @pl.when(part == 3)
    def _():
        at = lax.broadcasted_iota(jnp.int32, (160, IMG), 1)
        cols = wire_columns(OWN, IMG)
        for x in range(4):
            low = 3 * C + 128 * x
            pick = jnp.where(at == cols + 32 * x, 1.0, 0.0).astype(bf16)
            place(x, dot(pick, gall_ref[:, low : low + IMG], NT))

    product = dot(turned[...].astype(bf16), side_ref[...])
    for i in range(8):
        share[i] = product[80 * i : 80 * (i + 1)].astype(bf16)
    for k in range(8):
        outs[k][...] = share[(z_ref[0] + k) & 7]


def share_call(part, z, gall, side):
    smem = pl.BlockSpec(memory_space=pltpu.SMEM)
    vmem = pl.BlockSpec(memory_space=pltpu.VMEM)
    return pl.pallas_call(
        share_kernel,
        out_shape=[jax.ShapeDtypeStruct((80, C), bf16)] * 8,
        in_specs=[smem] * 2 + [vmem] * 2,
        out_specs=[vmem] * 8,
        scratch_shapes=[pltpu.VMEM((C, TOK), f32), pltpu.VMEM((8, 80, C), bf16)],
        compiler_params=pltpu.CompilerParams(vmem_limit_bytes=24 * MIB),
        cost_estimate=pl.CostEstimate(
            flops=4 * TOK * C * C, bytes_accessed=TOK * 5 * C * 2, transcendentals=0
        ),
        name="share",
    )(part, z, gall, side)


def half_kernel(
    z_ref, y_ref, a_ref, shares, gains_ref, out_ref, keep_ref, send_ref, acc, mid, ext, both
):
    total = a_ref[0].astype(f32)
    for i in range(1, 8):
        total = total + a_ref[i].astype(f32)
    acc[...] = total
    for i in range(8):
        for k in range(TAP_BLOCKS):
            mid[i, OWN * k : OWN * (k + 1), :] = acc[
                OWN * i : OWN * (i + 1), 128 * k : 128 * (k + 1)
            ]
    out_ref[...] = mid[...].astype(bf16)
    total = shares[0][...].astype(f32)
    for i in range(1, 8):
        total = total + shares[i][...].astype(f32)
    ext[:, 0:C] = total
    gains = gains_ref[...]
    high = gains.astype(bf16).astype(f32)
    rest = gains - high
    middle = rest.astype(bf16).astype(f32)
    stack = jnp.concatenate([high, middle, rest - middle, jnp.zeros((10, C), f32)], axis=0)
    n = lax.broadcasted_iota(jnp.int32, (80, C), 0)
    x = (n * 3277) >> 16
    cols = 160 * x + 20 * z_ref[0] + n - 20 * x
    pick = jnp.where(lax.broadcasted_iota(jnp.int32, (80, C), 1) == cols, 1.0, 0.0)
    sums = dot(pick.astype(bf16), stack.astype(bf16), NT)
    lane = lax.broadcasted_iota(jnp.int32, (80, 128), 1)
    gain = sums[:, 0:1] + sums[:, 2:3] + sums[:, 4:5]
    bias = sums[:, 1:2] + sums[:, 3:4] + sums[:, 5:6]
    ext[:, C:] = jnp.where(lane == 0, gain, jnp.where(lane == 1, bias, 0.0))
    both[...] = jnp.zeros(both.shape, f32)
    for i in range(4):
        for y in range(2):
            of = 20 * i + OWN * y
            both[y, i, 0:OWN, :] = ext[of : of + OWN, :]
    keep_ref[...] = both[y_ref[0]]
    send_ref[...] = both[1 - y_ref[0]].astype(bf16)


def half_call(z, y, a, shares, gains):
    smem = pl.BlockSpec(memory_space=pltpu.SMEM)
    vmem = pl.BlockSpec(memory_space=pltpu.VMEM)
    return pl.pallas_call(
        lambda z, y, a, *refs: half_kernel(z, y, a, refs[:8], *refs[8:]),
        out_shape=(
            jax.ShapeDtypeStruct((8, TAP_ROWS, 128), bf16),
            jax.ShapeDtypeStruct((4, 16, SIDE), f32),
            jax.ShapeDtypeStruct((4, 16, SIDE), bf16),
        ),
        in_specs=[smem] * 2 + [vmem] * 10,
        out_specs=[vmem] * 3,
        scratch_shapes=[
            pltpu.VMEM((80, WIDTH), f32),
            pltpu.VMEM((8, TAP_ROWS, 128), f32),
            pltpu.VMEM((80, SIDE), f32),
            pltpu.VMEM((2, 4, 16, SIDE), f32),
        ],
        compiler_params=pltpu.CompilerParams(vmem_limit_bytes=32 * MIB),
        name="half",
    )(z, y, a, *shares, gains)


def side_kernel(x_ref, keep_ref, got_ref, own_ref, one_ref, two_ref, three_ref, both):
    both[...] = keep_ref[...] + got_ref[...].astype(f32)
    x = x_ref[0]
    own_ref[...] = both[x]
    for k, ref in enumerate((one_ref, two_ref, three_ref)):
        ref[...] = both[(x + k + 1) & 3].astype(bf16)


def side_call(x, keep, got):
    smem = pl.BlockSpec(memory_space=pltpu.SMEM)
    vmem = pl.BlockSpec(memory_space=pltpu.VMEM)
    return pl.pallas_call(
        side_kernel,
        out_shape=[jax.ShapeDtypeStruct((16, SIDE), f32)]
        + [jax.ShapeDtypeStruct((16, SIDE), bf16)] * 3,
        in_specs=[smem] + [vmem] * 2,
        out_specs=[vmem] * 4,
        scratch_shapes=[pltpu.VMEM((4, 16, SIDE), f32)],
        compiler_params=pltpu.CompilerParams(vmem_limit_bytes=16 * MIB),
        name="side",
    )(x, keep, got)


def total_kernel(a_ref, own_ref, one_ref, two_ref, three_ref, out_ref, gain_ref, mid):
    total = a_ref[0].astype(f32)
    for i in range(1, 8):
        total = total + a_ref[i].astype(f32)
    out_ref[0:TAP_ROWS, :] = total
    mid[...] = (
        own_ref[...]
        + one_ref[...].astype(f32)
        + two_ref[...].astype(f32)
        + three_ref[...].astype(f32)
    )
    for k in range(5):
        at = TAP_ROWS + OWN * k
        out_ref[at : at + OWN, :] = mid[0:OWN, 128 * k : 128 * (k + 1)]
    out_ref[TAP_ROWS + 5 * OWN :, :] = jnp.zeros((CHUNK - TAP_ROWS - 5 * OWN, 128), f32)
    tail = jnp.concatenate([mid[:, C:], jnp.zeros((112, 128), f32)], axis=0)
    gain_ref[...] = jnp.transpose(tail)[0:8]


def total_call(a, own, one, two, three):
    vmem = pl.BlockSpec(memory_space=pltpu.VMEM)
    return pl.pallas_call(
        total_kernel,
        out_shape=(
            jax.ShapeDtypeStruct((CHUNK, 128), f32),
            jax.ShapeDtypeStruct((8, 128), f32),
        ),
        in_specs=[vmem] * 5,
        out_specs=[vmem] * 2,
        scratch_shapes=[pltpu.VMEM((16, SIDE), f32)],
        compiler_params=pltpu.CompilerParams(vmem_limit_bytes=16 * MIB),
        name="total",
    )(a, own, one, two, three)


def unpack_kernel(all_ref, conv_ref, qkv_ref, out_ref, time_ref):
    for part in range(4):
        for k in range(5):
            at = TAP_ROWS + OWN * k
            rows = all_ref[part, at : at + OWN, :]
            cols = slice(128 * k, 128 * (k + 1))
            if part < 3:
                qkv_ref[OWN * part : OWN * (part + 1), cols] = rows
            else:
                out_ref[:, cols] = rows
        for k in range(TAP_BLOCKS):
            rows = all_ref[part, OWN * k : OWN * (k + 1), :]
            place = part * TAP_BLOCKS + k
            tap, block = place // 5, place % 5
            if place < 45:
                conv_ref[tap // 3, :, tap % 3, 128 * block : 128 * (block + 1)] = rows
            else:
                wide = min(128, TDIM - 128 * (place - 45))
                low = 128 * (place - 45)
                time_ref[:, low : low + wide] = rows[:, 0:wide]


def unpack_call(whole):
    vmem = pl.BlockSpec(memory_space=pltpu.VMEM)
    return pl.pallas_call(
        unpack_kernel,
        out_shape=(
            jax.ShapeDtypeStruct((3, OWN, 3, C), f32),
            jax.ShapeDtypeStruct((3 * OWN, C), f32),
            jax.ShapeDtypeStruct((OWN, C), f32),
            jax.ShapeDtypeStruct((OWN, TDIM), f32),
        ),
        in_specs=[vmem],
        out_specs=[vmem] * 4,
        compiler_params=pltpu.CompilerParams(vmem_limit_bytes=16 * MIB),
        name="unpack",
    )(whole)


def on_device(
    section_input,
    target,
    conv_weight,
    conv_bias,
    norm_gain,
    qkv_weight,
    out_weight,
    time_weight,
    timesteps,
    labels,
    ref_error,
):
    part = lax.axis_index(SPACE_AXES).astype(jnp.int32).reshape(1)
    at_x, at_z, at_y = (lax.axis_index(a).astype(jnp.int32).reshape(1) for a in PAIR_AXES)
    swap = [(0, 1), (1, 0)]
    own_xt = jnp.concatenate([section_input.reshape(BAND, C), target.reshape(BAND, C)], axis=0)
    near = lax.ppermute(own_xt, "y_lo", swap)
    core = lax.ppermute(own_xt, "core", swap)
    far = lax.ppermute(near, "core", swap)
    conv = conv_weight.reshape(3, 3 * C, C)
    wire, x, gall, side, cg, own, stat, margin = pair_call(
        part,
        timesteps,
        labels,
        ref_error,
        own_xt,
        near,
        core,
        far,
        conv,
        conv_bias,
        norm_gain,
        qkv_weight,
        out_weight,
        time_weight,
    )
    moved = lax.all_to_all(wire.reshape(8, 80, WIDTH), ("x", "y_hi"), 0, 0)
    shares = share_call(part, at_z, gall, side)
    cg, shares = lax.optimization_barrier((cg, shares))
    shares = list(shares[:1]) + [
        lax.ppermute(shares[k], "z", [(i, (i + k) % 8) for i in range(8)]) for k in range(1, 8)
    ]
    input_grad, gains = input_call(part, x, cg, own, stat, norm_gain, conv)
    gains = lax.psum(gains, "z")
    moved, gains, shares = lax.optimization_barrier((moved, gains, shares))
    half, keep, send = half_call(at_z, at_y, moved, shares, gains)
    got = lax.ppermute(send, "y_hi", swap)
    moved = lax.all_to_all(half, "z", 0, 0)
    mine, *sides = side_call(at_x, keep, got)
    sides = [
        lax.ppermute(sides[k - 1], "x", [(i, (i + k) % 4) for i in range(4)]) for k in range(1, 4)
    ]
    total, gains = total_call(moved, mine, *sides)
    whole = lax.all_gather(total, SPACE_AXES, axis=0, tiled=False)
    conv_out, qkv_out, out_out, time_out = unpack_call(whole)
    pair_loss = jax.nn.softplus(BETA * margin[0, 0:1])
    return (
        input_grad.reshape(section_input.shape),
        conv_out.transpose(0, 2, 3, 1),
        qkv_out.T,
        out_out.T,
        time_out.T,
        gains[0, :OWN],
        gains[1, :OWN],
        pair_loss,
    )


def solution(mesh):
    fine = Mesh(mesh.devices.reshape(MESH_SHAPE), MESH_AXES)
    pairs = P(PAIR_AXES)
    rows = P(PAIR_AXES, None, SPACE_AXES, None, None)
    return jax.shard_map(
        on_device,
        mesh=fine,
        in_specs=(rows, rows, P(), P(), P(), P(), P(), P(), pairs, pairs, pairs),
        out_specs=(
            rows,
            P(None, None, None, PAIR_AXES),
            P(None, PAIR_AXES),
            P(None, PAIR_AXES),
            P(None, PAIR_AXES),
            pairs,
            pairs,
            pairs,
        ),
        check_vma=False,
    )
```

```python
import math

import jax
import jax.numpy as jnp
import numpy as np
from jax import lax
from jax.experimental import pallas as pl
from jax.experimental.pallas import tpu as pltpu
from jax.sharding import Mesh
from jax.sharding import PartitionSpec as P

HEADS = 10
GROUPS = 32
TDIM = 320
C = 640
COLS = 64
ROWS = 4
TOK = 2 * ROWS * COLS
IMG = ROWS * COLS
BAND = 2 * COLS
HEAD_PAIRS = HEADS // 2
GROUP_COUNT = ROWS * COLS * (C // GROUPS)
SCALE = 1.0 / math.sqrt(C // HEADS)
EPS = 1e-05
BETA = 2.0

PAIR_AXES = ("x", "z", "y_hi")
SPACE_AXES = ("y_lo", "core")
MESH_AXES = ("x", "z", "y_hi", "y_lo", "core")
MESH_SHAPE = (4, 8, 2, 2, 2)
OWN = C // 64
TAP_BLOCKS = 12
WIDTH = TAP_BLOCKS * 128
TAP_ROWS = OWN * TAP_BLOCKS
CHUNK = 176
SIDE = C + 128
MIB = 1024 * 1024
LIMIT = 56

f32 = jnp.float32
bf16 = jnp.bfloat16

NN = (((1,), (0,)), ((), ()))
NT = (((1,), (1,)), ((), ()))
TN = (((0,), (0,)), ((), ()))


def dot(a, b, dims=NN):
    return lax.dot_general(a, b, dims, preferred_element_type=f32)


def frequencies():
    half = TDIM // 2
    return np.exp(-math.log(10000.0) * (np.arange(TDIM) % half) / half).astype(np.float32)[None]


def wire_columns(step, width):
    n = lax.broadcasted_iota(jnp.int32, (160, width), 0)
    y = jnp.where(n >= 80, 1, 0)
    rest = n - 80 * y
    z = (rest * 6554) >> 16
    return 2 * step * z + step * y + rest - OWN * z


def row(i):
    return pl.ds(i, 1)


def group_sums(rows):
    a = lax.broadcasted_iota(jnp.int32, (C, C), 0)
    b = lax.broadcasted_iota(jnp.int32, (C, C), 1)
    same = ((a * 3277) >> 16) == ((b * 3277) >> 16)
    ones = jnp.where(same, 1.0, 0.0).astype(bf16)
    high = rows.astype(bf16).astype(f32)
    rest = rows - high
    middle = rest.astype(bf16).astype(f32)
    low = rest - middle
    stack = jnp.concatenate([high, middle, low, jnp.zeros_like(rows)], axis=0).astype(bf16)
    sums = dot(stack, ones)
    return sums[0:4] + sums[4:8] + sums[8:12]


def sigmoid(v):
    return 1.0 / (1.0 + jnp.exp(-v))


def blocks():
    return [(r, m, (2 * r + m) * COLS) for r in range(ROWS) for m in range(2)]


def shifted(v, step):
    at = lax.broadcasted_iota(jnp.int32, (COLS, C), 0)
    if step == 1:
        return jnp.where(at == 0, 0.0, pltpu.roll(v, 1, 0))
    return jnp.where(at == COLS - 1, 0.0, pltpu.roll(v, COLS - 1, 0))


def head_halves(v):
    lane = lax.broadcasted_iota(jnp.int32, (1, 128), 1)
    first = jnp.where(lane < 64, 1.0, 0.0).astype(bf16)
    second = jnp.where(lane < 64, 0.0, 1.0).astype(bf16)
    return jnp.concatenate([v * first, v * second], axis=0)


def head_join(v):
    lane = lax.broadcasted_iota(jnp.int32, (IMG, 128), 1)
    return jnp.where(lane < 64, v[:IMG], v[IMG:])


def pair_kernel(
    part_ref,
    step_ref,
    label_ref,
    error_ref,
    own_xt_ref,
    y_xt_ref,
    core_xt_ref,
    far_xt_ref,
    conv_ref,
    bias_ref,
    gain_ref,
    qkvw_ref,
    outw_ref,
    timew_ref,
    freq_ref,
    wire_ref,
    x_ref,
    gall_ref,
    side_ref,
    cg_ref,
    own_ref,
    stat_ref,
    loss_ref,
    acat,
    acc,
    resid,
    qkv,
    probs,
    attended,
    dev,
    gall,
    dattn,
    asel,
    feats_s,
    turned,
    wire_s,
    cg_s,
    own_s,
    x_s,
    t_s,
    side_s,
    conv_s,
    qkvw_s,
    outw_s,
    timew_s,
    sems,
):
    part = part_ref[0]
    taps = [pltpu.make_async_copy(conv_ref.at[i], conv_s.at[i], sems.at[i]) for i in range(3)]
    load_time = pltpu.make_async_copy(timew_ref, timew_s, sems.at[3])
    load_qkv = pltpu.make_async_copy(qkvw_ref, qkvw_s, sems.at[4])
    load_out = pltpu.make_async_copy(outw_ref, outw_s, sems.at[5])
    taps[0].start()
    load_time.start()
    taps[1].start()
    for ref, way in ((own_xt_ref, 0), (core_xt_ref, 1), (y_xt_ref, 2), (far_xt_ref, 3)):
        rows = pl.ds(pl.multiple_of((part ^ way) * BAND, BAND), BAND)
        x_s[rows, :] = ref[0:BAND, :]
        t_s[rows, :] = ref[BAND : 2 * BAND, :]
    stores = [pltpu.make_async_copy(x_s, x_ref, sems.at[6])]
    sums, squares = [], []
    for m in range(2):
        total = jnp.zeros((1, C), f32)
        square = jnp.zeros((1, C), f32)
        for r in range(ROWS):
            v = x_s[pl.ds((2 * r + m) * COLS, COLS), :].astype(f32)
            total = total + jnp.sum(v, axis=0, keepdims=True)
            square = square + jnp.sum(v * v, axis=0, keepdims=True)
        sums.append(total)
        squares.append(square)
    moments = group_sums(jnp.concatenate(sums + squares, axis=0)) / GROUP_COUNT
    mean = moments[0:2]
    inv = lax.rsqrt(moments[2:4] - mean * mean + EPS)
    stat_ref[...] = jnp.concatenate([mean, inv, jnp.zeros((4, C), f32)], axis=0)
    gain = gain_ref[...].reshape(1, C)
    acat[0:BAND, :] = jnp.zeros((BAND, 3 * C), bf16)
    acat[pl.ds(BAND + TOK, BAND), :] = jnp.zeros((BAND, 3 * C), bf16)
    for r, m, at in blocks():
        v = x_s[pl.ds(at, COLS), :].astype(f32)
        a = (v - mean[m : m + 1]) * inv[m : m + 1] * gain
        act = a * sigmoid(a)
        here = pl.ds(BAND + at, COLS)
        acat[here, 0:C] = shifted(act, 1).astype(bf16)
        acat[here, C : 2 * C] = act.astype(bf16)
        acat[here, 2 * C : 3 * C] = shifted(act, -1).astype(bf16)
    angle = step_ref[0].astype(f32) * freq_ref[...]
    lane = lax.broadcasted_iota(jnp.int32, (1, TDIM), 1)
    feats = jnp.where(lane < TDIM // 2, jnp.cos(angle), jnp.sin(angle))
    feats_s[...] = jnp.zeros((8, 384), f32)
    feats_s[0:1, 0:TDIM] = feats
    load_time.wait()
    shift = dot(jnp.broadcast_to(feats, (16, TDIM)).astype(bf16), timew_s[...])[0:1]
    offset = shift + bias_ref[...].reshape(1, C)
    taps[0].wait()
    taps[2].start()
    load_qkv.start()
    stores[0].start()
    acc[...] = dot(acat[0:TOK, :], conv_s[0])
    taps[1].wait()
    acc[...] += dot(acat[pl.ds(BAND, TOK), :], conv_s[1])
    taps[2].wait()
    acc[...] += dot(acat[pl.ds(2 * BAND, TOK), :], conv_s[2])
    resid[...] = (x_s[...].astype(f32) + acc[...] + offset).astype(bf16)
    load_qkv.wait()
    load_out.start()
    for third in range(3):
        cols = pl.ds(third * C, C)
        proj = dot(resid[...], qkvw_s[:, cols]).astype(bf16)
        for r, m, at in blocks():
            qkv[m, pl.ds(r * COLS, COLS), cols] = proj[at : at + COLS]
    for m in range(2):
        for h in range(HEAD_PAIRS):
            q2 = head_halves(qkv[m, :, pl.ds(h * 128, 128)])
            k = qkv[m, :, pl.ds(C + h * 128, 128)]
            v = qkv[m, :, pl.ds(2 * C + h * 128, 128)]
            scores = dot(k, q2, NT) * SCALE
            exps = jnp.exp(scores - jnp.max(scores, axis=0, keepdims=True))
            p = exps * (1.0 / jnp.sum(exps, axis=0, keepdims=True))
            probs[m * HEAD_PAIRS + h] = p
            joined = head_join(dot(p.astype(bf16), v, TN)).astype(bf16)
            for r in range(ROWS):
                attended[pl.ds((2 * r + m) * COLS, COLS), pl.ds(h * 128, 128)] = joined[
                    r * COLS : (r + 1) * COLS
                ]
    load_out.wait()
    dev[...] = (
        resid[...].astype(f32) + dot(attended[...], outw_s[...]) - t_s[...].astype(f32)
    )
    side_s[...] = jnp.where(part == 3, attended[...], resid[...])
    stores.append(pltpu.make_async_copy(side_s, side_ref, sems.at[12]))
    stores[1].start()
    margin = jnp.zeros((1, 1), f32)
    signs = []
    for m in range(2):
        total = jnp.zeros((1, C), f32)
        for r in range(ROWS):
            d = dev[pl.ds((2 * r + m) * COLS, COLS), :]
            total = total + jnp.sum(d * d, axis=0, keepdims=True)
        error = jnp.sum(total, axis=1, keepdims=True) / (IMG * C)
        sign = jnp.where(label_ref[0] == m, 1.0, -1.0)
        signs.append(sign)
        margin = margin + sign * (error - error_ref[0, m])
    twice = BETA * margin
    loss = jnp.maximum(twice, 0.0) + jnp.log1p(jnp.exp(-jnp.abs(twice)))
    loss_ref[0] = loss[0, 0]
    slope = BETA * sigmoid(BETA * margin)
    for r, m, at in blocks():
        here = pl.ds(at, COLS)
        gall[here, 3 * C : 4 * C] = (signs[m] * slope * dev[here, :]).astype(bf16)
    out_grad = gall[:, 3 * C : 4 * C]
    da = dot(out_grad, outw_s[...], NT).astype(bf16)
    for r, m, at in blocks():
        dattn[m, pl.ds(r * COLS, COLS), :] = da[at : at + COLS]
    for m in range(2):
        for h in range(HEAD_PAIRS):
            q2 = head_halves(qkv[m, :, pl.ds(h * 128, 128)])
            k = qkv[m, :, pl.ds(C + h * 128, 128)]
            v = qkv[m, :, pl.ds(2 * C + h * 128, 128)]
            da2 = head_halves(dattn[m, :, pl.ds(h * 128, 128)])
            p = probs[m * HEAD_PAIRS + h]
            dp = dot(v, da2, NT)
            dots = jnp.sum(p * dp, axis=0, keepdims=True)
            ds = (p * (dp - dots) * SCALE).astype(bf16)
            dq = head_join(dot(ds, k, TN)).astype(bf16)
            dk = dot(ds, q2).astype(bf16)
            dv = dot(p.astype(bf16), da2).astype(bf16)
            for r in range(ROWS):
                here = pl.ds((2 * r + m) * COLS, COLS)
                rows = slice(r * COLS, (r + 1) * COLS)
                gall[here, pl.ds(h * 128, 128)] = dq[rows]
                gall[here, pl.ds(C + h * 128, 128)] = dk[rows]
                gall[here, pl.ds(2 * C + h * 128, 128)] = dv[rows]
    stores.append(pltpu.make_async_copy(gall, gall_ref, sems.at[13]))
    stores[2].start()
    acc[...] = out_grad.astype(f32) + dot(gall[:, 0 : 3 * C], qkvw_s[...], NT)
    cg_s[...] = acc[...].astype(bf16)
    own_s[...] = acc[pl.ds(pl.multiple_of(part * BAND, BAND), BAND), :]
    stores.append(pltpu.make_async_copy(cg_s, cg_ref, sems.at[7]))
    stores.append(pltpu.make_async_copy(own_s, own_ref, sems.at[8]))
    for store in stores[3:]:
        store.start()
    lane = lax.broadcasted_iota(jnp.int32, (160, 2 * IMG), 1)
    own_cols = wire_columns(OWN, 2 * IMG)[:, 0:IMG]
    for x in range(4):
        low = 128 * x
        pick = jnp.where(lane[:, 0:IMG] == own_cols + 32 * x, 1.0, 0.0).astype(bf16)
        turned[160 * x : 160 * (x + 1), :] = dot(pick, cg_s[:, low : low + IMG], NT).astype(bf16)
    for k in range(TAP_BLOCKS):
        place = part * TAP_BLOCKS + k
        cols = slice(k * 128, (k + 1) * 128)

        def tap(place=place, cols=cols):
            up = place // 15
            lane = pl.multiple_of((place - 15 * up) * 128, 128)
            asel[:, cols] = acat[pl.ds(pl.multiple_of(up * BAND, BAND), TOK), pl.ds(lane, 128)]

        if k < 9:
            tap()
        else:
            pl.when(part < 3)(tap)

            @pl.when(part == 3)
            def _(k=k, cols=cols):
                f = feats_s[0:1, (k - 9) * 128 : (k - 8) * 128]
                asel[:, cols] = jnp.broadcast_to(f, (TOK, 128)).astype(bf16)

    for i, low in enumerate((0, 768)):
        cols = slice(low, low + 768)
        wire_s[:, cols] = dot(turned[...], asel[:, cols]).astype(bf16)
        store = pltpu.make_async_copy(wire_s.at[:, cols], wire_ref.at[:, cols], sems.at[9 + i])
        store.start()
        stores.append(store)
    for store in stores:
        store.wait()


def pair_call(part, steps, labels, errors, own, near, core, far, conv, bias, gain, qkvw, outw, timew):
    smem = pl.BlockSpec(memory_space=pltpu.SMEM)
    vmem = pl.BlockSpec(memory_space=pltpu.VMEM)
    hbm = pl.BlockSpec(memory_space=pl.ANY)
    return pl.pallas_call(
        pair_kernel,
        out_shape=(
            jax.ShapeDtypeStruct((C, WIDTH), bf16),
            jax.ShapeDtypeStruct((TOK, C), bf16),
            jax.ShapeDtypeStruct((TOK, 4 * C), bf16),
            jax.ShapeDtypeStruct((TOK, C), bf16),
            jax.ShapeDtypeStruct((TOK, C), bf16),
            jax.ShapeDtypeStruct((BAND, C), f32),
            jax.ShapeDtypeStruct((8, C), f32),
            jax.ShapeDtypeStruct((1,), f32),
        ),
        in_specs=[smem] * 4 + [vmem] * 4 + [hbm] + [vmem] * 2 + [hbm] * 3 + [vmem],
        out_specs=[hbm] * 6 + [vmem, smem],
        scratch_shapes=[
            pltpu.VMEM((TOK + 2 * BAND, 3 * C), bf16),
            pltpu.VMEM((TOK, C), f32),
            pltpu.VMEM((TOK, C), bf16),
            pltpu.VMEM((2, IMG, 3 * C), bf16),
            pltpu.VMEM((2 * HEAD_PAIRS, IMG, 2 * IMG), f32),
            pltpu.VMEM((TOK, C), bf16),
            pltpu.VMEM((TOK, C), f32),
            pltpu.VMEM((TOK, 4 * C), bf16),
            pltpu.VMEM((2, IMG, C), bf16),
            pltpu.VMEM((TOK, TAP_BLOCKS * 128), bf16),
            pltpu.VMEM((8, 384), f32),
            pltpu.VMEM((C, TOK), bf16),
            pltpu.VMEM((C, WIDTH), bf16),
            pltpu.VMEM((TOK, C), bf16),
            pltpu.VMEM((BAND, C), f32),
            pltpu.VMEM((TOK, C), bf16),
            pltpu.VMEM((TOK, C), bf16),
            pltpu.VMEM((TOK, C), bf16),
            pltpu.VMEM((3, 3 * C, C), bf16),
            pltpu.VMEM((C, 3 * C), bf16),
            pltpu.VMEM((C, C), bf16),
            pltpu.VMEM((TDIM, C), bf16),
            pltpu.SemaphoreType.DMA((14,)),
        ],
        compiler_params=pltpu.CompilerParams(vmem_limit_bytes=LIMIT * MIB),
        name="pair",
    )(
        part,
        steps,
        labels,
        errors,
        own,
        near,
        core,
        far,
        conv,
        bias,
        gain,
        qkvw,
        outw,
        timew,
        frequencies(),
    )


def input_kernel(
    part_ref,
    z_ref,
    stat_ref,
    gain_ref,
    cg_ref,
    x_ref,
    own_ref,
    gall_ref,
    side_ref,
    conv_ref,
    in_ref,
    *refs,
):
    outs = refs[:8]
    gcat, acc, cg_s, x_s, own_s, gall_s, side_s, conv_s, turned, columns, share, sems = refs[8:]
    part = part_ref[0]
    load_cg = pltpu.make_async_copy(cg_ref, cg_s, sems.at[0])
    taps = [pltpu.make_async_copy(conv_ref.at[i], conv_s.at[i], sems.at[1 + i]) for i in range(3)]
    rest = [
        pltpu.make_async_copy(ref, to, sems.at[4 + i])
        for i, (ref, to) in enumerate(
            ((x_ref, x_s), (own_ref, own_s), (gall_ref, gall_s), (side_ref, side_s))
        )
    ]
    load_cg.start()
    taps[0].start()
    gcat[0:BAND, :] = jnp.zeros((BAND, 3 * C), bf16)
    gcat[pl.ds(BAND + TOK, BAND), :] = jnp.zeros((BAND, 3 * C), bf16)
    load_cg.wait()
    taps[1].start()
    bias_sum = jnp.zeros((1, C), f32)
    for r, m, at in blocks():
        g = cg_s[pl.ds(at, COLS), :]
        wide = g.astype(f32)
        bias_sum = bias_sum + jnp.sum(wide, axis=0, keepdims=True)
        here = pl.ds(BAND + at, COLS)
        gcat[here, 0:C] = shifted(wide, -1).astype(bf16)
        gcat[here, C : 2 * C] = g
        gcat[here, 2 * C : 3 * C] = shifted(wide, 1).astype(bf16)
    for i in range(3):
        taps[i].wait()
        if i == 0:
            taps[2].start()
            rest[0].start()
        if i == 1:
            for load in rest[1:]:
                load.start()
        for j in range(3):
            term = dot(
                gcat[pl.ds((2 - i) * BAND, TOK), j * C : (j + 1) * C],
                conv_s[i, j * C : (j + 1) * C, :],
                NT,
            )
            if i == 0 and j == 0:
                acc[...] = term
            else:
                acc[...] += term
    for load in rest:
        load.wait()
    gain = gain_ref[...].reshape(1, C)
    gain_sum = jnp.zeros((1, C), f32)
    ones = [jnp.zeros((1, C), f32) for _ in range(2)]
    twos = [jnp.zeros((1, C), f32) for _ in range(2)]
    for r, m, at in blocks():
        here = pl.ds(at, COLS)
        normed = (x_s[here, :].astype(f32) - stat_ref[row(m), :]) * stat_ref[row(2 + m), :]
        a = normed * gain
        s = sigmoid(a)
        pre = acc[here, :] * (s * (1.0 + a * (1.0 - s)))
        gain_sum = gain_sum + jnp.sum(pre * normed, axis=0, keepdims=True)
        scaled = pre * gain
        acc[here, :] = scaled
        ones[m] = ones[m] + jnp.sum(scaled, axis=0, keepdims=True)
        twos[m] = twos[m] + jnp.sum(scaled * normed, axis=0, keepdims=True)
    lane = lax.broadcasted_iota(jnp.int32, (160, IMG), 1)
    own_cols = wire_columns(OWN, IMG)

    def place(to_ref, x, v):
        for y in range(2):
            for z in range(8):
                to, of = 80 * z + 20 * x + OWN * y, 80 * y + OWN * z
                to_ref[to : to + OWN, :] = v[of : of + OWN]

    rows = jnp.concatenate([gain_sum, bias_sum], axis=0)
    high = rows.astype(bf16).astype(f32)
    left = rows - high
    middle = left.astype(bf16).astype(f32)
    stack = jnp.concatenate([high, middle, left - middle, jnp.zeros((122, C), f32)], axis=0)
    stack = stack.astype(bf16)
    for x in range(4):
        pick = jnp.where(lane == own_cols + 32 * x, 1.0, 0.0).astype(bf16)
        place(columns, x, dot(pick, stack[:, 128 * x : 128 * x + IMG], NT))

    @pl.when(part < 3)
    def _():
        at = lax.broadcasted_iota(jnp.int32, (160, C), 1)
        cols = wire_columns(3 * OWN, C) + OWN * part
        for x, low in enumerate((0, 384, 896, 1280)):
            pick = jnp.where(at == cols + (480 * x - low), 1.0, 0.0).astype(bf16)
            place(turned, x, dot(pick, gall_s[:, low : low + C], NT))

    @pl.when(part == 3)
    def _():
        for x in range(4):
            low = 3 * C + 128 * x
            pick = jnp.where(lane == own_cols + 32 * x, 1.0, 0.0).astype(bf16)
            place(turned, x, dot(pick, gall_s[:, low : low + IMG], NT))

    product = dot(turned[...].astype(bf16), side_s[...])
    at = lax.broadcasted_iota(jnp.int32, (80, 128), 1)
    for i in range(8):
        here = slice(80 * i, 80 * (i + 1))
        share[i, :, 0:C] = product[here].astype(bf16)
        sums = columns[here, :]
        gains = sums[:, 0:1] + sums[:, 2:3] + sums[:, 4:5]
        biases = sums[:, 1:2] + sums[:, 3:4] + sums[:, 5:6]
        share[i, :, C:] = jnp.where(at == 0, gains, jnp.where(at == 1, biases, 0.0)).astype(bf16)
    for k in range(8):
        outs[k][...] = share[(z_ref[0] + k) & 7]
    means = group_sums(jnp.concatenate(ones + twos, axis=0)) / GROUP_COUNT
    for m in range(2):
        here = pl.ds(pl.multiple_of(part * BAND + m * COLS, COLS), COLS)
        inv = stat_ref[row(2 + m), :]
        normed = (x_s[here, :].astype(f32) - stat_ref[row(m), :]) * inv
        inner = inv * (acc[here, :] - means[m : m + 1] - normed * means[2 + m : 3 + m])
        mine = slice(m * COLS, (m + 1) * COLS)
        in_ref[mine, :] = (own_s[mine, :] + inner).astype(bf16)


def input_call(part, z, stat, gain, cg, x, own, gall, side, conv):
    smem = pl.BlockSpec(memory_space=pltpu.SMEM)
    vmem = pl.BlockSpec(memory_space=pltpu.VMEM)
    hbm = pl.BlockSpec(memory_space=pltpu.HBM)
    return pl.pallas_call(
        input_kernel,
        out_shape=[jax.ShapeDtypeStruct((BAND, C), bf16)]
        + [jax.ShapeDtypeStruct((80, SIDE), bf16)] * 8,
        in_specs=[smem] * 2 + [vmem] * 2 + [hbm] * 6,
        out_specs=[vmem] * 9,
        scratch_shapes=[
            pltpu.VMEM((TOK + 2 * BAND, 3 * C), bf16),
            pltpu.VMEM((TOK, C), f32),
            pltpu.VMEM((TOK, C), bf16),
            pltpu.VMEM((TOK, C), bf16),
            pltpu.VMEM((BAND, C), f32),
            pltpu.VMEM((TOK, 4 * C), bf16),
            pltpu.VMEM((TOK, C), bf16),
            pltpu.VMEM((3, 3 * C, C), bf16),
            pltpu.VMEM((C, TOK), f32),
            pltpu.VMEM((C, 128), f32),
            pltpu.VMEM((8, 80, SIDE), bf16),
            pltpu.SemaphoreType.DMA((8,)),
        ],
        compiler_params=pltpu.CompilerParams(vmem_limit_bytes=LIMIT * MIB),
        cost_estimate=pl.CostEstimate(
            flops=2 * TOK * 10 * C * C, bytes_accessed=9 * C * C * 2, transcendentals=TOK * C
        ),
        name="input",
    )(part, z, stat, gain, cg, x, own, gall, side, conv)


def chunk_kernel(y_ref, *refs):
    shares, keep_ref, send_ref, ext, both = refs[:8], *refs[8:]
    total = shares[0][...].astype(f32)
    for i in range(1, 8):
        total = total + shares[i][...].astype(f32)
    ext[...] = total
    both[...] = jnp.zeros(both.shape, f32)
    for i in range(4):
        for y in range(2):
            of = 20 * i + OWN * y
            both[y, i, 0:OWN, :] = ext[of : of + OWN, :]
    keep_ref[...] = both[y_ref[0]]
    send_ref[...] = both[1 - y_ref[0]].astype(bf16)


def chunk_call(y, shares):
    smem = pl.BlockSpec(memory_space=pltpu.SMEM)
    vmem = pl.BlockSpec(memory_space=pltpu.VMEM)
    return pl.pallas_call(
        chunk_kernel,
        out_shape=(
            jax.ShapeDtypeStruct((4, 16, SIDE), f32),
            jax.ShapeDtypeStruct((4, 16, SIDE), bf16),
        ),
        in_specs=[smem] + [vmem] * 8,
        out_specs=[vmem] * 2,
        scratch_shapes=[
            pltpu.VMEM((80, SIDE), f32),
            pltpu.VMEM((2, 4, 16, SIDE), f32),
        ],
        compiler_params=pltpu.CompilerParams(vmem_limit_bytes=16 * MIB),
        name="chunk",
    )(y, *shares)


def half_kernel(a_ref, out_ref, acc, mid):
    total = a_ref[0].astype(f32)
    for i in range(1, 8):
        total = total + a_ref[i].astype(f32)
    acc[...] = total
    for i in range(8):
        for k in range(TAP_BLOCKS):
            mid[i, OWN * k : OWN * (k + 1), :] = acc[
                OWN * i : OWN * (i + 1), 128 * k : 128 * (k + 1)
            ]
    out_ref[...] = mid[...].astype(bf16)


def half_call(a):
    vmem = pl.BlockSpec(memory_space=pltpu.VMEM)
    return pl.pallas_call(
        half_kernel,
        out_shape=jax.ShapeDtypeStruct((8, TAP_ROWS, 128), bf16),
        in_specs=[vmem],
        out_specs=vmem,
        scratch_shapes=[
            pltpu.VMEM((80, WIDTH), f32),
            pltpu.VMEM((8, TAP_ROWS, 128), f32),
        ],
        compiler_params=pltpu.CompilerParams(vmem_limit_bytes=32 * MIB),
        name="half",
    )(a)


def side_kernel(x_ref, keep_ref, got_ref, own_ref, one_ref, two_ref, three_ref, both):
    both[...] = keep_ref[...] + got_ref[...].astype(f32)
    x = x_ref[0]
    own_ref[...] = both[x]
    for k, ref in enumerate((one_ref, two_ref, three_ref)):
        ref[...] = both[(x + k + 1) & 3].astype(bf16)


def side_call(x, keep, got):
    smem = pl.BlockSpec(memory_space=pltpu.SMEM)
    vmem = pl.BlockSpec(memory_space=pltpu.VMEM)
    return pl.pallas_call(
        side_kernel,
        out_shape=[jax.ShapeDtypeStruct((16, SIDE), f32)]
        + [jax.ShapeDtypeStruct((16, SIDE), bf16)] * 3,
        in_specs=[smem] + [vmem] * 2,
        out_specs=[vmem] * 4,
        scratch_shapes=[pltpu.VMEM((4, 16, SIDE), f32)],
        compiler_params=pltpu.CompilerParams(vmem_limit_bytes=16 * MIB),
        name="side",
    )(x, keep, got)


def total_kernel(a_ref, own_ref, one_ref, two_ref, three_ref, out_ref, gain_ref, mid):
    total = a_ref[0].astype(f32)
    for i in range(1, 8):
        total = total + a_ref[i].astype(f32)
    out_ref[0:TAP_ROWS, :] = total
    mid[...] = (
        own_ref[...]
        + one_ref[...].astype(f32)
        + two_ref[...].astype(f32)
        + three_ref[...].astype(f32)
    )
    for k in range(5):
        at = TAP_ROWS + OWN * k
        out_ref[at : at + OWN, :] = mid[0:OWN, 128 * k : 128 * (k + 1)]
    out_ref[TAP_ROWS + 5 * OWN :, :] = jnp.zeros((CHUNK - TAP_ROWS - 5 * OWN, 128), f32)
    tail = jnp.concatenate([mid[:, C:], jnp.zeros((112, 128), f32)], axis=0)
    gain_ref[...] = jnp.transpose(tail)[0:8]


def total_call(a, own, one, two, three):
    vmem = pl.BlockSpec(memory_space=pltpu.VMEM)
    return pl.pallas_call(
        total_kernel,
        out_shape=(
            jax.ShapeDtypeStruct((CHUNK, 128), f32),
            jax.ShapeDtypeStruct((8, 128), f32),
        ),
        in_specs=[vmem] * 5,
        out_specs=[vmem] * 2,
        scratch_shapes=[pltpu.VMEM((16, SIDE), f32)],
        compiler_params=pltpu.CompilerParams(vmem_limit_bytes=16 * MIB),
        name="total",
    )(a, own, one, two, three)


def unpack_kernel(all_ref, conv_ref, qkv_ref, out_ref, time_ref):
    for part in range(4):
        for k in range(5):
            at = TAP_ROWS + OWN * k
            rows = all_ref[part, at : at + OWN, :]
            cols = slice(128 * k, 128 * (k + 1))
            if part < 3:
                qkv_ref[OWN * part : OWN * (part + 1), cols] = rows
            else:
                out_ref[:, cols] = rows
        for k in range(TAP_BLOCKS):
            rows = all_ref[part, OWN * k : OWN * (k + 1), :]
            place = part * TAP_BLOCKS + k
            tap, block = place // 5, place % 5
            if place < 45:
                conv_ref[tap // 3, :, tap % 3, 128 * block : 128 * (block + 1)] = rows
            else:
                wide = min(128, TDIM - 128 * (place - 45))
                low = 128 * (place - 45)
                time_ref[:, low : low + wide] = rows[:, 0:wide]


def unpack_call(whole):
    vmem = pl.BlockSpec(memory_space=pltpu.VMEM)
    return pl.pallas_call(
        unpack_kernel,
        out_shape=(
            jax.ShapeDtypeStruct((3, OWN, 3, C), f32),
            jax.ShapeDtypeStruct((3 * OWN, C), f32),
            jax.ShapeDtypeStruct((OWN, C), f32),
            jax.ShapeDtypeStruct((OWN, TDIM), f32),
        ),
        in_specs=[vmem],
        out_specs=[vmem] * 4,
        compiler_params=pltpu.CompilerParams(vmem_limit_bytes=16 * MIB),
        name="unpack",
    )(whole)


def on_device(
    section_input,
    target,
    conv_weight,
    conv_bias,
    norm_gain,
    qkv_weight,
    out_weight,
    time_weight,
    timesteps,
    labels,
    ref_error,
):
    part = lax.axis_index(SPACE_AXES).astype(jnp.int32).reshape(1)
    at_x, at_z, at_y = (lax.axis_index(a).astype(jnp.int32).reshape(1) for a in PAIR_AXES)
    swap = [(0, 1), (1, 0)]
    own_xt = jnp.concatenate([section_input.reshape(BAND, C), target.reshape(BAND, C)], axis=0)
    near = lax.ppermute(own_xt, "y_lo", swap)
    core = lax.ppermute(own_xt, "core", swap)
    far = lax.ppermute(near, "core", swap)
    conv = conv_weight.reshape(3, 3 * C, C)
    wire, x, gall, side, cg, own, stat, pair_loss = pair_call(
        part,
        timesteps,
        labels,
        ref_error,
        own_xt,
        near,
        core,
        far,
        conv,
        conv_bias,
        norm_gain,
        qkv_weight,
        out_weight,
        time_weight,
    )
    moved = lax.all_to_all(wire.reshape(8, 80, WIDTH), ("x", "y_hi"), 0, 0)
    input_grad, *shares = input_call(
        part, at_z, stat, norm_gain, cg, x, own, gall, side, conv
    )
    shares = shares[:1] + [
        lax.ppermute(shares[k], "z", [(i, (i + k) % 8) for i in range(8)]) for k in range(1, 8)
    ]
    keep, send = chunk_call(at_y, shares)
    got = lax.ppermute(send, "y_hi", swap)
    moved, keep = lax.optimization_barrier((moved, keep))
    moved = lax.all_to_all(half_call(moved), "z", 0, 0)
    mine, *sides = side_call(at_x, keep, got)
    sides = [
        lax.ppermute(sides[k - 1], "x", [(i, (i + k) % 4) for i in range(4)]) for k in range(1, 4)
    ]
    total, gains = total_call(moved, mine, *sides)
    whole = lax.all_gather(total, SPACE_AXES, axis=0, tiled=False)
    conv_out, qkv_out, out_out, time_out = unpack_call(whole)
    return (
        input_grad.reshape(section_input.shape),
        conv_out.transpose(0, 2, 3, 1),
        qkv_out.T,
        out_out.T,
        time_out.T,
        gains[0, :OWN],
        gains[1, :OWN],
        pair_loss,
    )


def solution(mesh):
    fine = Mesh(mesh.devices.reshape(MESH_SHAPE), MESH_AXES)
    pairs = P(PAIR_AXES)
    rows = P(PAIR_AXES, None, SPACE_AXES, None, None)
    return jax.shard_map(
        on_device,
        mesh=fine,
        in_specs=(rows, rows, P(), P(), P(), P(), P(), P(), pairs, pairs, pairs),
        out_specs=(
            rows,
            P(None, None, None, PAIR_AXES),
            P(None, PAIR_AXES),
            P(None, PAIR_AXES),
            P(None, PAIR_AXES),
            pairs,
            pairs,
            pairs,
        ),
        check_vma=False,
    )
```

```python
import math

import jax
import jax.numpy as jnp
import numpy as np
from jax import lax
from jax.experimental import pallas as pl
from jax.experimental.pallas import tpu as pltpu
from jax.sharding import Mesh
from jax.sharding import PartitionSpec as P

HEADS = 10
GROUPS = 32
TDIM = 320
C = 640
COLS = 64
ROWS = 4
TOK = 2 * ROWS * COLS
IMG = ROWS * COLS
BAND = 2 * COLS
HEAD_PAIRS = HEADS // 2
GROUP_COUNT = ROWS * COLS * (C // GROUPS)
SCALE = 1.0 / math.sqrt(C // HEADS)
EPS = 1e-05
BETA = 2.0

PAIR_AXES = ("x", "z", "y_hi")
SPACE_AXES = ("y_lo", "core")
MESH_AXES = ("x", "z", "y_hi", "y_lo", "core")
MESH_SHAPE = (4, 8, 2, 2, 2)
OWN = C // 64
TAP_BLOCKS = 12
BLOCKS = 5 + TAP_BLOCKS
WIDTH = BLOCKS * 128
CHUNK = 176
MIB = 1024 * 1024
LIMIT = 56

f32 = jnp.float32
bf16 = jnp.bfloat16

NN = (((1,), (0,)), ((), ()))
NT = (((1,), (1,)), ((), ()))
TN = (((0,), (0,)), ((), ()))


def dot(a, b, dims=NN):
    return lax.dot_general(a, b, dims, preferred_element_type=f32)


def frequencies():
    half = TDIM // 2
    return np.exp(-math.log(10000.0) * (np.arange(TDIM) % half) / half).astype(np.float32)[None]


def wire_columns(step, width):
    n = lax.broadcasted_iota(jnp.int32, (160, width), 0)
    y = jnp.where(n >= 80, 1, 0)
    rest = n - 80 * y
    z = (rest * 6554) >> 16
    return 2 * step * z + step * y + rest - OWN * z


def row(i):
    return pl.ds(i, 1)


def group_sums(rows):
    a = lax.broadcasted_iota(jnp.int32, (C, C), 0)
    b = lax.broadcasted_iota(jnp.int32, (C, C), 1)
    same = ((a * 3277) >> 16) == ((b * 3277) >> 16)
    ones = jnp.where(same, 1.0, 0.0).astype(bf16)
    high = rows.astype(bf16).astype(f32)
    rest = rows - high
    middle = rest.astype(bf16).astype(f32)
    low = rest - middle
    stack = jnp.concatenate([high, middle, low, jnp.zeros_like(rows)], axis=0).astype(bf16)
    sums = dot(stack, ones)
    return sums[0:4] + sums[4:8] + sums[8:12]


def sigmoid(v):
    return 1.0 / (1.0 + jnp.exp(-v))


def blocks():
    return [(r, m, (2 * r + m) * COLS) for r in range(ROWS) for m in range(2)]


def shifted(v, step):
    at = lax.broadcasted_iota(jnp.int32, (COLS, C), 0)
    if step == 1:
        return jnp.where(at == 0, 0.0, pltpu.roll(v, 1, 0))
    return jnp.where(at == COLS - 1, 0.0, pltpu.roll(v, COLS - 1, 0))


def head_halves(v):
    lane = lax.broadcasted_iota(jnp.int32, (1, 128), 1)
    first = jnp.where(lane < 64, 1.0, 0.0).astype(bf16)
    second = jnp.where(lane < 64, 0.0, 1.0).astype(bf16)
    return jnp.concatenate([v * first, v * second], axis=0)


def head_join(v):
    lane = lax.broadcasted_iota(jnp.int32, (IMG, 128), 1)
    return jnp.where(lane < 64, v[:IMG], v[IMG:])


def pair_kernel(
    part_ref,
    step_ref,
    label_ref,
    error_ref,
    own_xt_ref,
    y_xt_ref,
    core_xt_ref,
    far_xt_ref,
    conv_ref,
    bias_ref,
    gain_ref,
    qkvw_ref,
    outw_ref,
    timew_ref,
    freq_ref,
    wire_ref,
    x_ref,
    cg_ref,
    own_ref,
    stat_ref,
    loss_ref,
    acat,
    acc,
    resid,
    qkv,
    probs,
    attended,
    dev,
    gall,
    dattn,
    asel,
    feats_s,
    turned,
    wire_s,
    cg_s,
    own_s,
    x_s,
    t_s,
    conv_s,
    qkvw_s,
    outw_s,
    timew_s,
    sems,
):
    part = part_ref[0]
    taps = [pltpu.make_async_copy(conv_ref.at[i], conv_s.at[i], sems.at[i]) for i in range(3)]
    load_time = pltpu.make_async_copy(timew_ref, timew_s, sems.at[3])
    load_qkv = pltpu.make_async_copy(qkvw_ref, qkvw_s, sems.at[4])
    load_out = pltpu.make_async_copy(outw_ref, outw_s, sems.at[5])
    taps[0].start()
    load_time.start()
    taps[1].start()
    for ref, way in ((own_xt_ref, 0), (core_xt_ref, 1), (y_xt_ref, 2), (far_xt_ref, 3)):
        rows = pl.ds(pl.multiple_of((part ^ way) * BAND, BAND), BAND)
        x_s[rows, :] = ref[0:BAND, :]
        t_s[rows, :] = ref[BAND : 2 * BAND, :]
    stores = [pltpu.make_async_copy(x_s, x_ref, sems.at[6])]
    sums, squares = [], []
    for m in range(2):
        total = jnp.zeros((1, C), f32)
        square = jnp.zeros((1, C), f32)
        for r in range(ROWS):
            v = x_s[pl.ds((2 * r + m) * COLS, COLS), :].astype(f32)
            total = total + jnp.sum(v, axis=0, keepdims=True)
            square = square + jnp.sum(v * v, axis=0, keepdims=True)
        sums.append(total)
        squares.append(square)
    moments = group_sums(jnp.concatenate(sums + squares, axis=0)) / GROUP_COUNT
    mean = moments[0:2]
    inv = lax.rsqrt(moments[2:4] - mean * mean + EPS)
    stat_ref[...] = jnp.concatenate([mean, inv, jnp.zeros((4, C), f32)], axis=0)
    gain = gain_ref[...].reshape(1, C)
    acat[0:BAND, :] = jnp.zeros((BAND, 3 * C), bf16)
    acat[pl.ds(BAND + TOK, BAND), :] = jnp.zeros((BAND, 3 * C), bf16)
    for r, m, at in blocks():
        v = x_s[pl.ds(at, COLS), :].astype(f32)
        a = (v - mean[m : m + 1]) * inv[m : m + 1] * gain
        act = a * sigmoid(a)
        here = pl.ds(BAND + at, COLS)
        acat[here, 0:C] = shifted(act, 1).astype(bf16)
        acat[here, C : 2 * C] = act.astype(bf16)
        acat[here, 2 * C : 3 * C] = shifted(act, -1).astype(bf16)
    angle = step_ref[0].astype(f32) * freq_ref[...]
    lane = lax.broadcasted_iota(jnp.int32, (1, TDIM), 1)
    feats = jnp.where(lane < TDIM // 2, jnp.cos(angle), jnp.sin(angle))
    feats_s[...] = jnp.zeros((8, 384), f32)
    feats_s[0:1, 0:TDIM] = feats
    load_time.wait()
    shift = dot(jnp.broadcast_to(feats, (16, TDIM)).astype(bf16), timew_s[...])[0:1]
    offset = shift + bias_ref[...].reshape(1, C)
    taps[0].wait()
    taps[2].start()
    load_qkv.start()
    stores[0].start()
    acc[...] = dot(acat[0:TOK, :], conv_s[0])
    taps[1].wait()
    acc[...] += dot(acat[pl.ds(BAND, TOK), :], conv_s[1])
    taps[2].wait()
    acc[...] += dot(acat[pl.ds(2 * BAND, TOK), :], conv_s[2])
    resid[...] = (x_s[...].astype(f32) + acc[...] + offset).astype(bf16)
    load_qkv.wait()
    load_out.start()
    for third in range(3):
        cols = pl.ds(third * C, C)
        proj = dot(resid[...], qkvw_s[:, cols]).astype(bf16)
        for r, m, at in blocks():
            qkv[m, pl.ds(r * COLS, COLS), cols] = proj[at : at + COLS]
    for m in range(2):
        for h in range(HEAD_PAIRS):
            q2 = head_halves(qkv[m, :, pl.ds(h * 128, 128)])
            k = qkv[m, :, pl.ds(C + h * 128, 128)]
            v = qkv[m, :, pl.ds(2 * C + h * 128, 128)]
            scores = dot(k, q2, NT) * SCALE
            exps = jnp.exp(scores - jnp.max(scores, axis=0, keepdims=True))
            p = exps * (1.0 / jnp.sum(exps, axis=0, keepdims=True))
            probs[m * HEAD_PAIRS + h] = p
            joined = head_join(dot(p.astype(bf16), v, TN)).astype(bf16)
            for r in range(ROWS):
                attended[pl.ds((2 * r + m) * COLS, COLS), pl.ds(h * 128, 128)] = joined[
                    r * COLS : (r + 1) * COLS
                ]
    load_out.wait()
    dev[...] = (
        resid[...].astype(f32) + dot(attended[...], outw_s[...]) - t_s[...].astype(f32)
    )
    margin = jnp.zeros((1, 1), f32)
    signs = []
    for m in range(2):
        total = jnp.zeros((1, C), f32)
        for r in range(ROWS):
            d = dev[pl.ds((2 * r + m) * COLS, COLS), :]
            total = total + jnp.sum(d * d, axis=0, keepdims=True)
        error = jnp.sum(total, axis=1, keepdims=True) / (IMG * C)
        sign = jnp.where(label_ref[0] == m, 1.0, -1.0)
        signs.append(sign)
        margin = margin + sign * (error - error_ref[0, m])
    twice = BETA * margin
    loss = jnp.maximum(twice, 0.0) + jnp.log1p(jnp.exp(-jnp.abs(twice)))
    loss_ref[0] = loss[0, 0]
    slope = BETA * sigmoid(BETA * margin)
    for r, m, at in blocks():
        here = pl.ds(at, COLS)
        gall[here, 3 * C : 4 * C] = (signs[m] * slope * dev[here, :]).astype(bf16)
    out_grad = gall[:, 3 * C : 4 * C]
    da = dot(out_grad, outw_s[...], NT).astype(bf16)
    for r, m, at in blocks():
        dattn[m, pl.ds(r * COLS, COLS), :] = da[at : at + COLS]
    for m in range(2):
        for h in range(HEAD_PAIRS):
            q2 = head_halves(qkv[m, :, pl.ds(h * 128, 128)])
            k = qkv[m, :, pl.ds(C + h * 128, 128)]
            v = qkv[m, :, pl.ds(2 * C + h * 128, 128)]
            da2 = head_halves(dattn[m, :, pl.ds(h * 128, 128)])
            p = probs[m * HEAD_PAIRS + h]
            dp = dot(v, da2, NT)
            dots = jnp.sum(p * dp, axis=0, keepdims=True)
            ds = (p * (dp - dots) * SCALE).astype(bf16)
            dq = head_join(dot(ds, k, TN)).astype(bf16)
            dk = dot(ds, q2).astype(bf16)
            dv = dot(p.astype(bf16), da2).astype(bf16)
            for r in range(ROWS):
                here = pl.ds((2 * r + m) * COLS, COLS)
                rows = slice(r * COLS, (r + 1) * COLS)
                gall[here, pl.ds(h * 128, 128)] = dq[rows]
                gall[here, pl.ds(C + h * 128, 128)] = dk[rows]
                gall[here, pl.ds(2 * C + h * 128, 128)] = dv[rows]
    acc[...] = out_grad.astype(f32) + dot(gall[:, 0 : 3 * C], qkvw_s[...], NT)
    cg_s[...] = acc[...].astype(bf16)
    own_s[...] = acc[pl.ds(pl.multiple_of(part * BAND, BAND), BAND), :]
    stores.append(pltpu.make_async_copy(cg_s, cg_ref, sems.at[7]))
    stores.append(pltpu.make_async_copy(own_s, own_ref, sems.at[8]))
    for store in stores[1:]:
        store.start()
    lane = lax.broadcasted_iota(jnp.int32, (160, 2 * IMG), 1)
    own_cols = wire_columns(OWN, 2 * IMG)[:, 0:IMG]
    for x in range(4):
        low = 128 * x
        pick = jnp.where(lane[:, 0:IMG] == own_cols + 32 * x, 1.0, 0.0).astype(bf16)
        turned[160 * x : 160 * (x + 1), :] = dot(pick, cg_s[:, low : low + IMG], NT).astype(bf16)
    for k in range(TAP_BLOCKS):
        place = part * TAP_BLOCKS + k
        cols = slice(k * 128, (k + 1) * 128)

        def tap(place=place, cols=cols):
            up = place // 15
            lane = pl.multiple_of((place - 15 * up) * 128, 128)
            asel[:, cols] = acat[pl.ds(pl.multiple_of(up * BAND, BAND), TOK), pl.ds(lane, 128)]

        if k < 9:
            tap()
        else:
            pl.when(part < 3)(tap)

            @pl.when(part == 3)
            def _(k=k, cols=cols):
                f = feats_s[0:1, (k - 9) * 128 : (k - 8) * 128]
                asel[:, cols] = jnp.broadcast_to(f, (TOK, 128)).astype(bf16)

    for i, low in enumerate((C, C + 768)):
        cols = slice(low, low + 768)
        wire_s[:, cols] = dot(turned[...], asel[:, low - C : low - C + 768]).astype(bf16)
        store = pltpu.make_async_copy(wire_s.at[:, cols], wire_ref.at[:, cols], sems.at[9 + i])
        store.start()
        stores.append(store)

    @pl.when(part < 3)
    def _():
        at = lax.broadcasted_iota(jnp.int32, (160, C), 1)
        cols = wire_columns(3 * OWN, C) + OWN * part
        for x, low in enumerate((0, 384, 896, 1280)):
            pick = jnp.where(at == cols + (480 * x - low), 1.0, 0.0).astype(bf16)
            turned[160 * x : 160 * (x + 1), :] = dot(pick, gall[:, low : low + C], NT).astype(bf16)
        wire_s[:, 0:C] = dot(turned[...], resid[...]).astype(bf16)

    @pl.when(part == 3)
    def _():
        for x in range(4):
            low = 3 * C + 128 * x
            pick = jnp.where(lane[:, 0:IMG] == own_cols + 32 * x, 1.0, 0.0).astype(bf16)
            turned[160 * x : 160 * (x + 1), :] = dot(pick, gall[:, low : low + IMG], NT).astype(
                bf16
            )
        wire_s[:, 0:C] = dot(turned[...], attended[...]).astype(bf16)

    store = pltpu.make_async_copy(wire_s.at[:, 0:C], wire_ref.at[:, 0:C], sems.at[11])
    store.start()
    for each in stores + [store]:
        each.wait()


def pair_call(part, steps, labels, errors, own, near, core, far, conv, bias, gain, qkvw, outw, timew):
    smem = pl.BlockSpec(memory_space=pltpu.SMEM)
    vmem = pl.BlockSpec(memory_space=pltpu.VMEM)
    hbm = pl.BlockSpec(memory_space=pl.ANY)
    return pl.pallas_call(
        pair_kernel,
        out_shape=(
            jax.ShapeDtypeStruct((C, WIDTH), bf16),
            jax.ShapeDtypeStruct((TOK, C), bf16),
            jax.ShapeDtypeStruct((TOK, C), bf16),
            jax.ShapeDtypeStruct((BAND, C), f32),
            jax.ShapeDtypeStruct((8, C), f32),
            jax.ShapeDtypeStruct((1,), f32),
        ),
        in_specs=[smem] * 4 + [vmem] * 4 + [hbm] + [vmem] * 2 + [hbm] * 3 + [vmem],
        out_specs=[hbm] * 4 + [vmem, smem],
        scratch_shapes=[
            pltpu.VMEM((TOK + 2 * BAND, 3 * C), bf16),
            pltpu.VMEM((TOK, C), f32),
            pltpu.VMEM((TOK, C), bf16),
            pltpu.VMEM((2, IMG, 3 * C), bf16),
            pltpu.VMEM((2 * HEAD_PAIRS, IMG, 2 * IMG), f32),
            pltpu.VMEM((TOK, C), bf16),
            pltpu.VMEM((TOK, C), f32),
            pltpu.VMEM((TOK, 4 * C), bf16),
            pltpu.VMEM((2, IMG, C), bf16),
            pltpu.VMEM((TOK, TAP_BLOCKS * 128), bf16),
            pltpu.VMEM((8, 384), f32),
            pltpu.VMEM((C, TOK), bf16),
            pltpu.VMEM((C, WIDTH), bf16),
            pltpu.VMEM((TOK, C), bf16),
            pltpu.VMEM((BAND, C), f32),
            pltpu.VMEM((TOK, C), bf16),
            pltpu.VMEM((TOK, C), bf16),
            pltpu.VMEM((3, 3 * C, C), bf16),
            pltpu.VMEM((C, 3 * C), bf16),
            pltpu.VMEM((C, C), bf16),
            pltpu.VMEM((TDIM, C), bf16),
            pltpu.SemaphoreType.DMA((12,)),
        ],
        compiler_params=pltpu.CompilerParams(vmem_limit_bytes=LIMIT * MIB),
        name="pair",
    )(
        part,
        steps,
        labels,
        errors,
        own,
        near,
        core,
        far,
        conv,
        bias,
        gain,
        qkvw,
        outw,
        timew,
        frequencies(),
    )


def input_kernel(
    part_ref,
    stat_ref,
    gain_ref,
    cg_ref,
    x_ref,
    own_ref,
    conv_ref,
    in_ref,
    sum_ref,
    gcat,
    acc,
    cg_s,
    x_s,
    own_s,
    conv_s,
    sems,
):
    part = part_ref[0]
    load_cg = pltpu.make_async_copy(cg_ref, cg_s, sems.at[0])
    taps = [pltpu.make_async_copy(conv_ref.at[i], conv_s.at[i], sems.at[1 + i]) for i in range(3)]
    rest = [
        pltpu.make_async_copy(ref, to, sems.at[4 + i])
        for i, (ref, to) in enumerate(((x_ref, x_s), (own_ref, own_s)))
    ]
    load_cg.start()
    taps[0].start()
    gcat[0:BAND, :] = jnp.zeros((BAND, 3 * C), bf16)
    gcat[pl.ds(BAND + TOK, BAND), :] = jnp.zeros((BAND, 3 * C), bf16)
    load_cg.wait()
    taps[1].start()
    bias_sum = jnp.zeros((1, C), f32)
    for r, m, at in blocks():
        g = cg_s[pl.ds(at, COLS), :]
        wide = g.astype(f32)
        bias_sum = bias_sum + jnp.sum(wide, axis=0, keepdims=True)
        here = pl.ds(BAND + at, COLS)
        gcat[here, 0:C] = shifted(wide, -1).astype(bf16)
        gcat[here, C : 2 * C] = g
        gcat[here, 2 * C : 3 * C] = shifted(wide, 1).astype(bf16)
    for i in range(3):
        taps[i].wait()
        if i == 0:
            taps[2].start()
            rest[0].start()
        if i == 1:
            rest[1].start()
        for j in range(3):
            term = dot(
                gcat[pl.ds((2 - i) * BAND, TOK), j * C : (j + 1) * C],
                conv_s[i, j * C : (j + 1) * C, :],
                NT,
            )
            if i == 0 and j == 0:
                acc[...] = term
            else:
                acc[...] += term
    for load in rest:
        load.wait()
    gain = gain_ref[...].reshape(1, C)
    gain_sum = jnp.zeros((1, C), f32)
    ones = [jnp.zeros((1, C), f32) for _ in range(2)]
    twos = [jnp.zeros((1, C), f32) for _ in range(2)]
    for r, m, at in blocks():
        here = pl.ds(at, COLS)
        normed = (x_s[here, :].astype(f32) - stat_ref[row(m), :]) * stat_ref[row(2 + m), :]
        a = normed * gain
        s = sigmoid(a)
        pre = acc[here, :] * (s * (1.0 + a * (1.0 - s)))
        gain_sum = gain_sum + jnp.sum(pre * normed, axis=0, keepdims=True)
        scaled = pre * gain
        acc[here, :] = scaled
        ones[m] = ones[m] + jnp.sum(scaled, axis=0, keepdims=True)
        twos[m] = twos[m] + jnp.sum(scaled * normed, axis=0, keepdims=True)
    sum_ref[...] = jnp.concatenate([gain_sum, bias_sum], axis=0)
    means = group_sums(jnp.concatenate(ones + twos, axis=0)) / GROUP_COUNT
    for m in range(2):
        here = pl.ds(pl.multiple_of(part * BAND + m * COLS, COLS), COLS)
        inv = stat_ref[row(2 + m), :]
        normed = (x_s[here, :].astype(f32) - stat_ref[row(m), :]) * inv
        inner = inv * (acc[here, :] - means[m : m + 1] - normed * means[2 + m : 3 + m])
        mine = slice(m * COLS, (m + 1) * COLS)
        in_ref[mine, :] = (own_s[mine, :] + inner).astype(bf16)


def input_call(part, stat, gain, cg, x, own, conv):
    smem = pl.BlockSpec(memory_space=pltpu.SMEM)
    vmem = pl.BlockSpec(memory_space=pltpu.VMEM)
    hbm = pl.BlockSpec(memory_space=pltpu.HBM)
    return pl.pallas_call(
        input_kernel,
        out_shape=(
            jax.ShapeDtypeStruct((BAND, C), bf16),
            jax.ShapeDtypeStruct((2, C), f32),
        ),
        in_specs=[smem] + [vmem] * 2 + [hbm] * 4,
        out_specs=[vmem] * 2,
        scratch_shapes=[
            pltpu.VMEM((TOK + 2 * BAND, 3 * C), bf16),
            pltpu.VMEM((TOK, C), f32),
            pltpu.VMEM((TOK, C), bf16),
            pltpu.VMEM((TOK, C), bf16),
            pltpu.VMEM((BAND, C), f32),
            pltpu.VMEM((3, 3 * C, C), bf16),
            pltpu.SemaphoreType.DMA((6,)),
        ],
        compiler_params=pltpu.CompilerParams(vmem_limit_bytes=LIMIT * MIB),
        cost_estimate=pl.CostEstimate(
            flops=2 * TOK * 10 * C * C, bytes_accessed=9 * C * C * 2, transcendentals=TOK * C
        ),
        name="input",
    )(part, stat, gain, cg, x, own, conv)


def half_kernel(a_ref, out_ref, acc, mid):
    total = a_ref[0].astype(f32)
    for i in range(1, 8):
        total = total + a_ref[i].astype(f32)
    acc[...] = total
    mid[:, OWN * BLOCKS :, :] = jnp.zeros((8, CHUNK - OWN * BLOCKS, 128), f32)
    for i in range(8):
        for k in range(BLOCKS):
            mid[i, OWN * k : OWN * (k + 1), :] = acc[
                OWN * i : OWN * (i + 1), 128 * k : 128 * (k + 1)
            ]
    out_ref[...] = mid[...].astype(bf16)


def half_call(a):
    vmem = pl.BlockSpec(memory_space=pltpu.VMEM)
    return pl.pallas_call(
        half_kernel,
        out_shape=jax.ShapeDtypeStruct((8, CHUNK, 128), bf16),
        in_specs=[vmem],
        out_specs=vmem,
        scratch_shapes=[
            pltpu.VMEM((80, WIDTH), f32),
            pltpu.VMEM((8, CHUNK, 128), f32),
        ],
        compiler_params=pltpu.CompilerParams(vmem_limit_bytes=32 * MIB),
        name="half",
    )(a)


def total_kernel(a_ref, out_ref):
    total = a_ref[0].astype(f32)
    for i in range(1, 8):
        total = total + a_ref[i].astype(f32)
    out_ref[...] = total


def total_call(a):
    vmem = pl.BlockSpec(memory_space=pltpu.VMEM)
    return pl.pallas_call(
        total_kernel,
        out_shape=jax.ShapeDtypeStruct((CHUNK, 128), f32),
        in_specs=[vmem],
        out_specs=vmem,
        compiler_params=pltpu.CompilerParams(vmem_limit_bytes=16 * MIB),
        name="total",
    )(a)


def unpack_kernel(all_ref, conv_ref, qkv_ref, out_ref, time_ref):
    for part in range(4):
        for k in range(5):
            rows = all_ref[part, OWN * k : OWN * (k + 1), :]
            cols = slice(128 * k, 128 * (k + 1))
            if part < 3:
                qkv_ref[OWN * part : OWN * (part + 1), cols] = rows
            else:
                out_ref[:, cols] = rows
        for k in range(TAP_BLOCKS):
            rows = all_ref[part, OWN * (5 + k) : OWN * (6 + k), :]
            place = part * TAP_BLOCKS + k
            tap, block = place // 5, place % 5
            if place < 45:
                conv_ref[tap // 3, :, tap % 3, 128 * block : 128 * (block + 1)] = rows
            else:
                wide = min(128, TDIM - 128 * (place - 45))
                low = 128 * (place - 45)
                time_ref[:, low : low + wide] = rows[:, 0:wide]


def unpack_call(whole):
    vmem = pl.BlockSpec(memory_space=pltpu.VMEM)
    return pl.pallas_call(
        unpack_kernel,
        out_shape=(
            jax.ShapeDtypeStruct((3, OWN, 3, C), f32),
            jax.ShapeDtypeStruct((3 * OWN, C), f32),
            jax.ShapeDtypeStruct((OWN, C), f32),
            jax.ShapeDtypeStruct((OWN, TDIM), f32),
        ),
        in_specs=[vmem],
        out_specs=[vmem] * 4,
        compiler_params=pltpu.CompilerParams(vmem_limit_bytes=16 * MIB),
        name="unpack",
    )(whole)


def on_device(
    section_input,
    target,
    conv_weight,
    conv_bias,
    norm_gain,
    qkv_weight,
    out_weight,
    time_weight,
    timesteps,
    labels,
    ref_error,
):
    part = lax.axis_index(SPACE_AXES).astype(jnp.int32).reshape(1)
    swap = [(0, 1), (1, 0)]
    own_xt = jnp.concatenate([section_input.reshape(BAND, C), target.reshape(BAND, C)], axis=0)
    near = lax.ppermute(own_xt, "y_lo", swap)
    core = lax.ppermute(own_xt, "core", swap)
    far = lax.ppermute(near, "core", swap)
    conv = conv_weight.reshape(3, 3 * C, C)
    wire, x, cg, own, stat, pair_loss = pair_call(
        part,
        timesteps,
        labels,
        ref_error,
        own_xt,
        near,
        core,
        far,
        conv,
        conv_bias,
        norm_gain,
        qkv_weight,
        out_weight,
        time_weight,
    )
    moved = lax.all_to_all(wire.reshape(8, 80, WIDTH), ("x", "y_hi"), 0, 0)
    input_grad, gains = input_call(part, stat, norm_gain, cg, x, own, conv)
    gains = lax.psum(gains, "z")
    gains = gains + lax.ppermute(gains, "y_hi", swap)
    moved, gains = lax.optimization_barrier((moved, gains))
    half, gains = lax.optimization_barrier((half_call(moved), gains))
    moved = lax.all_to_all(half, "z", 0, 0)
    gains = gains + lax.ppermute(gains, "x", [(0, 1), (1, 0), (2, 3), (3, 2)])
    total, gains = lax.optimization_barrier((total_call(moved), gains))
    gains = gains + lax.ppermute(gains, "x", [(0, 3), (3, 0), (1, 2), (2, 1)])
    gains = lax.dynamic_slice_in_dim(gains, lax.axis_index(PAIR_AXES) * OWN, OWN, 1)
    whole = lax.all_gather(total, SPACE_AXES, axis=0, tiled=False)
    conv_out, qkv_out, out_out, time_out = unpack_call(whole)
    return (
        input_grad.reshape(section_input.shape),
        conv_out.transpose(0, 2, 3, 1),
        qkv_out.T,
        out_out.T,
        time_out.T,
        gains[0],
        gains[1],
        pair_loss,
    )


def solution(mesh):
    fine = Mesh(mesh.devices.reshape(MESH_SHAPE), MESH_AXES)
    pairs = P(PAIR_AXES)
    rows = P(PAIR_AXES, None, SPACE_AXES, None, None)
    return jax.shard_map(
        on_device,
        mesh=fine,
        in_specs=(rows, rows, P(), P(), P(), P(), P(), P(), pairs, pairs, pairs),
        out_specs=(
            rows,
            P(None, None, None, PAIR_AXES),
            P(None, PAIR_AXES),
            P(None, PAIR_AXES),
            P(None, PAIR_AXES),
            pairs,
            pairs,
            pairs,
        ),
        check_vma=False,
    )
```

```python
import math

import jax
import jax.numpy as jnp
import numpy as np
from jax import lax
from jax.experimental import pallas as pl
from jax.experimental.pallas import tpu as pltpu
from jax.sharding import Mesh
from jax.sharding import PartitionSpec as P

HEADS = 10
GROUPS = 32
TDIM = 320
C = 640
COLS = 64
ROWS = 4
TOK = 2 * ROWS * COLS
IMG = ROWS * COLS
BAND = 2 * COLS
HEAD_PAIRS = HEADS // 2
GROUP_COUNT = ROWS * COLS * (C // GROUPS)
SCALE = 1.0 / math.sqrt(C // HEADS)
EPS = 1e-05
BETA = 2.0

PAIR_AXES = ("x", "z", "y_hi")
SPACE_AXES = ("y_lo", "core")
MESH_AXES = ("x", "z", "y_hi", "y_lo", "core")
MESH_SHAPE = (4, 8, 2, 2, 2)
OWN = C // 64
TAP_BLOCKS = 12
BLOCKS = 5 + TAP_BLOCKS
WIDTH = BLOCKS * 128
CHUNK = 176
MIB = 1024 * 1024
LIMIT = 56

f32 = jnp.float32
bf16 = jnp.bfloat16

NN = (((1,), (0,)), ((), ()))
NT = (((1,), (1,)), ((), ()))
TN = (((0,), (0,)), ((), ()))


def dot(a, b, dims=NN):
    return lax.dot_general(a, b, dims, preferred_element_type=f32)


def frequencies():
    half = TDIM // 2
    return np.exp(-math.log(10000.0) * (np.arange(TDIM) % half) / half).astype(np.float32)[None]


def wire_columns(step, width):
    n = lax.broadcasted_iota(jnp.int32, (160, width), 0)
    y = jnp.where(n >= 80, 1, 0)
    rest = n - 80 * y
    z = (rest * 6554) >> 16
    return 2 * step * z + step * y + rest - OWN * z


def row(i):
    return pl.ds(i, 1)


def group_sums(rows):
    a = lax.broadcasted_iota(jnp.int32, (C, C), 0)
    b = lax.broadcasted_iota(jnp.int32, (C, C), 1)
    same = ((a * 3277) >> 16) == ((b * 3277) >> 16)
    ones = jnp.where(same, 1.0, 0.0).astype(bf16)
    high = rows.astype(bf16).astype(f32)
    rest = rows - high
    middle = rest.astype(bf16).astype(f32)
    low = rest - middle
    stack = jnp.concatenate([high, middle, low, jnp.zeros_like(rows)], axis=0).astype(bf16)
    sums = dot(stack, ones)
    return sums[0:4] + sums[4:8] + sums[8:12]


def sigmoid(v):
    return 1.0 / (1.0 + jnp.exp(-v))


def blocks():
    return [(r, m, (2 * r + m) * COLS) for r in range(ROWS) for m in range(2)]


def shifted(v, step):
    at = lax.broadcasted_iota(jnp.int32, (COLS, C), 0)
    if step == 1:
        return jnp.where(at == 0, 0.0, pltpu.roll(v, 1, 0))
    return jnp.where(at == COLS - 1, 0.0, pltpu.roll(v, COLS - 1, 0))


def head_halves(v):
    lane = lax.broadcasted_iota(jnp.int32, (1, 128), 1)
    first = jnp.where(lane < 64, 1.0, 0.0).astype(bf16)
    second = jnp.where(lane < 64, 0.0, 1.0).astype(bf16)
    return jnp.concatenate([v * first, v * second], axis=0)


def head_join(v):
    lane = lax.broadcasted_iota(jnp.int32, (IMG, 128), 1)
    return jnp.where(lane < 64, v[:IMG], v[IMG:])


def pair_kernel(
    part_ref,
    step_ref,
    label_ref,
    error_ref,
    own_x_ref,
    y_x_ref,
    core_x_ref,
    far_x_ref,
    own_t_ref,
    y_t_ref,
    core_t_ref,
    far_t_ref,
    conv_ref,
    bias_ref,
    gain_ref,
    qkvw_ref,
    outw_ref,
    timew_ref,
    freq_ref,
    wire_ref,
    x_ref,
    cg_ref,
    own_ref,
    stat_ref,
    loss_ref,
    acat,
    acc,
    resid,
    qkv,
    probs,
    attended,
    dev,
    gall,
    dattn,
    asel,
    feats_s,
    turned,
    wire_s,
    cg_s,
    own_s,
    x_s,
    t_s,
    conv_s,
    qkvw_s,
    outw_s,
    timew_s,
    sems,
):
    part = part_ref[0]
    taps = [pltpu.make_async_copy(conv_ref.at[i], conv_s.at[i], sems.at[i]) for i in range(3)]
    load_time = pltpu.make_async_copy(timew_ref, timew_s, sems.at[3])
    load_qkv = pltpu.make_async_copy(qkvw_ref, qkvw_s, sems.at[4])
    load_out = pltpu.make_async_copy(outw_ref, outw_s, sems.at[5])
    taps[0].start()
    load_time.start()
    taps[1].start()
    x_refs = (own_x_ref, core_x_ref, y_x_ref, far_x_ref)
    t_refs = (own_t_ref, core_t_ref, y_t_ref, far_t_ref)
    for way in range(4):
        rows = pl.ds(pl.multiple_of((part ^ way) * BAND, BAND), BAND)
        x_s[rows, :] = x_refs[way][...]
        t_s[rows, :] = t_refs[way][...]
    stores = [pltpu.make_async_copy(x_s, x_ref, sems.at[6])]
    sums, squares = [], []
    for m in range(2):
        total = jnp.zeros((1, C), f32)
        square = jnp.zeros((1, C), f32)
        for r in range(ROWS):
            v = x_s[pl.ds((2 * r + m) * COLS, COLS), :].astype(f32)
            total = total + jnp.sum(v, axis=0, keepdims=True)
            square = square + jnp.sum(v * v, axis=0, keepdims=True)
        sums.append(total)
        squares.append(square)
    moments = group_sums(jnp.concatenate(sums + squares, axis=0)) / GROUP_COUNT
    mean = moments[0:2]
    inv = lax.rsqrt(moments[2:4] - mean * mean + EPS)
    stat_ref[...] = jnp.concatenate([mean, inv, jnp.zeros((4, C), f32)], axis=0)
    gain = gain_ref[...].reshape(1, C)
    acat[0:BAND, :] = jnp.zeros((BAND, 3 * C), bf16)
    acat[pl.ds(BAND + TOK, BAND), :] = jnp.zeros((BAND, 3 * C), bf16)
    for r, m, at in blocks():
        v = x_s[pl.ds(at, COLS), :].astype(f32)
        a = (v - mean[m : m + 1]) * inv[m : m + 1] * gain
        act = a * sigmoid(a)
        here = pl.ds(BAND + at, COLS)
        acat[here, 0:C] = shifted(act, 1).astype(bf16)
        acat[here, C : 2 * C] = act.astype(bf16)
        acat[here, 2 * C : 3 * C] = shifted(act, -1).astype(bf16)
    angle = step_ref[0].astype(f32) * freq_ref[...]
    lane = lax.broadcasted_iota(jnp.int32, (1, TDIM), 1)
    feats = jnp.where(lane < TDIM // 2, jnp.cos(angle), jnp.sin(angle))
    feats_s[...] = jnp.zeros((8, 384), f32)
    feats_s[0:1, 0:TDIM] = feats
    load_time.wait()
    shift = dot(jnp.broadcast_to(feats, (16, TDIM)).astype(bf16), timew_s[...])[0:1]
    offset = shift + bias_ref[...].reshape(1, C)
    taps[0].wait()
    taps[2].start()
    load_qkv.start()
    stores[0].start()
    acc[...] = dot(acat[0:TOK, :], conv_s[0])
    taps[1].wait()
    acc[...] += dot(acat[pl.ds(BAND, TOK), :], conv_s[1])
    taps[2].wait()
    acc[...] += dot(acat[pl.ds(2 * BAND, TOK), :], conv_s[2])
    resid[...] = (x_s[...].astype(f32) + acc[...] + offset).astype(bf16)
    load_qkv.wait()
    load_out.start()
    for third in range(3):
        cols = pl.ds(third * C, C)
        proj = dot(resid[...], qkvw_s[:, cols]).astype(bf16)
        for r, m, at in blocks():
            qkv[m, pl.ds(r * COLS, COLS), cols] = proj[at : at + COLS]
    for m in range(2):
        for h in range(HEAD_PAIRS):
            q2 = head_halves(qkv[m, :, pl.ds(h * 128, 128)])
            k = qkv[m, :, pl.ds(C + h * 128, 128)]
            v = qkv[m, :, pl.ds(2 * C + h * 128, 128)]
            scores = dot(k, q2, NT) * SCALE
            exps = jnp.exp(scores - jnp.max(scores, axis=0, keepdims=True))
            p = exps * (1.0 / jnp.sum(exps, axis=0, keepdims=True))
            probs[m * HEAD_PAIRS + h] = p
            joined = head_join(dot(p.astype(bf16), v, TN)).astype(bf16)
            for r in range(ROWS):
                attended[pl.ds((2 * r + m) * COLS, COLS), pl.ds(h * 128, 128)] = joined[
                    r * COLS : (r + 1) * COLS
                ]
    load_out.wait()
    dev[...] = (
        resid[...].astype(f32) + dot(attended[...], outw_s[...]) - t_s[...].astype(f32)
    )
    margin = jnp.zeros((1, 1), f32)
    signs = []
    for m in range(2):
        total = jnp.zeros((1, C), f32)
        for r in range(ROWS):
            d = dev[pl.ds((2 * r + m) * COLS, COLS), :]
            total = total + jnp.sum(d * d, axis=0, keepdims=True)
        error = jnp.sum(total, axis=1, keepdims=True) / (IMG * C)
        sign = jnp.where(label_ref[0] == m, 1.0, -1.0)
        signs.append(sign)
        margin = margin + sign * (error - error_ref[0, m])
    twice = BETA * margin
    loss = jnp.maximum(twice, 0.0) + jnp.log1p(jnp.exp(-jnp.abs(twice)))
    loss_ref[0] = loss[0, 0]
    slope = BETA * sigmoid(BETA * margin)
    for r, m, at in blocks():
        here = pl.ds(at, COLS)
        gall[here, 3 * C : 4 * C] = (signs[m] * slope * dev[here, :]).astype(bf16)
    out_grad = gall[:, 3 * C : 4 * C]
    da = dot(out_grad, outw_s[...], NT).astype(bf16)
    for r, m, at in blocks():
        dattn[m, pl.ds(r * COLS, COLS), :] = da[at : at + COLS]
    for m in range(2):
        for h in range(HEAD_PAIRS):
            q2 = head_halves(qkv[m, :, pl.ds(h * 128, 128)])
            k = qkv[m, :, pl.ds(C + h * 128, 128)]
            v = qkv[m, :, pl.ds(2 * C + h * 128, 128)]
            da2 = head_halves(dattn[m, :, pl.ds(h * 128, 128)])
            p = probs[m * HEAD_PAIRS + h]
            dp = dot(v, da2, NT)
            dots = jnp.sum(p * dp, axis=0, keepdims=True)
            ds = (p * (dp - dots) * SCALE).astype(bf16)
            dq = head_join(dot(ds, k, TN)).astype(bf16)
            dk = dot(ds, q2).astype(bf16)
            dv = dot(p.astype(bf16), da2).astype(bf16)
            for r in range(ROWS):
                here = pl.ds((2 * r + m) * COLS, COLS)
                rows = slice(r * COLS, (r + 1) * COLS)
                gall[here, pl.ds(h * 128, 128)] = dq[rows]
                gall[here, pl.ds(C + h * 128, 128)] = dk[rows]
                gall[here, pl.ds(2 * C + h * 128, 128)] = dv[rows]
    acc[...] = out_grad.astype(f32) + dot(gall[:, 0 : 3 * C], qkvw_s[...], NT)
    cg_s[...] = acc[...].astype(bf16)
    own_s[...] = acc[pl.ds(pl.multiple_of(part * BAND, BAND), BAND), :]
    stores.append(pltpu.make_async_copy(cg_s, cg_ref, sems.at[7]))
    stores.append(pltpu.make_async_copy(own_s, own_ref, sems.at[8]))
    for store in stores[1:]:
        store.start()
    lane = lax.broadcasted_iota(jnp.int32, (160, 2 * IMG), 1)
    own_cols = wire_columns(OWN, 2 * IMG)[:, 0:IMG]
    for x in range(4):
        low = 128 * x
        pick = jnp.where(lane[:, 0:IMG] == own_cols + 32 * x, 1.0, 0.0).astype(bf16)
        turned[160 * x : 160 * (x + 1), :] = dot(pick, cg_s[:, low : low + IMG], NT).astype(bf16)
    for k in range(TAP_BLOCKS):
        place = part * TAP_BLOCKS + k
        cols = slice(k * 128, (k + 1) * 128)

        def tap(place=place, cols=cols):
            up = place // 15
            lane = pl.multiple_of((place - 15 * up) * 128, 128)
            asel[:, cols] = acat[pl.ds(pl.multiple_of(up * BAND, BAND), TOK), pl.ds(lane, 128)]

        if k < 9:
            tap()
        else:
            pl.when(part < 3)(tap)

            @pl.when(part == 3)
            def _(k=k, cols=cols):
                f = feats_s[0:1, (k - 9) * 128 : (k - 8) * 128]
                asel[:, cols] = jnp.broadcast_to(f, (TOK, 128)).astype(bf16)

    for i, low in enumerate((C, C + 768)):
        cols = slice(low, low + 768)
        wire_s[:, cols] = dot(turned[...], asel[:, low - C : low - C + 768]).astype(bf16)
        store = pltpu.make_async_copy(wire_s.at[:, cols], wire_ref.at[:, cols], sems.at[9 + i])
        store.start()
        stores.append(store)

    @pl.when(part < 3)
    def _():
        at = lax.broadcasted_iota(jnp.int32, (160, C), 1)
        cols = wire_columns(3 * OWN, C) + OWN * part
        for x, low in enumerate((0, 384, 896, 1280)):
            pick = jnp.where(at == cols + (480 * x - low), 1.0, 0.0).astype(bf16)
            turned[160 * x : 160 * (x + 1), :] = dot(pick, gall[:, low : low + C], NT).astype(bf16)
        wire_s[:, 0:C] = dot(turned[...], resid[...]).astype(bf16)

    @pl.when(part == 3)
    def _():
        for x in range(4):
            low = 3 * C + 128 * x
            pick = jnp.where(lane[:, 0:IMG] == own_cols + 32 * x, 1.0, 0.0).astype(bf16)
            turned[160 * x : 160 * (x + 1), :] = dot(pick, gall[:, low : low + IMG], NT).astype(
                bf16
            )
        wire_s[:, 0:C] = dot(turned[...], attended[...]).astype(bf16)

    store = pltpu.make_async_copy(wire_s.at[:, 0:C], wire_ref.at[:, 0:C], sems.at[11])
    store.start()
    for each in stores + [store]:
        each.wait()


def pair_call(part, steps, labels, errors, rows, conv, bias, gain, qkvw, outw, timew):
    smem = pl.BlockSpec(memory_space=pltpu.SMEM)
    vmem = pl.BlockSpec(memory_space=pltpu.VMEM)
    hbm = pl.BlockSpec(memory_space=pl.ANY)
    return pl.pallas_call(
        pair_kernel,
        out_shape=(
            jax.ShapeDtypeStruct((C, WIDTH), bf16),
            jax.ShapeDtypeStruct((TOK, C), bf16),
            jax.ShapeDtypeStruct((TOK, C), bf16),
            jax.ShapeDtypeStruct((BAND, C), f32),
            jax.ShapeDtypeStruct((8, C), f32),
            jax.ShapeDtypeStruct((1,), f32),
        ),
        in_specs=[smem] * 4 + [vmem] * 8 + [hbm] + [vmem] * 2 + [hbm] * 3 + [vmem],
        out_specs=[hbm] * 4 + [vmem, smem],
        scratch_shapes=[
            pltpu.VMEM((TOK + 2 * BAND, 3 * C), bf16),
            pltpu.VMEM((TOK, C), f32),
            pltpu.VMEM((TOK, C), bf16),
            pltpu.VMEM((2, IMG, 3 * C), bf16),
            pltpu.VMEM((2 * HEAD_PAIRS, IMG, 2 * IMG), f32),
            pltpu.VMEM((TOK, C), bf16),
            pltpu.VMEM((TOK, C), f32),
            pltpu.VMEM((TOK, 4 * C), bf16),
            pltpu.VMEM((2, IMG, C), bf16),
            pltpu.VMEM((TOK, TAP_BLOCKS * 128), bf16),
            pltpu.VMEM((8, 384), f32),
            pltpu.VMEM((C, TOK), bf16),
            pltpu.VMEM((C, WIDTH), bf16),
            pltpu.VMEM((TOK, C), bf16),
            pltpu.VMEM((BAND, C), f32),
            pltpu.VMEM((TOK, C), bf16),
            pltpu.VMEM((TOK, C), bf16),
            pltpu.VMEM((3, 3 * C, C), bf16),
            pltpu.VMEM((C, 3 * C), bf16),
            pltpu.VMEM((C, C), bf16),
            pltpu.VMEM((TDIM, C), bf16),
            pltpu.SemaphoreType.DMA((12,)),
        ],
        compiler_params=pltpu.CompilerParams(vmem_limit_bytes=LIMIT * MIB),
        name="pair",
    )(
        part,
        steps,
        labels,
        errors,
        *rows,
        conv,
        bias,
        gain,
        qkvw,
        outw,
        timew,
        frequencies(),
    )


def input_kernel(
    part_ref,
    stat_ref,
    gain_ref,
    cg_ref,
    x_ref,
    own_ref,
    conv_ref,
    in_ref,
    sum_ref,
    gcat,
    acc,
    cg_s,
    x_s,
    own_s,
    conv_s,
    sems,
):
    part = part_ref[0]
    load_cg = pltpu.make_async_copy(cg_ref, cg_s, sems.at[0])
    taps = [pltpu.make_async_copy(conv_ref.at[i], conv_s.at[i], sems.at[1 + i]) for i in range(3)]
    rest = [
        pltpu.make_async_copy(ref, to, sems.at[4 + i])
        for i, (ref, to) in enumerate(((x_ref, x_s), (own_ref, own_s)))
    ]
    load_cg.start()
    taps[0].start()
    gcat[0:BAND, :] = jnp.zeros((BAND, 3 * C), bf16)
    gcat[pl.ds(BAND + TOK, BAND), :] = jnp.zeros((BAND, 3 * C), bf16)
    load_cg.wait()
    taps[1].start()
    bias_sum = jnp.zeros((1, C), f32)
    for r, m, at in blocks():
        g = cg_s[pl.ds(at, COLS), :]
        wide = g.astype(f32)
        bias_sum = bias_sum + jnp.sum(wide, axis=0, keepdims=True)
        here = pl.ds(BAND + at, COLS)
        gcat[here, 0:C] = shifted(wide, -1).astype(bf16)
        gcat[here, C : 2 * C] = g
        gcat[here, 2 * C : 3 * C] = shifted(wide, 1).astype(bf16)
    for i in range(3):
        taps[i].wait()
        if i == 0:
            taps[2].start()
            rest[0].start()
        if i == 1:
            rest[1].start()
        for j in range(3):
            term = dot(
                gcat[pl.ds((2 - i) * BAND, TOK), j * C : (j + 1) * C],
                conv_s[i, j * C : (j + 1) * C, :],
                NT,
            )
            if i == 0 and j == 0:
                acc[...] = term
            else:
                acc[...] += term
    for load in rest:
        load.wait()
    gain = gain_ref[...].reshape(1, C)
    gain_sum = jnp.zeros((1, C), f32)
    ones = [jnp.zeros((1, C), f32) for _ in range(2)]
    twos = [jnp.zeros((1, C), f32) for _ in range(2)]
    for r, m, at in blocks():
        here = pl.ds(at, COLS)
        normed = (x_s[here, :].astype(f32) - stat_ref[row(m), :]) * stat_ref[row(2 + m), :]
        a = normed * gain
        s = sigmoid(a)
        pre = acc[here, :] * (s * (1.0 + a * (1.0 - s)))
        gain_sum = gain_sum + jnp.sum(pre * normed, axis=0, keepdims=True)
        scaled = pre * gain
        acc[here, :] = scaled
        ones[m] = ones[m] + jnp.sum(scaled, axis=0, keepdims=True)
        twos[m] = twos[m] + jnp.sum(scaled * normed, axis=0, keepdims=True)
    sum_ref[...] = jnp.concatenate([gain_sum, bias_sum], axis=0)
    means = group_sums(jnp.concatenate(ones + twos, axis=0)) / GROUP_COUNT
    for m in range(2):
        here = pl.ds(pl.multiple_of(part * BAND + m * COLS, COLS), COLS)
        inv = stat_ref[row(2 + m), :]
        normed = (x_s[here, :].astype(f32) - stat_ref[row(m), :]) * inv
        inner = inv * (acc[here, :] - means[m : m + 1] - normed * means[2 + m : 3 + m])
        mine = slice(m * COLS, (m + 1) * COLS)
        in_ref[mine, :] = (own_s[mine, :] + inner).astype(bf16)


def input_call(part, stat, gain, cg, x, own, conv):
    smem = pl.BlockSpec(memory_space=pltpu.SMEM)
    vmem = pl.BlockSpec(memory_space=pltpu.VMEM)
    hbm = pl.BlockSpec(memory_space=pltpu.HBM)
    return pl.pallas_call(
        input_kernel,
        out_shape=(
            jax.ShapeDtypeStruct((BAND, C), bf16),
            jax.ShapeDtypeStruct((2, C), f32),
        ),
        in_specs=[smem] + [vmem] * 2 + [hbm] * 4,
        out_specs=[vmem] * 2,
        scratch_shapes=[
            pltpu.VMEM((TOK + 2 * BAND, 3 * C), bf16),
            pltpu.VMEM((TOK, C), f32),
            pltpu.VMEM((TOK, C), bf16),
            pltpu.VMEM((TOK, C), bf16),
            pltpu.VMEM((BAND, C), f32),
            pltpu.VMEM((3, 3 * C, C), bf16),
            pltpu.SemaphoreType.DMA((6,)),
        ],
        compiler_params=pltpu.CompilerParams(vmem_limit_bytes=LIMIT * MIB),
        cost_estimate=pl.CostEstimate(
            flops=2 * TOK * 10 * C * C, bytes_accessed=9 * C * C * 2, transcendentals=TOK * C
        ),
        name="input",
    )(part, stat, gain, cg, x, own, conv)


def half_kernel(a_ref, out_ref, acc, mid):
    total = a_ref[0].astype(f32)
    for i in range(1, 8):
        total = total + a_ref[i].astype(f32)
    acc[...] = total
    mid[:, OWN * BLOCKS :, :] = jnp.zeros((8, CHUNK - OWN * BLOCKS, 128), f32)
    for i in range(8):
        for k in range(BLOCKS):
            mid[i, OWN * k : OWN * (k + 1), :] = acc[
                OWN * i : OWN * (i + 1), 128 * k : 128 * (k + 1)
            ]
    out_ref[...] = mid[...].astype(bf16)


def half_call(a):
    vmem = pl.BlockSpec(memory_space=pltpu.VMEM)
    return pl.pallas_call(
        half_kernel,
        out_shape=jax.ShapeDtypeStruct((8, CHUNK, 128), bf16),
        in_specs=[vmem],
        out_specs=vmem,
        scratch_shapes=[
            pltpu.VMEM((80, WIDTH), f32),
            pltpu.VMEM((8, CHUNK, 128), f32),
        ],
        compiler_params=pltpu.CompilerParams(vmem_limit_bytes=32 * MIB),
        name="half",
    )(a)


def total_kernel(a_ref, out_ref):
    total = a_ref[0].astype(f32)
    for i in range(1, 8):
        total = total + a_ref[i].astype(f32)
    out_ref[...] = total.astype(bf16)


def total_call(a):
    vmem = pl.BlockSpec(memory_space=pltpu.VMEM)
    return pl.pallas_call(
        total_kernel,
        out_shape=jax.ShapeDtypeStruct((CHUNK, 128), bf16),
        in_specs=[vmem],
        out_specs=vmem,
        compiler_params=pltpu.CompilerParams(vmem_limit_bytes=16 * MIB),
        name="total",
    )(a)


def unpack_kernel(all_ref, conv_ref, qkv_ref, out_ref, time_ref):
    for part in range(4):
        whole = all_ref[part].astype(f32)
        for k in range(5):
            rows = whole[OWN * k : OWN * (k + 1), :]
            cols = slice(128 * k, 128 * (k + 1))
            if part < 3:
                qkv_ref[OWN * part : OWN * (part + 1), cols] = rows
            else:
                out_ref[:, cols] = rows
        for k in range(TAP_BLOCKS):
            rows = whole[OWN * (5 + k) : OWN * (6 + k), :]
            place = part * TAP_BLOCKS + k
            tap, block = place // 5, place % 5
            if place < 45:
                conv_ref[tap // 3, :, tap % 3, 128 * block : 128 * (block + 1)] = rows
            else:
                wide = min(128, TDIM - 128 * (place - 45))
                low = 128 * (place - 45)
                time_ref[:, low : low + wide] = rows[:, 0:wide]


def unpack_call(whole):
    vmem = pl.BlockSpec(memory_space=pltpu.VMEM)
    return pl.pallas_call(
        unpack_kernel,
        out_shape=(
            jax.ShapeDtypeStruct((3, OWN, 3, C), f32),
            jax.ShapeDtypeStruct((3 * OWN, C), f32),
            jax.ShapeDtypeStruct((OWN, C), f32),
            jax.ShapeDtypeStruct((OWN, TDIM), f32),
        ),
        in_specs=[vmem],
        out_specs=[vmem] * 4,
        compiler_params=pltpu.CompilerParams(vmem_limit_bytes=16 * MIB),
        name="unpack",
    )(whole)


def on_device(
    section_input,
    target,
    conv_weight,
    conv_bias,
    norm_gain,
    qkv_weight,
    out_weight,
    time_weight,
    timesteps,
    labels,
    ref_error,
):
    part = lax.axis_index(SPACE_AXES).astype(jnp.int32).reshape(1)
    swap = [(0, 1), (1, 0)]
    own_x, own_t = section_input.reshape(BAND, C), target.reshape(BAND, C)
    near_x = lax.ppermute(own_x, "y_lo", swap)
    near_t = lax.ppermute(own_t, "y_lo", swap)
    core_x = lax.ppermute(own_x, "core", swap)
    core_t = lax.ppermute(own_t, "core", swap)
    far_x = lax.ppermute(near_x, "core", swap)
    far_t = lax.ppermute(near_t, "core", swap)
    rows = (own_x, near_x, core_x, far_x, own_t, near_t, core_t, far_t)
    conv = conv_weight.reshape(3, 3 * C, C)
    wire, x, cg, own, stat, pair_loss = pair_call(
        part,
        timesteps,
        labels,
        ref_error,
        rows,
        conv,
        conv_bias,
        norm_gain,
        qkv_weight,
        out_weight,
        time_weight,
    )
    moved = lax.all_to_all(wire.reshape(8, 80, WIDTH), ("x", "y_hi"), 0, 0)
    input_grad, gains = input_call(part, stat, norm_gain, cg, x, own, conv)
    gains = lax.psum(gains, "z")
    gains = gains + lax.ppermute(gains, "y_hi", swap)
    moved, gains = lax.optimization_barrier((moved, gains))
    half, gains = lax.optimization_barrier((half_call(moved), gains))
    moved = lax.all_to_all(half, "z", 0, 0)
    gains = gains + lax.ppermute(gains, "x", [(0, 1), (1, 0), (2, 3), (3, 2)])
    gains = gains + lax.ppermute(gains, "x", [(0, 3), (3, 0), (1, 2), (2, 1)])
    gains = lax.dynamic_slice_in_dim(gains, lax.axis_index(PAIR_AXES) * OWN, OWN, 1)
    moved, gains = lax.optimization_barrier((moved, gains))
    whole = lax.all_gather(total_call(moved), SPACE_AXES, axis=0, tiled=False)
    conv_out, qkv_out, out_out, time_out = unpack_call(whole)
    return (
        input_grad.reshape(section_input.shape),
        conv_out.transpose(0, 2, 3, 1),
        qkv_out.T,
        out_out.T,
        time_out.T,
        gains[0],
        gains[1],
        pair_loss,
    )


def solution(mesh):
    fine = Mesh(mesh.devices.reshape(MESH_SHAPE), MESH_AXES)
    pairs = P(PAIR_AXES)
    rows = P(PAIR_AXES, None, SPACE_AXES, None, None)
    return jax.shard_map(
        on_device,
        mesh=fine,
        in_specs=(rows, rows, P(), P(), P(), P(), P(), P(), pairs, pairs, pairs),
        out_specs=(
            rows,
            P(None, None, None, PAIR_AXES),
            P(None, PAIR_AXES),
            P(None, PAIR_AXES),
            P(None, PAIR_AXES),
            pairs,
            pairs,
            pairs,
        ),
        check_vma=False,
    )
```

```python
import math

import jax
import jax.numpy as jnp
import numpy as np
from jax import lax
from jax.experimental import pallas as pl
from jax.experimental.pallas import tpu as pltpu
from jax.sharding import Mesh
from jax.sharding import PartitionSpec as P

HEADS = 10
GROUPS = 32
TDIM = 320
C = 640
COLS = 64
ROWS = 4
TOK = 2 * ROWS * COLS
IMG = ROWS * COLS
BAND = 2 * COLS
HEAD_PAIRS = HEADS // 2
GROUP_COUNT = ROWS * COLS * (C // GROUPS)
SCALE = 1.0 / math.sqrt(C // HEADS)
EPS = 1e-05
BETA = 2.0

PAIR_AXES = ("x", "z", "y_hi")
SPACE_AXES = ("y_lo", "core")
MESH_AXES = ("x", "z", "y_hi", "y_lo", "core")
MESH_SHAPE = (4, 8, 2, 2, 2)
OWN = C // 64
TAP_BLOCKS = 12
BLOCKS = 5 + TAP_BLOCKS
WIDTH = BLOCKS * 128
CHUNK = 176
MIB = 1024 * 1024
LIMIT = 56

f32 = jnp.float32
bf16 = jnp.bfloat16

NN = (((1,), (0,)), ((), ()))
NT = (((1,), (1,)), ((), ()))
TN = (((0,), (0,)), ((), ()))


def dot(a, b, dims=NN):
    return lax.dot_general(a, b, dims, preferred_element_type=f32)


def frequencies():
    half = TDIM // 2
    return np.exp(-math.log(10000.0) * (np.arange(TDIM) % half) / half).astype(np.float32)[None]


def wire_columns(step, width):
    n = lax.broadcasted_iota(jnp.int32, (160, width), 0)
    y = jnp.where(n >= 80, 1, 0)
    rest = n - 80 * y
    z = (rest * 6554) >> 16
    return 2 * step * z + step * y + rest - OWN * z


def row(i):
    return pl.ds(i, 1)


def group_sums(rows):
    a = lax.broadcasted_iota(jnp.int32, (C, C), 0)
    b = lax.broadcasted_iota(jnp.int32, (C, C), 1)
    same = ((a * 3277) >> 16) == ((b * 3277) >> 16)
    ones = jnp.where(same, 1.0, 0.0).astype(bf16)
    high = rows.astype(bf16).astype(f32)
    rest = rows - high
    middle = rest.astype(bf16).astype(f32)
    low = rest - middle
    stack = jnp.concatenate([high, middle, low, jnp.zeros_like(rows)], axis=0).astype(bf16)
    sums = dot(stack, ones)
    return sums[0:4] + sums[4:8] + sums[8:12]


def sigmoid(v):
    return 1.0 / (1.0 + jnp.exp(-v))


def blocks():
    return [(r, m, (2 * r + m) * COLS) for r in range(ROWS) for m in range(2)]


def shifted(v, step):
    at = lax.broadcasted_iota(jnp.int32, (COLS, C), 0)
    if step == 1:
        return jnp.where(at == 0, 0.0, pltpu.roll(v, 1, 0))
    return jnp.where(at == COLS - 1, 0.0, pltpu.roll(v, COLS - 1, 0))


def head_halves(v):
    lane = lax.broadcasted_iota(jnp.int32, (1, 128), 1)
    first = jnp.where(lane < 64, 1.0, 0.0).astype(bf16)
    second = jnp.where(lane < 64, 0.0, 1.0).astype(bf16)
    return jnp.concatenate([v * first, v * second], axis=0)


def head_join(v):
    lane = lax.broadcasted_iota(jnp.int32, (IMG, 128), 1)
    return jnp.where(lane < 64, v[:IMG], v[IMG:])


def pair_kernel(
    part_ref,
    step_ref,
    label_ref,
    error_ref,
    own_x_ref,
    y_x_ref,
    core_x_ref,
    far_x_ref,
    own_t_ref,
    y_t_ref,
    core_t_ref,
    far_t_ref,
    conv_ref,
    bias_ref,
    gain_ref,
    qkvw_ref,
    outw_ref,
    timew_ref,
    freq_ref,
    wire_ref,
    x_ref,
    cg_ref,
    own_ref,
    stat_ref,
    loss_ref,
    acat,
    acc,
    resid,
    qkv,
    probs,
    attended,
    dev,
    gall,
    dattn,
    asel,
    feats_s,
    turned,
    wire_s,
    cg_s,
    own_s,
    x_s,
    t_s,
    conv_s,
    qkvw_s,
    outw_s,
    timew_s,
    sems,
):
    part = part_ref[0]
    taps = [pltpu.make_async_copy(conv_ref.at[i], conv_s.at[i], sems.at[i]) for i in range(3)]
    load_time = pltpu.make_async_copy(timew_ref, timew_s, sems.at[3])
    load_qkv = pltpu.make_async_copy(qkvw_ref, qkvw_s, sems.at[4])
    load_out = pltpu.make_async_copy(outw_ref, outw_s, sems.at[5])
    taps[0].start()
    load_time.start()
    taps[1].start()
    x_refs = (own_x_ref, core_x_ref, y_x_ref, far_x_ref)
    t_refs = (own_t_ref, core_t_ref, y_t_ref, far_t_ref)
    for way in range(4):
        rows = pl.ds(pl.multiple_of((part ^ way) * BAND, BAND), BAND)
        x_s[rows, :] = x_refs[way][...]
        t_s[rows, :] = t_refs[way][...]
    stores = [pltpu.make_async_copy(x_s, x_ref, sems.at[6])]
    sums, squares = [], []
    for m in range(2):
        total = jnp.zeros((1, C), f32)
        square = jnp.zeros((1, C), f32)
        for r in range(ROWS):
            v = x_s[pl.ds((2 * r + m) * COLS, COLS), :].astype(f32)
            total = total + jnp.sum(v, axis=0, keepdims=True)
            square = square + jnp.sum(v * v, axis=0, keepdims=True)
        sums.append(total)
        squares.append(square)
    moments = group_sums(jnp.concatenate(sums + squares, axis=0)) / GROUP_COUNT
    mean = moments[0:2]
    inv = lax.rsqrt(moments[2:4] - mean * mean + EPS)
    stat_ref[...] = jnp.concatenate([mean, inv, jnp.zeros((4, C), f32)], axis=0)
    gain = gain_ref[...].reshape(1, C)
    acat[0:BAND, :] = jnp.zeros((BAND, 3 * C), bf16)
    acat[pl.ds(BAND + TOK, BAND), :] = jnp.zeros((BAND, 3 * C), bf16)
    for r, m, at in blocks():
        v = x_s[pl.ds(at, COLS), :].astype(f32)
        a = (v - mean[m : m + 1]) * inv[m : m + 1] * gain
        act = a * sigmoid(a)
        here = pl.ds(BAND + at, COLS)
        acat[here, 0:C] = shifted(act, 1).astype(bf16)
        acat[here, C : 2 * C] = act.astype(bf16)
        acat[here, 2 * C : 3 * C] = shifted(act, -1).astype(bf16)
    angle = step_ref[0].astype(f32) * freq_ref[...]
    lane = lax.broadcasted_iota(jnp.int32, (1, TDIM), 1)
    feats = jnp.where(lane < TDIM // 2, jnp.cos(angle), jnp.sin(angle))
    feats_s[...] = jnp.zeros((8, 384), f32)
    feats_s[0:1, 0:TDIM] = feats
    load_time.wait()
    shift = dot(jnp.broadcast_to(feats, (16, TDIM)).astype(bf16), timew_s[...])[0:1]
    offset = shift + bias_ref[...].reshape(1, C)
    taps[0].wait()
    taps[2].start()
    load_qkv.start()
    stores[0].start()
    acc[...] = dot(acat[0:TOK, :], conv_s[0])
    taps[1].wait()
    acc[...] += dot(acat[pl.ds(BAND, TOK), :], conv_s[1])
    taps[2].wait()
    acc[...] += dot(acat[pl.ds(2 * BAND, TOK), :], conv_s[2])
    resid[...] = (x_s[...].astype(f32) + acc[...] + offset).astype(bf16)
    load_qkv.wait()
    load_out.start()
    for third in range(3):
        cols = pl.ds(third * C, C)
        proj = dot(resid[...], qkvw_s[:, cols]).astype(bf16)
        for r, m, at in blocks():
            qkv[m, pl.ds(r * COLS, COLS), cols] = proj[at : at + COLS]
    for m in range(2):
        for h in range(HEAD_PAIRS):
            q2 = head_halves(qkv[m, :, pl.ds(h * 128, 128)])
            k = qkv[m, :, pl.ds(C + h * 128, 128)]
            v = qkv[m, :, pl.ds(2 * C + h * 128, 128)]
            scores = dot(k, q2, NT) * SCALE
            exps = jnp.exp(scores - jnp.max(scores, axis=0, keepdims=True))
            p = exps * (1.0 / jnp.sum(exps, axis=0, keepdims=True))
            probs[m * HEAD_PAIRS + h] = p
            joined = head_join(dot(p.astype(bf16), v, TN)).astype(bf16)
            for r in range(ROWS):
                attended[pl.ds((2 * r + m) * COLS, COLS), pl.ds(h * 128, 128)] = joined[
                    r * COLS : (r + 1) * COLS
                ]
    load_out.wait()
    dev[...] = (
        resid[...].astype(f32) + dot(attended[...], outw_s[...]) - t_s[...].astype(f32)
    )
    margin = jnp.zeros((1, 1), f32)
    signs = []
    for m in range(2):
        total = jnp.zeros((1, C), f32)
        for r in range(ROWS):
            d = dev[pl.ds((2 * r + m) * COLS, COLS), :]
            total = total + jnp.sum(d * d, axis=0, keepdims=True)
        error = jnp.sum(total, axis=1, keepdims=True) / (IMG * C)
        sign = jnp.where(label_ref[0] == m, 1.0, -1.0)
        signs.append(sign)
        margin = margin + sign * (error - error_ref[0, m])
    twice = BETA * margin
    loss = jnp.maximum(twice, 0.0) + jnp.log1p(jnp.exp(-jnp.abs(twice)))
    loss_ref[0] = loss[0, 0]
    slope = BETA * sigmoid(BETA * margin)
    for r, m, at in blocks():
        here = pl.ds(at, COLS)
        gall[here, 3 * C : 4 * C] = (signs[m] * slope * dev[here, :]).astype(bf16)
    out_grad = gall[:, 3 * C : 4 * C]
    da = dot(out_grad, outw_s[...], NT).astype(bf16)
    for r, m, at in blocks():
        dattn[m, pl.ds(r * COLS, COLS), :] = da[at : at + COLS]
    for m in range(2):
        for h in range(HEAD_PAIRS):
            q2 = head_halves(qkv[m, :, pl.ds(h * 128, 128)])
            k = qkv[m, :, pl.ds(C + h * 128, 128)]
            v = qkv[m, :, pl.ds(2 * C + h * 128, 128)]
            da2 = head_halves(dattn[m, :, pl.ds(h * 128, 128)])
            p = probs[m * HEAD_PAIRS + h]
            dp = dot(v, da2, NT)
            dots = jnp.sum(p * dp, axis=0, keepdims=True)
            ds = (p * (dp - dots) * SCALE).astype(bf16)
            dq = head_join(dot(ds, k, TN)).astype(bf16)
            dk = dot(ds, q2).astype(bf16)
            dv = dot(p.astype(bf16), da2).astype(bf16)
            for r in range(ROWS):
                here = pl.ds((2 * r + m) * COLS, COLS)
                rows = slice(r * COLS, (r + 1) * COLS)
                gall[here, pl.ds(h * 128, 128)] = dq[rows]
                gall[here, pl.ds(C + h * 128, 128)] = dk[rows]
                gall[here, pl.ds(2 * C + h * 128, 128)] = dv[rows]
    acc[...] = out_grad.astype(f32) + dot(gall[:, 0 : 3 * C], qkvw_s[...], NT)
    cg_s[...] = acc[...].astype(bf16)
    own_s[...] = acc[pl.ds(pl.multiple_of(part * BAND, BAND), BAND), :]
    stores.append(pltpu.make_async_copy(cg_s, cg_ref, sems.at[7]))
    stores.append(pltpu.make_async_copy(own_s, own_ref, sems.at[8]))
    for store in stores[1:]:
        store.start()
    lane = lax.broadcasted_iota(jnp.int32, (160, 2 * IMG), 1)
    own_cols = wire_columns(OWN, 2 * IMG)[:, 0:IMG]
    for x in range(4):
        low = 128 * x
        pick = jnp.where(lane[:, 0:IMG] == own_cols + 32 * x, 1.0, 0.0).astype(bf16)
        rows = dot(pick, cg_s[:, low : low + IMG], NT).astype(bf16)
        turned[80 * x : 80 * (x + 1), :] = rows[0:80]
        turned[320 + 80 * x : 400 + 80 * x, :] = rows[80:160]
    for k in range(TAP_BLOCKS):
        place = part * TAP_BLOCKS + k
        cols = slice(k * 128, (k + 1) * 128)

        def tap(place=place, cols=cols):
            up = place // 15
            lane = pl.multiple_of((place - 15 * up) * 128, 128)
            asel[:, cols] = acat[pl.ds(pl.multiple_of(up * BAND, BAND), TOK), pl.ds(lane, 128)]

        if k < 9:
            tap()
        else:
            pl.when(part < 3)(tap)

            @pl.when(part == 3)
            def _(k=k, cols=cols):
                f = feats_s[0:1, (k - 9) * 128 : (k - 8) * 128]
                asel[:, cols] = jnp.broadcast_to(f, (TOK, 128)).astype(bf16)

    for i, low in enumerate((C, C + 768)):
        cols = slice(low, low + 768)
        wire_s[:, cols] = dot(turned[...], asel[:, low - C : low - C + 768]).astype(bf16)
        store = pltpu.make_async_copy(wire_s.at[:, cols], wire_ref.at[:, cols], sems.at[9 + i])
        store.start()
        stores.append(store)

    @pl.when(part < 3)
    def _():
        at = lax.broadcasted_iota(jnp.int32, (160, C), 1)
        cols = wire_columns(3 * OWN, C) + OWN * part
        for x, low in enumerate((0, 384, 896, 1280)):
            pick = jnp.where(at == cols + (480 * x - low), 1.0, 0.0).astype(bf16)
            rows = dot(pick, gall[:, low : low + C], NT).astype(bf16)
            turned[80 * x : 80 * (x + 1), :] = rows[0:80]
            turned[320 + 80 * x : 400 + 80 * x, :] = rows[80:160]
        wire_s[:, 0:C] = dot(turned[...], resid[...]).astype(bf16)

    @pl.when(part == 3)
    def _():
        for x in range(4):
            low = 3 * C + 128 * x
            pick = jnp.where(lane[:, 0:IMG] == own_cols + 32 * x, 1.0, 0.0).astype(bf16)
            rows = dot(pick, gall[:, low : low + IMG], NT).astype(
                bf16
            )
            turned[80 * x : 80 * (x + 1), :] = rows[0:80]
            turned[320 + 80 * x : 400 + 80 * x, :] = rows[80:160]
        wire_s[:, 0:C] = dot(turned[...], attended[...]).astype(bf16)

    store = pltpu.make_async_copy(wire_s.at[:, 0:C], wire_ref.at[:, 0:C], sems.at[11])
    store.start()
    for each in stores + [store]:
        each.wait()


def pair_call(part, steps, labels, errors, rows, conv, bias, gain, qkvw, outw, timew):
    smem = pl.BlockSpec(memory_space=pltpu.SMEM)
    vmem = pl.BlockSpec(memory_space=pltpu.VMEM)
    hbm = pl.BlockSpec(memory_space=pl.ANY)
    return pl.pallas_call(
        pair_kernel,
        out_shape=(
            jax.ShapeDtypeStruct((C, WIDTH), bf16),
            jax.ShapeDtypeStruct((TOK, C), bf16),
            jax.ShapeDtypeStruct((TOK, C), bf16),
            jax.ShapeDtypeStruct((BAND, C), f32),
            jax.ShapeDtypeStruct((8, C), f32),
            jax.ShapeDtypeStruct((1,), f32),
        ),
        in_specs=[smem] * 4 + [vmem] * 8 + [hbm] + [vmem] * 2 + [hbm] * 3 + [vmem],
        out_specs=[hbm] * 4 + [vmem, smem],
        scratch_shapes=[
            pltpu.VMEM((TOK + 2 * BAND, 3 * C), bf16),
            pltpu.VMEM((TOK, C), f32),
            pltpu.VMEM((TOK, C), bf16),
            pltpu.VMEM((2, IMG, 3 * C), bf16),
            pltpu.VMEM((2 * HEAD_PAIRS, IMG, 2 * IMG), f32),
            pltpu.VMEM((TOK, C), bf16),
            pltpu.VMEM((TOK, C), f32),
            pltpu.VMEM((TOK, 4 * C), bf16),
            pltpu.VMEM((2, IMG, C), bf16),
            pltpu.VMEM((TOK, TAP_BLOCKS * 128), bf16),
            pltpu.VMEM((8, 384), f32),
            pltpu.VMEM((C, TOK), bf16),
            pltpu.VMEM((C, WIDTH), bf16),
            pltpu.VMEM((TOK, C), bf16),
            pltpu.VMEM((BAND, C), f32),
            pltpu.VMEM((TOK, C), bf16),
            pltpu.VMEM((TOK, C), bf16),
            pltpu.VMEM((3, 3 * C, C), bf16),
            pltpu.VMEM((C, 3 * C), bf16),
            pltpu.VMEM((C, C), bf16),
            pltpu.VMEM((TDIM, C), bf16),
            pltpu.SemaphoreType.DMA((12,)),
        ],
        compiler_params=pltpu.CompilerParams(vmem_limit_bytes=LIMIT * MIB),
        name="pair",
    )(
        part,
        steps,
        labels,
        errors,
        *rows,
        conv,
        bias,
        gain,
        qkvw,
        outw,
        timew,
        frequencies(),
    )


def input_kernel(
    part_ref,
    stat_ref,
    gain_ref,
    cg_ref,
    x_ref,
    own_ref,
    conv_ref,
    in_ref,
    sum_ref,
    gcat,
    acc,
    cg_s,
    x_s,
    own_s,
    conv_s,
    sems,
):
    part = part_ref[0]
    load_cg = pltpu.make_async_copy(cg_ref, cg_s, sems.at[0])
    taps = [pltpu.make_async_copy(conv_ref.at[i], conv_s.at[i], sems.at[1 + i]) for i in range(3)]
    rest = [
        pltpu.make_async_copy(ref, to, sems.at[4 + i])
        for i, (ref, to) in enumerate(((x_ref, x_s), (own_ref, own_s)))
    ]
    load_cg.start()
    taps[0].start()
    gcat[0:BAND, :] = jnp.zeros((BAND, 3 * C), bf16)
    gcat[pl.ds(BAND + TOK, BAND), :] = jnp.zeros((BAND, 3 * C), bf16)
    load_cg.wait()
    taps[1].start()
    bias_sum = jnp.zeros((1, C), f32)
    for r, m, at in blocks():
        g = cg_s[pl.ds(at, COLS), :]
        wide = g.astype(f32)
        bias_sum = bias_sum + jnp.sum(wide, axis=0, keepdims=True)
        here = pl.ds(BAND + at, COLS)
        gcat[here, 0:C] = shifted(wide, -1).astype(bf16)
        gcat[here, C : 2 * C] = g
        gcat[here, 2 * C : 3 * C] = shifted(wide, 1).astype(bf16)
    for i in range(3):
        taps[i].wait()
        if i == 0:
            taps[2].start()
            rest[0].start()
        if i == 1:
            rest[1].start()
        for j in range(3):
            term = dot(
                gcat[pl.ds((2 - i) * BAND, TOK), j * C : (j + 1) * C],
                conv_s[i, j * C : (j + 1) * C, :],
                NT,
            )
            if i == 0 and j == 0:
                acc[...] = term
            else:
                acc[...] += term
    for load in rest:
        load.wait()
    gain = gain_ref[...].reshape(1, C)
    gain_sum = jnp.zeros((1, C), f32)
    ones = [jnp.zeros((1, C), f32) for _ in range(2)]
    twos = [jnp.zeros((1, C), f32) for _ in range(2)]
    for r, m, at in blocks():
        here = pl.ds(at, COLS)
        normed = (x_s[here, :].astype(f32) - stat_ref[row(m), :]) * stat_ref[row(2 + m), :]
        a = normed * gain
        s = sigmoid(a)
        pre = acc[here, :] * (s * (1.0 + a * (1.0 - s)))
        gain_sum = gain_sum + jnp.sum(pre * normed, axis=0, keepdims=True)
        scaled = pre * gain
        acc[here, :] = scaled
        ones[m] = ones[m] + jnp.sum(scaled, axis=0, keepdims=True)
        twos[m] = twos[m] + jnp.sum(scaled * normed, axis=0, keepdims=True)
    sum_ref[...] = jnp.concatenate([gain_sum, bias_sum], axis=0)
    means = group_sums(jnp.concatenate(ones + twos, axis=0)) / GROUP_COUNT
    for m in range(2):
        here = pl.ds(pl.multiple_of(part * BAND + m * COLS, COLS), COLS)
        inv = stat_ref[row(2 + m), :]
        normed = (x_s[here, :].astype(f32) - stat_ref[row(m), :]) * inv
        inner = inv * (acc[here, :] - means[m : m + 1] - normed * means[2 + m : 3 + m])
        mine = slice(m * COLS, (m + 1) * COLS)
        in_ref[mine, :] = (own_s[mine, :] + inner).astype(bf16)


def input_call(part, stat, gain, cg, x, own, conv):
    smem = pl.BlockSpec(memory_space=pltpu.SMEM)
    vmem = pl.BlockSpec(memory_space=pltpu.VMEM)
    hbm = pl.BlockSpec(memory_space=pltpu.HBM)
    return pl.pallas_call(
        input_kernel,
        out_shape=(
            jax.ShapeDtypeStruct((BAND, C), bf16),
            jax.ShapeDtypeStruct((2, C), f32),
        ),
        in_specs=[smem] + [vmem] * 2 + [hbm] * 4,
        out_specs=[vmem] * 2,
        scratch_shapes=[
            pltpu.VMEM((TOK + 2 * BAND, 3 * C), bf16),
            pltpu.VMEM((TOK, C), f32),
            pltpu.VMEM((TOK, C), bf16),
            pltpu.VMEM((TOK, C), bf16),
            pltpu.VMEM((BAND, C), f32),
            pltpu.VMEM((3, 3 * C, C), bf16),
            pltpu.SemaphoreType.DMA((6,)),
        ],
        compiler_params=pltpu.CompilerParams(vmem_limit_bytes=LIMIT * MIB),
        cost_estimate=pl.CostEstimate(
            flops=2 * TOK * 10 * C * C, bytes_accessed=9 * C * C * 2, transcendentals=TOK * C
        ),
        name="input",
    )(part, stat, gain, cg, x, own, conv)


def half_kernel(a_ref, out_ref, acc, mid):
    total = a_ref[0].astype(f32)
    for i in range(1, 8):
        total = total + a_ref[i].astype(f32)
    acc[...] = total
    mid[:, OWN * BLOCKS :, :] = jnp.zeros((8, CHUNK - OWN * BLOCKS, 128), f32)
    for i in range(8):
        for k in range(BLOCKS):
            mid[i, OWN * k : OWN * (k + 1), :] = acc[
                OWN * i : OWN * (i + 1), 128 * k : 128 * (k + 1)
            ]
    out_ref[...] = mid[...].astype(bf16)


def half_call(a):
    vmem = pl.BlockSpec(memory_space=pltpu.VMEM)
    return pl.pallas_call(
        half_kernel,
        out_shape=jax.ShapeDtypeStruct((8, CHUNK, 128), bf16),
        in_specs=[vmem],
        out_specs=vmem,
        scratch_shapes=[
            pltpu.VMEM((80, WIDTH), f32),
            pltpu.VMEM((8, CHUNK, 128), f32),
        ],
        compiler_params=pltpu.CompilerParams(vmem_limit_bytes=32 * MIB),
        name="half",
    )(a)


def total_kernel(a_ref, out_ref):
    total = a_ref[0].astype(f32)
    for i in range(1, 8):
        total = total + a_ref[i].astype(f32)
    out_ref[...] = total.astype(bf16)


def total_call(a):
    vmem = pl.BlockSpec(memory_space=pltpu.VMEM)
    return pl.pallas_call(
        total_kernel,
        out_shape=jax.ShapeDtypeStruct((CHUNK, 128), bf16),
        in_specs=[vmem],
        out_specs=vmem,
        compiler_params=pltpu.CompilerParams(vmem_limit_bytes=16 * MIB),
        name="total",
    )(a)


def unpack_kernel(all_ref, conv_ref, qkv_ref, out_ref, time_ref):
    for part in range(4):
        whole = all_ref[part].astype(f32)
        for k in range(5):
            rows = whole[OWN * k : OWN * (k + 1), :]
            cols = slice(128 * k, 128 * (k + 1))
            if part < 3:
                qkv_ref[OWN * part : OWN * (part + 1), cols] = rows
            else:
                out_ref[:, cols] = rows
        for k in range(TAP_BLOCKS):
            rows = whole[OWN * (5 + k) : OWN * (6 + k), :]
            place = part * TAP_BLOCKS + k
            tap, block = place // 5, place % 5
            if place < 45:
                conv_ref[tap // 3, :, tap % 3, 128 * block : 128 * (block + 1)] = rows
            else:
                wide = min(128, TDIM - 128 * (place - 45))
                low = 128 * (place - 45)
                time_ref[:, low : low + wide] = rows[:, 0:wide]


def unpack_call(whole):
    vmem = pl.BlockSpec(memory_space=pltpu.VMEM)
    return pl.pallas_call(
        unpack_kernel,
        out_shape=(
            jax.ShapeDtypeStruct((3, OWN, 3, C), f32),
            jax.ShapeDtypeStruct((3 * OWN, C), f32),
            jax.ShapeDtypeStruct((OWN, C), f32),
            jax.ShapeDtypeStruct((OWN, TDIM), f32),
        ),
        in_specs=[vmem],
        out_specs=[vmem] * 4,
        compiler_params=pltpu.CompilerParams(vmem_limit_bytes=16 * MIB),
        name="unpack",
    )(whole)


def on_device(
    section_input,
    target,
    conv_weight,
    conv_bias,
    norm_gain,
    qkv_weight,
    out_weight,
    time_weight,
    timesteps,
    labels,
    ref_error,
):
    part = lax.axis_index(SPACE_AXES).astype(jnp.int32).reshape(1)
    swap = [(0, 1), (1, 0)]
    own_x, own_t = section_input.reshape(BAND, C), target.reshape(BAND, C)
    near_x = lax.ppermute(own_x, "y_lo", swap)
    near_t = lax.ppermute(own_t, "y_lo", swap)
    core_x = lax.ppermute(own_x, "core", swap)
    core_t = lax.ppermute(own_t, "core", swap)
    far_x = lax.ppermute(near_x, "core", swap)
    far_t = lax.ppermute(near_t, "core", swap)
    rows = (own_x, near_x, core_x, far_x, own_t, near_t, core_t, far_t)
    conv = conv_weight.reshape(3, 3 * C, C)
    wire, x, cg, own, stat, pair_loss = pair_call(
        part,
        timesteps,
        labels,
        ref_error,
        rows,
        conv,
        conv_bias,
        norm_gain,
        qkv_weight,
        out_weight,
        time_weight,
    )
    moved = lax.all_to_all(wire.reshape(8, 80, WIDTH), ("y_hi", "x"), 0, 0)
    input_grad, gains = input_call(part, stat, norm_gain, cg, x, own, conv)
    gains = lax.psum(gains, "z")
    gains = gains + lax.ppermute(gains, "y_hi", swap)
    moved, gains = lax.optimization_barrier((moved, gains))
    half, gains = lax.optimization_barrier((half_call(moved), gains))
    moved = lax.all_to_all(half, "z", 0, 0)
    gains = gains + lax.ppermute(gains, "x", [(0, 1), (1, 0), (2, 3), (3, 2)])
    gains = gains + lax.ppermute(gains, "x", [(0, 3), (3, 0), (1, 2), (2, 1)])
    gains = lax.dynamic_slice_in_dim(gains, lax.axis_index(PAIR_AXES) * OWN, OWN, 1)
    moved, gains = lax.optimization_barrier((moved, gains))
    whole = lax.all_gather(total_call(moved), SPACE_AXES, axis=0, tiled=False)
    conv_out, qkv_out, out_out, time_out = unpack_call(whole)
    return (
        input_grad.reshape(section_input.shape),
        conv_out.transpose(0, 2, 3, 1),
        qkv_out.T,
        out_out.T,
        time_out.T,
        gains[0],
        gains[1],
        pair_loss,
    )


def solution(mesh):
    fine = Mesh(mesh.devices.reshape(MESH_SHAPE), MESH_AXES)
    pairs = P(PAIR_AXES)
    rows = P(PAIR_AXES, None, SPACE_AXES, None, None)
    return jax.shard_map(
        on_device,
        mesh=fine,
        in_specs=(rows, rows, P(), P(), P(), P(), P(), P(), pairs, pairs, pairs),
        out_specs=(
            rows,
            P(None, None, None, PAIR_AXES),
            P(None, PAIR_AXES),
            P(None, PAIR_AXES),
            P(None, PAIR_AXES),
            pairs,
            pairs,
            pairs,
        ),
        check_vma=False,
    )
```
